128 devices in a mesh: facet: 64 (over x, y, z_lo, core), rows: 2 (over z_hi).
Axes of the slice: x: 4, y: 4, z: 4 (z_hi: 2, z_lo: 2; z = z_hi * 2 + z_lo), core: 2. Of those that a mesh axis runs over, the one named last changes fastest.
Arguments:
- facets: float32 [64, 2, 8, 16384], P('facet', None, 'rows'), may hold values from -6 to 6
- facet_window: float32 [16384], replicated, may hold values from 0.3 to 3
- band_window: float32 [1024], replicated, may hold values from 0.3 to 3
- facet_order: int32 [64], replicated, may hold values from 0 to 63, each once
- facet_offsets: int32 [64, 2], replicated, may hold values from 0 to 262143
- sub_cols: int32 [64], replicated, may hold values from 0 to 262143
- sub_rows: int32 [64], replicated, may hold values from 0 to 262143
Outputs:
- subgrids: float32 [64, 2, 1024, 1024], P('facet', None, 'rows')
The draws below stay inside these ranges and needn't reach their ends.
All inputs are finite; a program needn't handle non-finite values.
Results may differ from the reference program's by a relative error of at most 0.0003.
The reference program's roundings to bfloat16 on the way count: a program that leaves them out, or rounds other values in their place, can miss the bound.
Values sent between devices are 32-bit elements; how exact they have to be, the bound alone decides.
No kernel may reach another device: no remote copies, remote signals or barrier semaphores. Data moves between devices by JAX's collectives and lax.ppermute only.
A program may use at most 128 MiB of HBM per device.

```python
import math
import jax
import jax.numpy as jnp
from jax import lax

NIMG = 262144
FW = 16384
M = 1024
SUBROWS = 1024
FACETS = 64
SUBGRIDS = 64
FROWS = 8


def touch_ends(values, key, smallest, top_value):
    shape = values.shape
    index_at = [jax.random.randint(jax.random.fold_in(key, axis), (), 0, shape[axis]) for axis in range(len(shape))]
    values = values.at[tuple(index_at)].set(smallest)
    longest = shape.index(max(shape))
    index_at[longest] = (index_at[longest] + 1) % shape[longest]
    return values.at[tuple(index_at)].set(top_value)


def level_of(stream_key, shape, split, low, high):
    loudness = 1.0
    for position, parts in split:
        draws = jax.random.uniform(jax.random.fold_in(jax.random.fold_in(stream_key, 6), position), (parts,), jnp.float32, low / len(split), high / len(split))
        loudness = loudness * jnp.repeat(jnp.exp(draws), shape[position] // parts).reshape((-1,) + (1,) * (len(shape) - 1 - position))
    return loudness


def normal_values(key, extent, scale, bound, cuts=(), held_as=jnp.bfloat16):
    level = level_of(key, extent, cuts, -0.22, 0.18) if cuts else 1.0
    values = jax.random.normal(key, extent, jnp.float32) * scale * level
    return jnp.minimum(jnp.maximum(values, -bound), bound).astype(held_as)


def setup_inputs(seed: int = 0) -> dict:
    key_of = jax.random.split(jax.random.key(seed), 8)
    return {
        "facets": normal_values(key_of[0], (FACETS, 2, FROWS, FW), 1.0, 6.0, ((0, 64), (2, 2)), jnp.float32),
        "facet_window": jnp.clip(jnp.exp(jax.random.uniform(key_of[1], (FW,), jnp.float32, math.log(0.3), math.log(3.0))), 0.3, 3.0),
        "band_window": jnp.clip(jnp.exp(jax.random.uniform(key_of[2], (M,), jnp.float32, math.log(0.3), math.log(3.0))), 0.3, 3.0),
        "facet_order": jax.random.permutation(key_of[3], FACETS).astype(jnp.int32),
        "facet_offsets": touch_ends(jax.random.randint(key_of[4], (FACETS, 2), 0, NIMG), jax.random.fold_in(key_of[4], 1), 0, NIMG - 1).astype(jnp.int32),
        "sub_cols": touch_ends(jax.random.randint(key_of[5], (SUBGRIDS,), 0, NIMG), jax.random.fold_in(key_of[5], 1), 0, NIMG - 1).astype(jnp.int32),
        "sub_rows": touch_ends(jax.random.randint(key_of[6], (SUBGRIDS,), 0, NIMG), jax.random.fold_in(key_of[6], 1), 0, NIMG - 1).astype(jnp.int32),
    }


TWO_PI = 2.0 * math.pi

def mulmod(left, right, modulus):
    high = right // 1024
    low = right % 1024
    return (left * high % modulus * 1024 + left * low) % modulus

def reference(facets, facet_window, band_window, facet_order, facet_offsets, sub_cols, sub_rows):
    scale = TWO_PI / NIMG
    col_off = facet_offsets[:, 0][facet_order]
    row_off = facet_offsets[:, 1][facet_order]
    columns = jnp.arange(FW, dtype=jnp.int32)
    bands = jnp.arange(M, dtype=jnp.int32)
    hi = lax.Precision.HIGHEST
    block = min(FW, 1024)
    nblocks = FW // block
    inner = jnp.arange(block, dtype=jnp.int32)
    tangle = scale * mulmod(inner[:, None], bands[None, :], NIMG).astype(jnp.float32)
    table_c = jnp.cos(tangle).astype(jnp.bfloat16).astype(jnp.float32)
    table_s = jnp.sin(tangle).astype(jnp.bfloat16).astype(jnp.float32)
    starts = jnp.arange(nblocks, dtype=jnp.int32) * block

    def one_facet(index):
        data = facets[index]
        place = (col_off[index] + columns) % NIMG
        windowed = data * facet_window
        angle = scale * mulmod(place[None, :], sub_cols[:, None], NIMG).astype(jnp.float32)
        cosine = jnp.cos(angle)[:, None, :]
        sine = jnp.sin(angle)[:, None, :]
        real_in = windowed[0][None]
        imag_in = windowed[1][None]
        shift_re = (real_in * cosine + imag_in * sine).astype(jnp.bfloat16).astype(jnp.float32)
        shift_im = (imag_in * cosine - real_in * sine).astype(jnp.bfloat16).astype(jnp.float32)
        flat_re = shift_re.reshape(-1, nblocks, block)
        flat_im = shift_im.reshape(-1, nblocks, block)
        part_re = jnp.einsum('abt,tk->abk', flat_re, table_c, precision=hi) + jnp.einsum('abt,tk->abk', flat_im, table_s, precision=hi)
        part_im = jnp.einsum('abt,tk->abk', flat_im, table_c, precision=hi) - jnp.einsum('abt,tk->abk', flat_re, table_s, precision=hi)
        bstart = (col_off[index] + starts) % NIMG
        pangle = scale * mulmod(bstart[:, None], bands[None, :], NIMG).astype(jnp.float32)
        pcos = jnp.cos(pangle)[None]
        psin = jnp.sin(pangle)[None]
        out_re = lax.optimization_barrier(jnp.sum(part_re * pcos + part_im * psin, 1))
        out_im = lax.optimization_barrier(jnp.sum(part_im * pcos - part_re * psin, 1))
        both = jnp.stack([out_re, out_im], 0).reshape(2, SUBGRIDS, FROWS, M)
        return jnp.transpose(both, (1, 0, 2, 3)) * band_window
    contrib = lax.map(one_facet, jnp.arange(FACETS, dtype=jnp.int32))
    frows = jnp.arange(FROWS, dtype=jnp.int32)
    subq = jnp.arange(SUBROWS, dtype=jnp.int32)
    place_rows = (row_off[:, None] + frows[None, :]) % NIMG

    def one_subgrid(index):
        blockc = contrib[:, index]
        target = (sub_rows[index] + subq) % NIMG
        angle = scale * mulmod(place_rows[:, :, None], target[None, None, :], NIMG).astype(jnp.float32)
        cosine = angle.reshape(-1, SUBROWS)
        sine = jnp.sin(cosine)
        cosine = jnp.cos(cosine)
        real_in = blockc[:, 0].reshape(-1, M)
        imag_in = blockc[:, 1].reshape(-1, M)
        out_re = jnp.dot(cosine.T, real_in, precision=hi) + jnp.dot(sine.T, imag_in, precision=hi)
        out_im = jnp.dot(cosine.T, imag_in, precision=hi) - jnp.dot(sine.T, real_in, precision=hi)
        rowed = jnp.stack([out_re, out_im], 0)
        mean = jnp.sum(rowed * rowed) / (2.0 * SUBROWS * M)
        return rowed * lax.rsqrt(mean + 1e-06)
    return lax.map(one_subgrid, jnp.arange(SUBGRIDS, dtype=jnp.int32))
```

```python
import functools
import math

import jax
import jax.numpy as jnp
import ml_dtypes
import numpy as np
from jax import lax
from jax.experimental import pallas as pl
from jax.experimental.pallas import tpu as pltpu
from jax.sharding import PartitionSpec as P

NIMG = 262144
M = 1024
SUBROWS = 1024
TWO_PI = 2.0 * math.pi

BLOCK = 1024
SPAN = 4096
NODES = 32
RANK = 4
ERANK = 2
ROW_SCALE = 4.0

f32 = jnp.float32
bf16 = jnp.bfloat16


def _split(values):
    high = values.astype(np.float32).astype(ml_dtypes.bfloat16)
    low = (values - high.astype(np.float64)).astype(np.float32).astype(ml_dtypes.bfloat16)
    return high, low


def _kernel_sum(x, count):
    den = np.sin(np.pi * x / NIMG)
    zero = np.abs(den) < 1e-14
    return np.where(zero, float(count), np.sin(np.pi * x * count / NIMG) / np.where(zero, 1.0, den))


def _solve(gram, right):
    gram, right = gram.copy(), right.copy()
    n = len(gram)
    for i in range(n):
        for j in range(i + 1, n):
            factor = gram[j, i] / gram[i, i]
            gram[j] = gram[j] - factor * gram[i]
            right[j] = right[j] - factor * right[i]
    out = np.zeros_like(right)
    for i in range(n - 1, -1, -1):
        total = right[i].copy()
        for j in range(i + 1, n):
            total = total - gram[i, j] * out[j]
        out[i] = total / gram[i, i]
    return out


@functools.lru_cache(maxsize=None)
def _tables():
    scale = TWO_PI / NIMG
    bands = np.arange(M)
    product = (np.arange(BLOCK)[:, None] * bands[None, :]) % NIMG
    angle = (np.float32(scale) * product.astype(np.float32)).astype(np.float64)
    exact = scale * product
    resid_c = np.cos(angle).astype(np.float32).astype(ml_dtypes.bfloat16).astype(np.float64) - np.cos(exact)
    resid_s = np.sin(angle).astype(np.float32).astype(ml_dtypes.bfloat16).astype(np.float64) - np.sin(exact)
    half = M // 2
    resid = np.stack(
        [np.concatenate([resid_c[:, h * half:(h + 1) * half], resid_s[:, h * half:(h + 1) * half]], 1) for h in range(2)]
    ).astype(np.float32).astype(ml_dtypes.bfloat16)
    i = np.arange(NODES)
    nodes = 511.5 + 512 * 1.05 * (0.25 * ((2 * i + 1) / NODES - 1) - 0.75 * np.cos(np.pi * (i + 0.5) / NODES))
    gram = _kernel_sum(nodes[:, None] - nodes[None, :], SPAN) + 1e-13 * SPAN * np.eye(NODES)
    interp = _solve(gram, _kernel_sum(nodes[:, None] - bands[None, :], SPAN))
    centre = (SPAN - 1) / 2
    at = scale * (np.arange(SPAN) - centre)[:, None] * nodes[None, :]
    sample = np.concatenate([np.cos(at), -np.sin(at)], 1)
    sample = np.concatenate(_split(sample), 1)
    rows = []
    for span in range(16384 // SPAN):
        turn = scale * (span * SPAN + centre) * bands
        re, im = interp * np.cos(turn), -interp * np.sin(turn)
        rows.append(np.concatenate([re, im], 1))
        rows.append(np.concatenate([-im, re], 1))
    weave = np.concatenate(rows, 0)
    weave_hi, weave_lo = _split(weave)
    turn = TWO_PI * ((np.arange(16)[:, None] * (bands[None, :half] % 256)) % 256) / 256
    return dict(
        resid=resid, sample=sample, weave_hi=weave_hi, weave_lo=weave_lo,
        turn_c=np.cos(turn).astype(np.float32), turn_s=np.sin(turn).astype(np.float32),
    )


COL_A, COL_L8, COL_P8, COL_ROW = 384, 400, 408, 416


def _pick(table, index):
    lane = lax.broadcasted_iota(jnp.int32, table.shape, 1)
    return jnp.sum(jnp.where(lane == index, table, 0.0), axis=1, keepdims=True)


def _fill_columns(cos_ref, sin_ref, lc_ref, ls_ref):
    low_c, low_s = cos_ref[:, 0:128], sin_ref[:, 0:128]
    for i in range(8):
        c, s = cos_ref[:, COL_L8 + i:COL_L8 + i + 1], sin_ref[:, COL_L8 + i:COL_L8 + i + 1]
        lc_ref[:, i * 128:(i + 1) * 128] = c * low_c - s * low_s
        ls_ref[:, i * 128:(i + 1) * 128] = s * low_c + c * low_s


def _exact_kernel(data_ref, window_ref, cos_ref, sin_ref, sample_ref, out_ref, lc_ref, ls_ref, acc_ref):
    step = pl.program_id(0)

    @pl.when(step == 0)
    def _():
        _fill_columns(cos_ref, sin_ref, lc_ref, ls_ref)

    block_c = _pick(cos_ref[:, 384:512], step)
    block_s = _pick(sin_ref[:, 384:512], step)
    span = step // 4
    total = None
    width = 256
    for i in range(BLOCK // width):
        cols = slice(i * width, (i + 1) * width)
        lc, ls = lc_ref[:, cols], ls_ref[:, cols]
        ec = block_c * lc - block_s * ls
        es = block_s * lc + block_c * ls
        data = data_ref[:, cols] * window_ref[:, cols]
        re, im = [], []
        for r in range(4):
            dr, di = data[r:r + 1], data[4 + r:5 + r]
            re.append((dr * ec + di * es).astype(bf16))
            im.append((di * ec - dr * es).astype(bf16))
        shifted = jnp.concatenate(re + im, 0)
        part = jnp.dot(shifted, sample_ref[cols, :], preferred_element_type=f32)
        total = part if total is None else total + part

    @pl.when(step % 4 == 0)
    def _():
        acc_ref[span] = total

    @pl.when(step % 4 != 0)
    def _():
        acc_ref[span] = acc_ref[span] + total

    @pl.when(step == 15)
    def _():
        lane = lax.broadcasted_iota(jnp.int32, (64, 128), 1)
        sign = jnp.where(lane & 32 == 0, -1.0, 1.0).astype(f32)
        sums = [[None] * 4 for _ in range(RANK)]
        for sp in range(4):
            for r in range(4):
                ar = acc_ref[sp, r * 64:(r + 1) * 64]
                ai = acc_ref[sp, 256 + r * 64:256 + (r + 1) * 64]
                ar = ar + pltpu.roll(ar, 64, 1)
                ai = ai + pltpu.roll(ai, 64, 1)
                value = ar + sign * pltpu.roll(ai, 32, 1)
                turned = sign * pltpu.roll(value, 32, 1)
                for n in range(RANK):
                    col = COL_ROW + n * 8 + r
                    term = cos_ref[:, col:col + 1] * value + sin_ref[:, col:col + 1] * turned
                    sums[n][sp] = term if sums[n][sp] is None else sums[n][sp] + term
        for n in range(RANK):
            out_ref[:, n * 256:n * 256 + 128] = jnp.where(lane < 64, sums[n][0], sums[n][1])
            out_ref[:, n * 256 + 128:n * 256 + 256] = jnp.where(lane < 64, sums[n][2], sums[n][3])


def _resid_kernel(half_ref, own_ref, peer_ref, window_ref, cos_ref, sin_ref, combine_ref, table_ref, tc_ref, ts_ref,
                  out_ref, lc_ref, ls_ref, mixed_ref):
    step = pl.program_id(0)

    @pl.when(step == 0)
    def _():
        _fill_columns(cos_ref, sin_ref, lc_ref, ls_ref)
        out_ref[...] = jnp.zeros_like(out_ref)

    for j in range(4):
        block = step * 4 + j
        block_c = _pick(cos_ref[:, 384:512], block)
        block_s = _pick(sin_ref[:, 384:512], block)
        for i in range(4):
            cols = slice(i * 256, (i + 1) * 256)
            here = slice(j * BLOCK + i * 256, j * BLOCK + (i + 1) * 256)
            window = window_ref[:, here]
            data = jnp.concatenate([own_ref[:, here] * window, peer_ref[:, here] * window], 0).astype(bf16)
            rows = jnp.dot(combine_ref[...], data, preferred_element_type=f32)
            lc, ls = lc_ref[:, cols], ls_ref[:, cols]
            ec = block_c * lc - block_s * ls
            es = block_s * lc + block_c * ls
            for n in range(ERANK):
                gr, gi = rows[n * 64:(n + 1) * 64], rows[128 + n * 64:128 + (n + 1) * 64]
                mixed_ref[j * 256 + n * 64:j * 256 + (n + 1) * 64, cols] = (gr * ec + gi * es).astype(bf16)
                mixed_ref[j * 256 + 128 + n * 64:j * 256 + 128 + (n + 1) * 64, cols] = (gi * ec - gr * es).astype(bf16)
    for kc in range(2):
        cols = slice(kc * 256, (kc + 1) * 256)
        by_c = jnp.dot(mixed_ref[...], table_ref[0, :, kc * 256:(kc + 1) * 256], preferred_element_type=f32)
        by_s = jnp.dot(mixed_ref[...], table_ref[0, :, 512 + kc * 256:512 + (kc + 1) * 256], preferred_element_type=f32)
        sum_re, sum_im = out_ref[0, :, cols], out_ref[1, :, cols]
        for j in range(4):
            re = by_c[j * 256:j * 256 + 128] + by_s[j * 256 + 128:j * 256 + 256]
            im = by_c[j * 256 + 128:j * 256 + 256] - by_s[j * 256:j * 256 + 128]
            tc = tc_ref[pl.ds(step * 4 + j, 1), cols]
            ts = ts_ref[pl.ds(step * 4 + j, 1), cols]
            sum_re = sum_re + (re * tc + im * ts)
            sum_im = sum_im + (im * tc - re * ts)
        out_ref[0, :, cols] = sum_re
        out_ref[1, :, cols] = sum_im


def _halves(value):
    high = value.astype(bf16)
    return high, (value - high.astype(f32)).astype(bf16)


def _rows_kernel(nodes_ref, resid_ref, cos_ref, sin_ref, band_ref, left_ref, wh_ref, wl_ref, out_ref,
                 right_ref, lcat_ref):
    lh, ll = _halves(left_ref[...])
    lcat_ref[:, 0:512] = lh
    lcat_ref[:, 512:1024] = lh
    lcat_ref[:, 1024:1536] = ll
    nh, nl = _halves(nodes_ref[...])
    low_c, low_s = cos_ref[:, 128:256], sin_ref[:, 128:256]
    for i in range(4):
        cols = slice(i * 256, (i + 1) * 256)
        vals = []
        for part in range(2):
            wcols = slice(part * 1024 + i * 256, part * 1024 + (i + 1) * 256)
            wh, wl = wh_ref[:, wcols], wl_ref[:, wcols]
            vals.append(
                jnp.dot(nh, wh, preferred_element_type=f32)
                + (jnp.dot(nh, wl, preferred_element_type=f32) + jnp.dot(nl, wh, preferred_element_type=f32))
            )
        pcs, pss = [], []
        for m in range(2):
            col = COL_P8 + i * 2 + m
            c, s = cos_ref[:, col:col + 1], sin_ref[:, col:col + 1]
            pcs.append(c * low_c - s * low_s)
            pss.append(s * low_c + c * low_s)
        band = band_ref[:, cols]
        pc = jnp.concatenate(pcs, 1) * band
        ps = jnp.concatenate(pss, 1) * band
        for n in range(RANK):
            vr, vi = vals[0][n * 64:(n + 1) * 64], vals[1][n * 64:(n + 1) * 64]
            if n < ERANK:
                vr = vr + resid_ref[n, 0, :, cols]
                vi = vi + resid_ref[n, 1, :, cols]
            cr = vr * pc + vi * ps
            ci = vi * pc - vr * ps
            for value, row, col in ((cr, 0, 0), (ci, 256, 0), (ci, 0, 1024), (-cr, 256, 1024)):
                high, low = _halves(value)
                base = row + n * 64
                ccols = slice(col + i * 256, col + (i + 1) * 256)
                right_ref[base:base + 64, ccols] = high
                right_ref[512 + base:512 + base + 64, ccols] = low
                right_ref[1024 + base:1024 + base + 64, ccols] = high

    total = jnp.zeros((8, 512), f32)
    for part in range(2):
        for i in range(2):
            cols = slice(part * 1024 + i * 512, part * 1024 + (i + 1) * 512)
            result = jnp.dot(lcat_ref[...], right_ref[:, cols], preferred_element_type=f32)
            out_ref[0, part, :, i * 512:(i + 1) * 512] = result[:512]
            total = total + jnp.sum((result * result).reshape(128, 8, 512), 0)
    mean = jnp.sum(total) / (2.0 * SUBROWS * M)
    factor = lax.rsqrt(jnp.full((8, 128), mean, f32) + 1e-06)[0:1, 0:1]
    for part in range(2):
        out_ref[0, part] = out_ref[0, part] * factor


def _angle(product):
    turns = lax.bitwise_and(product + NIMG, 2 * NIMG - 1) - NIMG
    return turns.astype(f32) * (math.pi / NIMG)


def per_device(facets, facet_window, band_window, facet_order, facet_offsets, sub_cols, sub_rows):
    tables = _tables()
    own = facets.reshape(8, 16384)
    rows_at = lax.axis_index("rows")
    peer = lax.ppermute(own, "rows", [(0, 1), (1, 0)])
    slots = jnp.arange(64, dtype=jnp.int32)
    own_slot = lax.axis_index("facet")
    match = facet_order[:, None] == slots[None, :]
    col_off = jnp.sum(jnp.where(match, facet_offsets[None, :, 0], 0), 1)
    row_off = jnp.sum(jnp.where(match, facet_offsets[None, :, 1], 0), 1)
    own_cols = jnp.sum(jnp.where(slots == own_slot, col_off, 0))
    own_subrow = jnp.sum(jnp.where(slots == own_slot, sub_rows, 0))

    lanes = jnp.arange(128, dtype=jnp.int32)
    rows8 = (4 * rows_at + jnp.arange(8, dtype=jnp.int32)) % 8
    small = jnp.arange(8, dtype=jnp.int32) * 128
    products = jnp.concatenate(
        [
            2 * lanes[None, :] * sub_cols[:, None],
            2 * lanes[None, :] * col_off[:, None],
            jnp.zeros((64, 128), jnp.int32),
            2 * (own_cols + 1024 * jnp.arange(16, dtype=jnp.int32))[None, :] * sub_cols[:, None],
            2 * small[None, :] * sub_cols[:, None],
            2 * small[None, :] * col_off[:, None],
            jnp.tile((2 * rows8 - 7)[None, :] * (sub_rows[:, None] + 512), (1, 4)),
            jnp.zeros((64, 64), jnp.int32),
        ],
        1,
    )
    angles = _angle(products)
    rho = (2 * rows8 - 7).astype(f32) / (2.0 * ROW_SCALE)
    powers = jnp.concatenate([jnp.ones(8, f32), rho, rho * rho, rho * rho * rho])
    scales = jnp.concatenate([jnp.ones(COL_ROW, f32), powers, jnp.ones(64, f32)])[None, :]
    signs = jnp.where((jnp.arange(512) >= COL_ROW) & (jnp.arange(512) < COL_ROW + 32), -1.0, 1.0).astype(f32)[None, :]
    tab_c = jnp.cos(angles) * scales
    tab_s = jnp.sin(angles) * (scales * signs)

    turn_c = tab_c[:, COL_ROW:COL_ROW + 16].reshape(64, ERANK, 2, 4)
    turn_s = tab_s[:, COL_ROW:COL_ROW + 16].reshape(64, ERANK, 2, 4)
    to_re = jnp.stack([turn_c, -turn_s], 3)
    to_im = jnp.stack([turn_s, turn_c], 3)
    combine = jnp.stack([to_re, to_im], 0).transpose(0, 2, 1, 3, 4, 5).reshape(256, 16).astype(bf16)

    q = (rows_at * 512 + jnp.arange(1024, dtype=jnp.int32)) % 1024
    turn = _angle((2 * row_off + 7)[None, :] * (own_subrow + q)[:, None])
    c, s = jnp.cos(turn), jnp.sin(turn)
    g = ((q - 512).astype(f32) * (TWO_PI / NIMG * ROW_SCALE))[:, None]
    g2, g3 = g * g * 0.5, g * g * g * (1.0 / 6.0)
    left = jnp.concatenate([c, -g * s, -g2 * c, g3 * s, s, g * c, -g2 * s, -g3 * c], 1)

    window = facet_window.reshape(1, 16384)
    whole = lambda shape: pl.BlockSpec(shape, lambda *_: (0,) * len(shape))
    params = dict(vmem_limit_bytes=56 * 1024 * 1024)
    nodes = pl.pallas_call(
        _exact_kernel,
        grid=(16,),
        in_specs=[
            pl.BlockSpec((8, BLOCK), lambda b: (0, b)),
            pl.BlockSpec((1, BLOCK), lambda b: (0, b)),
            whole((64, 512)),
            whole((64, 512)),
            pl.BlockSpec((BLOCK, 128), lambda b: (b % 4, 0)),
        ],
        out_specs=whole((64, 1024)),
        out_shape=jax.ShapeDtypeStruct((64, 1024), f32),
        scratch_shapes=[
            pltpu.VMEM((64, 1024), f32),
            pltpu.VMEM((64, 1024), f32),
            pltpu.VMEM((4, 512, 128), f32),
        ],
        compiler_params=pltpu.CompilerParams(dimension_semantics=("arbitrary",), **params),
        cost_estimate=pl.CostEstimate(flops=8 * 10**9, bytes_accessed=2 * 10**6, transcendentals=0),
        name="exact_part",
    )(own, window, tab_c, tab_s, jnp.asarray(tables["sample"]))

    resid = pl.pallas_call(
        _resid_kernel,
        grid_spec=pltpu.PrefetchScalarGridSpec(
            num_scalar_prefetch=1,
            grid=(4,),
            in_specs=[
                pl.BlockSpec((8, 4096), lambda b, h: (0, b)),
                pl.BlockSpec((8, 4096), lambda b, h: (0, b)),
                pl.BlockSpec((1, 4096), lambda b, h: (0, b)),
                whole((64, 512)),
                whole((64, 512)),
                whole((256, 16)),
                pl.BlockSpec((1, 1024, 1024), lambda b, h: (h[0], 0, 0)),
                whole((16, 512)),
                whole((16, 512)),
            ],
            out_specs=whole((2, 128, 512)),
            scratch_shapes=[
                pltpu.VMEM((64, 1024), f32),
                pltpu.VMEM((64, 1024), f32),
                pltpu.VMEM((1024, 1024), bf16),
            ],
        ),
        out_shape=jax.ShapeDtypeStruct((2, 128, 512), f32),
        compiler_params=pltpu.CompilerParams(dimension_semantics=("arbitrary",), **params),
        cost_estimate=pl.CostEstimate(flops=9 * 10**9, bytes_accessed=4 * 10**6, transcendentals=0),
        name="residual_part",
    )(
        rows_at.reshape(1).astype(jnp.int32), own, peer, window, tab_c, tab_s, combine,
        jnp.asarray(tables["resid"]), jnp.asarray(tables["turn_c"]), jnp.asarray(tables["turn_s"]),
    )

    send = jnp.concatenate(
        [
            resid.reshape(2, ERANK, 64, 512).transpose(2, 1, 0, 3).reshape(64, 16, 128),
            nodes.reshape(64, 8, 128),
        ],
        1,
    )
    send = jnp.broadcast_to(send[:, None], (64, 2, 24, 128)).reshape(128, 24, 128)
    got = lax.all_to_all(send, ("facet", "rows"), split_axis=0, concat_axis=0, tiled=True)
    got = got.reshape(64, 2, 24, 128)
    resid_got = got[:, :, :16].reshape(64, 2, ERANK, 2, 512).transpose(2, 3, 0, 1, 4).reshape(ERANK, 2, 64, 1024)
    nodes_got = (got[:, 0, 16:] + got[:, 1, 16:]).reshape(64, RANK, 256).transpose(1, 0, 2).reshape(256, 256)

    return pl.pallas_call(
        _rows_kernel,
        out_shape=jax.ShapeDtypeStruct((1, 2, 512, 1024), f32),
        scratch_shapes=[pltpu.VMEM((1536, 2048), bf16), pltpu.VMEM((1024, 1536), bf16)],
        compiler_params=pltpu.CompilerParams(**params),
        cost_estimate=pl.CostEstimate(flops=7 * 10**9, bytes_accessed=12 * 10**6, transcendentals=0),
        name="row_transform",
    )(
        nodes_got, resid_got, tab_c, tab_s, band_window.reshape(1, M), left,
        jnp.asarray(tables["weave_hi"]), jnp.asarray(tables["weave_lo"]),
    )


def solution(mesh):
    return jax.shard_map(
        per_device,
        mesh=mesh,
        in_specs=(P("facet", None, "rows", None), P(), P(), P(), P(), P(), P()),
        out_specs=P("facet", None, "rows", None),
        check_vma=False,
    )
```

```python
import functools
import math

import jax
import jax.numpy as jnp
import ml_dtypes
import numpy as np
from jax import lax
from jax.experimental import pallas as pl
from jax.experimental.pallas import tpu as pltpu
from jax.sharding import PartitionSpec as P

NIMG = 262144
M = 1024
SUBROWS = 1024
TWO_PI = 2.0 * math.pi

BLOCK = 1024
SPAN = 4096
NODES = 32
RANK = 4
ERANK = 2
ROW_SCALE = 4.0

f32 = jnp.float32
bf16 = jnp.bfloat16


def _split(values):
    high = values.astype(np.float32).astype(ml_dtypes.bfloat16)
    low = (values - high.astype(np.float64)).astype(np.float32).astype(ml_dtypes.bfloat16)
    return high, low


def _kernel_sum(x, count):
    den = np.sin(np.pi * x / NIMG)
    zero = np.abs(den) < 1e-14
    return np.where(zero, float(count), np.sin(np.pi * x * count / NIMG) / np.where(zero, 1.0, den))


def _solve(gram, right):
    gram, right = gram.copy(), right.copy()
    n = len(gram)
    for i in range(n):
        for j in range(i + 1, n):
            factor = gram[j, i] / gram[i, i]
            gram[j] = gram[j] - factor * gram[i]
            right[j] = right[j] - factor * right[i]
    out = np.zeros_like(right)
    for i in range(n - 1, -1, -1):
        total = right[i].copy()
        for j in range(i + 1, n):
            total = total - gram[i, j] * out[j]
        out[i] = total / gram[i, i]
    return out


@functools.lru_cache(maxsize=None)
def _tables():
    scale = TWO_PI / NIMG
    bands = np.arange(M)
    product = (np.arange(BLOCK)[:, None] * bands[None, :]) % NIMG
    angle = (np.float32(scale) * product.astype(np.float32)).astype(np.float64)
    exact = scale * product
    resid_c = np.cos(angle).astype(np.float32).astype(ml_dtypes.bfloat16).astype(np.float64) - np.cos(exact)
    resid_s = np.sin(angle).astype(np.float32).astype(ml_dtypes.bfloat16).astype(np.float64) - np.sin(exact)
    half = M // 2
    resid = np.stack(
        [np.concatenate([resid_c[:, h * half:(h + 1) * half], resid_s[:, h * half:(h + 1) * half]], 1) for h in range(2)]
    ).astype(np.float32).astype(ml_dtypes.bfloat16)
    i = np.arange(NODES)
    nodes = 511.5 + 512 * 1.05 * (0.25 * ((2 * i + 1) / NODES - 1) - 0.75 * np.cos(np.pi * (i + 0.5) / NODES))
    gram = _kernel_sum(nodes[:, None] - nodes[None, :], SPAN) + 1e-13 * SPAN * np.eye(NODES)
    interp = _solve(gram, _kernel_sum(nodes[:, None] - bands[None, :], SPAN))
    centre = (SPAN - 1) / 2
    at = scale * (np.arange(SPAN) - centre)[:, None] * nodes[None, :]
    sample = np.concatenate([np.cos(at), -np.sin(at)], 1)
    sample = np.concatenate(_split(sample), 1)
    rows = []
    for span in range(16384 // SPAN):
        turn = scale * (span * SPAN + centre) * bands
        re, im = interp * np.cos(turn), -interp * np.sin(turn)
        rows.append(np.concatenate([re, im], 1))
        rows.append(np.concatenate([-im, re], 1))
    weave = np.concatenate(rows, 0)
    weave_hi, weave_lo = _split(weave)
    turn = TWO_PI * ((np.arange(16)[:, None] * (bands[None, :half] % 256)) % 256) / 256
    return dict(
        resid=resid, sample=sample, weave_hi=weave_hi, weave_lo=weave_lo,
        turn_c=np.cos(turn).astype(np.float32), turn_s=np.sin(turn).astype(np.float32),
    )


COL_A, COL_SC8, COL_CF8, COL_ROW = 0, 16, 24, 32
CHUNKS = 24


def _angle(product):
    turns = lax.bitwise_and(product + NIMG, 2 * NIMG - 1) - NIMG
    return turns.astype(f32) * (math.pi / NIMG)


def _offset_row(order_ref, offsets_ref, which):
    slots = lax.broadcasted_iota(jnp.int32, (64, 64), 0)
    offsets = offsets_ref[:, which:which + 1].astype(f32)
    return jnp.sum(jnp.where(slots == order_ref[...], offsets, 0.0), axis=0, keepdims=True)


def _to_column(row):
    at = lax.broadcasted_iota(jnp.int32, (64, 64), 0) == lax.broadcasted_iota(jnp.int32, (64, 64), 1)
    return jnp.sum(jnp.where(at, row, 0.0), axis=1, keepdims=True)


def _pick(row, index):
    lane = lax.broadcasted_iota(jnp.int32, row.shape, 1)
    return jnp.sum(jnp.where(lane == index, row, 0.0), axis=1, keepdims=True)


def _prepare_kernel(where_ref, order_ref, offsets_ref, cols_ref, rows_ref, band_ref,
                    lc_ref, ls_ref, pc_ref, ps_ref, mc_ref, ms_ref, wc_ref, ws_ref, combine_ref):
    slot, half = where_ref[0], where_ref[1]
    cf_row = _offset_row(order_ref, offsets_ref, 0)
    own_cf = _pick(cf_row, slot).astype(jnp.int32)
    cf = _to_column(cf_row).astype(jnp.int32)
    sc = _to_column(cols_ref[...].astype(f32)).astype(jnp.int32)
    sr = _to_column(rows_ref[...].astype(f32)).astype(jnp.int32)
    lane = lax.broadcasted_iota(jnp.int32, (64, 128), 1)
    row = lax.bitwise_and(4 * half + 4 * lax.bitwise_and(lane // 8, 1) + lax.bitwise_and(lane, 3), 7)
    odd = 2 * row - 7
    factor = jnp.where(
        lane < COL_SC8, 2 * (own_cf + 1024 * lane),
        jnp.where(lane < COL_CF8, 256 * (lane - COL_SC8), jnp.where(lane < COL_ROW, 256 * (lane - COL_CF8), odd)),
    )
    other = jnp.where(lane < COL_CF8, sc, jnp.where(lane < COL_ROW, cf, sr + 512))
    angle = _angle(factor * other)
    mc, ms = jnp.cos(angle), jnp.sin(angle)
    mc_ref[...] = mc
    ms_ref[...] = ms
    angle = _angle(2 * lane * sc)
    low_c, low_s = jnp.cos(angle), jnp.sin(angle)
    for i in range(8):
        c, s = mc[:, COL_SC8 + i:COL_SC8 + i + 1], ms[:, COL_SC8 + i:COL_SC8 + i + 1]
        lc_ref[:, i * 128:(i + 1) * 128] = c * low_c - s * low_s
        ls_ref[:, i * 128:(i + 1) * 128] = s * low_c + c * low_s
    angle = _angle(2 * lane * cf)
    low_c, low_s = jnp.cos(angle), jnp.sin(angle)
    for i in range(8):
        c, s = mc[:, COL_CF8 + i:COL_CF8 + i + 1], ms[:, COL_CF8 + i:COL_CF8 + i + 1]
        band = band_ref[:, i * 128:(i + 1) * 128]
        pc_ref[:, i * 128:(i + 1) * 128] = (c * low_c - s * low_s) * band
        ps_ref[:, i * 128:(i + 1) * 128] = (s * low_c + c * low_s) * band
    rho = odd.astype(f32) * (0.5 / ROW_SCALE)
    power = jnp.ones((64, 128), f32)
    first = lax.bitwise_and(lane, 4) == 0
    to_re, to_im = jnp.where(first, mc, ms), jnp.where(first, -ms, mc)
    for n in range(RANK):
        wc_ref[n] = mc * power
        ws_ref[n] = ms * power
        if n < ERANK:
            for part, value in ((0, to_re), (1, to_im)):
                base = part * 128 + n * 64
                combine_ref[base:base + 64, :] = (value * power)[:, COL_ROW:COL_ROW + 16].astype(bf16)
        power = power * rho


def _exact_kernel(data_ref, window_ref, lc_ref, ls_ref, mc_ref, ms_ref, wc_ref, ws_ref, sample_ref, out_ref,
                  even_ref, odd_ref, acc_ref):
    def build(block, x_ref):
        bc, bs = _pick(mc_ref[...], block), _pick(ms_ref[...], block)
        for i in range(4):
            cols = slice(i * 256, (i + 1) * 256)
            here = pl.ds(pl.multiple_of(block * BLOCK + i * 256, 256), 256)
            window = window_ref[:, here]
            re_rows = data_ref[0, 0, :, here] * window
            im_rows = data_ref[0, 1, :, here] * window
            for g in range(4):
                rows = slice(g * 16, (g + 1) * 16)
                lc, ls = lc_ref[rows, cols], ls_ref[rows, cols]
                c, s = bc[rows], bs[rows]
                ec = c * lc - s * ls
                es = s * lc + c * ls
                for r in range(4):
                    dr, di = re_rows[r:r + 1], im_rows[r:r + 1]
                    at = r * 64 + g * 16
                    x_ref[at:at + 16, cols] = (dr * ec + di * es).astype(bf16)
                    x_ref[256 + at:256 + at + 16, cols] = (di * ec - dr * es).astype(bf16)

    def add(block, x_ref):
        rows = pl.ds(pl.multiple_of((block % 4) * BLOCK, BLOCK), BLOCK)
        part = jnp.dot(x_ref[...], sample_ref[rows, :], preferred_element_type=f32)
        acc_ref[block // 4] = acc_ref[block // 4] + part

    acc_ref[...] = jnp.zeros_like(acc_ref)
    build(0, even_ref)

    def body(pair, carry):
        add(2 * pair, even_ref)
        build(2 * pair + 1, odd_ref)
        add(2 * pair + 1, odd_ref)
        build((2 * pair + 2) % 16, even_ref)
        return carry

    lax.fori_loop(0, 8, body, 0)

    lane = lax.broadcasted_iota(jnp.int32, (64, 128), 1)
    sign = jnp.where(lax.bitwise_and(lane, 32) == 0, -1.0, 1.0).astype(f32)
    sums = [[None] * 4 for _ in range(RANK)]
    for span in range(4):
        for r in range(4):
            re = acc_ref[span, r * 64:(r + 1) * 64]
            im = acc_ref[span, 256 + r * 64:256 + (r + 1) * 64]
            re = re + pltpu.roll(re, 64, 1)
            im = im + pltpu.roll(im, 64, 1)
            value = re + sign * pltpu.roll(im, 32, 1)
            turned = sign * pltpu.roll(value, 32, 1)
            for n in range(RANK):
                col = slice(COL_ROW + r, COL_ROW + r + 1)
                term = wc_ref[n, :, col] * value - ws_ref[n, :, col] * turned
                sums[n][span] = term if sums[n][span] is None else sums[n][span] + term
    for n in range(RANK):
        out_ref[:, n * 256:n * 256 + 128] = jnp.where(lane < 64, sums[n][0], sums[n][1])
        out_ref[:, n * 256 + 128:n * 256 + 256] = jnp.where(lane < 64, sums[n][2], sums[n][3])


def _residual_kernel(half_ref, own_ref, peer_ref, window_ref, lc_ref, ls_ref, mc_ref, ms_ref, combine_ref, table_ref,
                     tc_ref, ts_ref, nodes_ref, out_ref, even_ref, odd_ref, sum_ref):
    def build(group, z_ref):
        for j in range(4):
            block = group * 4 + j
            bc, bs = _pick(mc_ref[...], block), _pick(ms_ref[...], block)
            for i in range(4):
                cols = slice(i * 256, (i + 1) * 256)
                here = pl.ds(pl.multiple_of(block * BLOCK + i * 256, 256), 256)
                window = window_ref[:, here]
                data = jnp.concatenate(
                    [own_ref[0, 0, :, here], own_ref[0, 1, :, here], peer_ref[0, 0, :, here], peer_ref[0, 1, :, here]], 0
                )
                data = (data * window).astype(bf16)
                rows = jnp.dot(combine_ref[...], data, preferred_element_type=f32)
                lc, ls = lc_ref[:, cols], ls_ref[:, cols]
                ec = bc * lc - bs * ls
                es = bs * lc + bc * ls
                for n in range(ERANK):
                    gr, gi = rows[n * 64:(n + 1) * 64], rows[128 + n * 64:128 + (n + 1) * 64]
                    at = j * 256 + n * 64
                    z_ref[at:at + 64, cols] = (gr * ec + gi * es).astype(bf16)
                    z_ref[at + 128:at + 192, cols] = (gi * ec - gr * es).astype(bf16)

    def add(group, z_ref):
        for kc in range(2):
            cols = slice(kc * 256, (kc + 1) * 256)
            by_c = jnp.dot(z_ref[...], table_ref[0, :, cols], preferred_element_type=f32)
            by_s = jnp.dot(z_ref[...], table_ref[0, :, 512 + kc * 256:768 + kc * 256], preferred_element_type=f32)
            sum_re, sum_im = sum_ref[0, :, cols], sum_ref[1, :, cols]
            for j in range(4):
                re = by_c[j * 256:j * 256 + 128] + by_s[j * 256 + 128:j * 256 + 256]
                im = by_c[j * 256 + 128:j * 256 + 256] - by_s[j * 256:j * 256 + 128]
                tc = tc_ref[pl.ds(group * 4 + j, 1), cols]
                ts = ts_ref[pl.ds(group * 4 + j, 1), cols]
                sum_re = sum_re + (re * tc + im * ts)
                sum_im = sum_im + (im * tc - re * ts)
            sum_ref[0, :, cols] = sum_re
            sum_ref[1, :, cols] = sum_im

    sum_ref[...] = jnp.zeros_like(sum_ref)
    build(0, even_ref)

    def body(pair, carry):
        add(2 * pair, even_ref)
        build(2 * pair + 1, odd_ref)
        add(2 * pair + 1, odd_ref)
        build((2 * pair + 2) % 4, even_ref)
        return carry

    lax.fori_loop(0, 2, body, 0)

    for copy in range(2):
        for n in range(ERANK):
            for part in range(2):
                for kc in range(4):
                    at = copy * CHUNKS + n * 8 + part * 4 + kc
                    out_ref[pl.ds(at, 64, stride=2 * CHUNKS), :] = (
                        sum_ref[part, n * 64:(n + 1) * 64, kc * 128:(kc + 1) * 128]
                    )
        for i in range(8):
            out_ref[pl.ds(copy * CHUNKS + 16 + i, 64, stride=2 * CHUNKS), :] = nodes_ref[:, i * 128:(i + 1) * 128]


def _halves(value):
    high = value.astype(bf16)
    return high, (value - high.astype(f32)).astype(bf16)


def _phase_kernel(where_ref, order_ref, offsets_ref, rows_ref, out_ref):
    slot, half = where_ref[0], where_ref[1]
    rf = _offset_row(order_ref, offsets_ref, 1).astype(jnp.int32)
    own_sr = _pick(rows_ref[...].astype(f32), slot).astype(jnp.int32)
    odd = jnp.concatenate([2 * rf + 7, 2 * rf + 7], 1)
    lane = lax.broadcasted_iota(jnp.int32, (128, 128), 1)
    quarter = jnp.where(lane < 64, 0, -(NIMG // 2))
    sign = jnp.where(lane < 64, -1.0, 1.0).astype(f32)
    for i in range(8):
        here = slice(i * 128, (i + 1) * 128)
        q = lax.broadcasted_iota(jnp.int32, (128, 128), 0) + i * 128 + half * 512
        q = lax.bitwise_and(q, 1023)
        turn = jnp.cos(_angle(odd * (own_sr + q) + quarter))
        other = sign * pltpu.roll(turn, 64, 1)
        g = (q - 512).astype(f32) * (TWO_PI / NIMG * ROW_SCALE)
        g2, g3 = g * g * 0.5, g * g * g * (1.0 / 6.0)
        for n, value in ((0, turn), (1, g * other)):
            high, low = _halves(value)
            out_ref[here, n * 128:(n + 1) * 128] = high
            out_ref[here, 256 + n * 128:256 + (n + 1) * 128] = high
            out_ref[here, 512 + n * 128:512 + (n + 1) * 128] = low
        out_ref[here, 768:896] = (-g2 * turn).astype(bf16)
        out_ref[here, 896:1024] = (-g3 * other).astype(bf16)


def _rows_kernel(got_ref, pc_ref, ps_ref, left_ref, wh_ref, wl_ref, out_ref, right_ref, high_ref, low_ref):
    for n in range(RANK):
        for i in range(2):
            chunk = 16 + n * 2 + i
            value = (
                got_ref[pl.ds(chunk, 64, stride=2 * CHUNKS), :]
                + got_ref[pl.ds(CHUNKS + chunk, 64, stride=2 * CHUNKS), :]
            )
            high, low = _halves(value)
            high_ref[n * 64:(n + 1) * 64, i * 128:(i + 1) * 128] = high
            if n < 2:
                low_ref[n * 64:(n + 1) * 64, i * 128:(i + 1) * 128] = low
    for i in range(4):
        cols = slice(i * 256, (i + 1) * 256)
        vals = []
        for part in range(2):
            wcols = slice(part * 1024 + i * 256, part * 1024 + (i + 1) * 256)
            wh, wl = wh_ref[:, wcols], wl_ref[:, wcols]
            main = jnp.dot(high_ref[...], wh, preferred_element_type=f32)
            rest = (
                jnp.dot(high_ref[0:128], wl, preferred_element_type=f32)
                + jnp.dot(low_ref[...], wh, preferred_element_type=f32)
            )
            vals.append((main, rest))
        pc, ps = pc_ref[:, cols], ps_ref[:, cols]
        for n in range(RANK):
            rows = slice(n * 64, (n + 1) * 64)
            vr, vi = vals[0][0][rows], vals[1][0][rows]
            if n < ERANK:
                parts = []
                for part in range(2):
                    at = (i // 2) * CHUNKS + n * 8 + part * 4 + 2 * (i % 2)
                    parts.append(jnp.concatenate(
                        [got_ref[pl.ds(at + m, 64, stride=2 * CHUNKS), :] for m in range(2)], 1))
                vr = vr + vals[0][1][rows] + parts[0]
                vi = vi + vals[1][1][rows] + parts[1]
            cr = vr * pc + vi * ps
            ci = vi * pc - vr * ps
            for value, part, col in ((cr, 0, 0), (ci, 1, 0), (ci, 0, 1024), (-cr, 1, 1024)):
                ccols = slice(col + i * 256, col + (i + 1) * 256)
                at = n * 128 + part * 64
                if n < 2:
                    high, low = _halves(value)
                    right_ref[at:at + 64, ccols] = high
                    right_ref[256 + at:256 + at + 64, ccols] = low
                    right_ref[512 + at:512 + at + 64, ccols] = high
                else:
                    right_ref[512 + at:512 + at + 64, ccols] = value.astype(bf16)

    total = jnp.zeros((8, 512), f32)
    for part in range(2):
        for i in range(2):
            cols = slice(part * 1024 + i * 512, part * 1024 + (i + 1) * 512)
            result = jnp.dot(left_ref[...], right_ref[:, cols], preferred_element_type=f32)
            out_ref[0, part, :, i * 512:(i + 1) * 512] = result[:512]
            total = total + jnp.sum((result * result).reshape(128, 8, 512), 0)
    mean = jnp.sum(total) / (2.0 * SUBROWS * M)
    factor = lax.rsqrt(jnp.full((8, 128), mean, f32) + 1e-06)[0:1, 0:1]
    for part in range(2):
        out_ref[0, part] = out_ref[0, part] * factor


def per_device(facets, facet_window, band_window, facet_order, facet_offsets, sub_cols, sub_rows):
    tables = _tables()
    peer = lax.ppermute(facets, "rows", [(0, 1), (1, 0)])
    where = jnp.stack([lax.axis_index("facet"), lax.axis_index("rows")]).astype(jnp.int32)
    order, cols, rows = (v.reshape(1, 64) for v in (facet_order, sub_cols, sub_rows))
    window = facet_window.reshape(1, 16384)
    scalars = pl.BlockSpec(memory_space=pltpu.SMEM)
    vmem = pl.BlockSpec(memory_space=pltpu.VMEM)
    shape = jax.ShapeDtypeStruct

    def params(mib):
        return pltpu.CompilerParams(vmem_limit_bytes=mib * 1024 * 1024)

    wide, narrow = shape((64, 1024), f32), shape((64, 128), f32)
    lc, ls, pc, ps, mc, ms, wc, ws, combine = pl.pallas_call(
        _prepare_kernel,
        in_specs=[scalars] + [vmem] * 5,
        out_shape=[wide, wide, wide, wide, narrow, narrow, shape((RANK, 64, 128), f32), shape((RANK, 64, 128), f32),
                   shape((256, 16), bf16)],
        compiler_params=params(16),
        cost_estimate=pl.CostEstimate(flops=10**6, bytes_accessed=10**6, transcendentals=5 * 10**4),
        name="prepare",
    )(where, order, facet_offsets, cols, rows, band_window.reshape(1, M))

    nodes = pl.pallas_call(
        _exact_kernel,
        in_specs=[vmem] * 9,
        out_shape=wide,
        scratch_shapes=[pltpu.VMEM((512, BLOCK), bf16), pltpu.VMEM((512, BLOCK), bf16), pltpu.VMEM((4, 512, 128), f32)],
        compiler_params=params(24),
        cost_estimate=pl.CostEstimate(flops=8 * 10**9, bytes_accessed=2 * 10**6, transcendentals=0),
        name="exact_part",
    )(facets, window, lc, ls, mc, ms, wc, ws, jnp.asarray(tables["sample"]))

    whole = lambda *sizes: pl.BlockSpec(sizes, lambda b, h: (0,) * len(sizes))
    send = pl.pallas_call(
        _residual_kernel,
        grid_spec=pltpu.PrefetchScalarGridSpec(
            num_scalar_prefetch=1,
            grid=(1,),
            in_specs=[
                whole(1, 2, 4, 16384), whole(1, 2, 4, 16384), whole(1, 16384),
                whole(64, 1024), whole(64, 1024), whole(64, 128), whole(64, 128), whole(256, 16),
                pl.BlockSpec((1, 1024, 1024), lambda b, h: (h[1], 0, 0)),
                whole(16, 512), whole(16, 512), whole(64, 1024),
            ],
            out_specs=whole(128 * CHUNKS, 128),
            scratch_shapes=[pltpu.VMEM((1024, 1024), bf16), pltpu.VMEM((1024, 1024), bf16),
                            pltpu.VMEM((2, 128, 512), f32)],
        ),
        out_shape=shape((128 * CHUNKS, 128), f32),
        compiler_params=params(48),
        cost_estimate=pl.CostEstimate(flops=9 * 10**9, bytes_accessed=4 * 10**6, transcendentals=0),
        name="residual_part",
    )(
        where, facets, peer, window, lc, ls, mc, ms, combine,
        jnp.asarray(tables["resid"]), jnp.asarray(tables["turn_c"]), jnp.asarray(tables["turn_s"]), nodes,
    )

    got = lax.all_to_all(send.reshape(128, CHUNKS, 128), ("facet", "rows"), split_axis=0, concat_axis=0, tiled=True)
    left = pl.pallas_call(
        _phase_kernel,
        in_specs=[scalars] + [vmem] * 3,
        out_shape=shape((1024, 1024), bf16),
        compiler_params=params(16),
        cost_estimate=pl.CostEstimate(flops=10**9, bytes_accessed=2 * 10**6, transcendentals=2 * 10**5),
        name="row_phases",
    )(where, order, facet_offsets, rows)

    return pl.pallas_call(
        _rows_kernel,
        in_specs=[vmem] * 6,
        out_shape=shape((1, 2, 512, 1024), f32),
        scratch_shapes=[pltpu.VMEM((1024, 2048), bf16), pltpu.VMEM((256, 256), bf16), pltpu.VMEM((128, 256), bf16)],
        compiler_params=params(40),
        cost_estimate=pl.CostEstimate(flops=5 * 10**9, bytes_accessed=12 * 10**6, transcendentals=0),
        name="row_transform",
    )(got.reshape(128 * CHUNKS, 128), pc, ps, left, jnp.asarray(tables["weave_hi"]), jnp.asarray(tables["weave_lo"]))


def solution(mesh):
    return jax.shard_map(
        per_device,
        mesh=mesh,
        in_specs=(P("facet", None, "rows", None), P(), P(), P(), P(), P(), P()),
        out_specs=P("facet", None, "rows", None),
        check_vma=False,
    )
```

```python
import functools
import math

import jax
import jax.numpy as jnp
import ml_dtypes
import numpy as np
from jax import lax
from jax.experimental import pallas as pl
from jax.experimental.pallas import tpu as pltpu
from jax.sharding import PartitionSpec as P

NIMG = 262144
M = 1024
SUBROWS = 1024
TWO_PI = 2.0 * math.pi

BLOCK = 1024
SPAN = 4096
NODES = 32
RANK = 4
ERANK = 2
ROW_SCALE = 4.0
TABLE_SCALE = 32768.0
DATA_SCALE = 16.0

f32 = jnp.float32
bf16 = jnp.bfloat16
f8 = jnp.float8_e4m3fn


def _split(values):
    high = values.astype(np.float32).astype(ml_dtypes.bfloat16)
    low = (values - high.astype(np.float64)).astype(np.float32).astype(ml_dtypes.bfloat16)
    return high, low


def _kernel_sum(x, count):
    den = np.sin(np.pi * x / NIMG)
    zero = np.abs(den) < 1e-14
    return np.where(zero, float(count), np.sin(np.pi * x * count / NIMG) / np.where(zero, 1.0, den))


def _solve(gram, right):
    gram, right = gram.copy(), right.copy()
    n = len(gram)
    for i in range(n):
        for j in range(i + 1, n):
            factor = gram[j, i] / gram[i, i]
            gram[j] = gram[j] - factor * gram[i]
            right[j] = right[j] - factor * right[i]
    out = np.zeros_like(right)
    for i in range(n - 1, -1, -1):
        total = right[i].copy()
        for j in range(i + 1, n):
            total = total - gram[i, j] * out[j]
        out[i] = total / gram[i, i]
    return out


@functools.lru_cache(maxsize=None)
def _tables():
    scale = TWO_PI / NIMG
    bands = np.arange(M)
    product = (np.arange(BLOCK)[:, None] * bands[None, :]) % NIMG
    angle = (np.float32(scale) * product.astype(np.float32)).astype(np.float64)
    exact = scale * product
    resid_c = np.cos(angle).astype(np.float32).astype(ml_dtypes.bfloat16).astype(np.float64) - np.cos(exact)
    resid_s = np.sin(angle).astype(np.float32).astype(ml_dtypes.bfloat16).astype(np.float64) - np.sin(exact)
    half = M // 2
    resid = np.stack(
        [np.concatenate([resid_c[:, h * half:(h + 1) * half], resid_s[:, h * half:(h + 1) * half]], 1) for h in range(2)]
    )
    resid = (resid * TABLE_SCALE).astype(np.float32).astype(ml_dtypes.float8_e4m3fn)
    i = np.arange(NODES)
    nodes = 511.5 + 512 * 1.05 * (0.25 * ((2 * i + 1) / NODES - 1) - 0.75 * np.cos(np.pi * (i + 0.5) / NODES))
    gram = _kernel_sum(nodes[:, None] - nodes[None, :], SPAN) + 1e-13 * SPAN * np.eye(NODES)
    interp = _solve(gram, _kernel_sum(nodes[:, None] - bands[None, :], SPAN))
    centre = (SPAN - 1) / 2
    at = scale * (np.arange(SPAN) - centre)[:, None] * nodes[None, :]
    sample = np.concatenate([np.cos(at), -np.sin(at)], 1)
    sample = np.concatenate(_split(sample), 1)
    rows = []
    for span in range(16384 // SPAN):
        turn = scale * (span * SPAN + centre) * bands
        re, im = interp * np.cos(turn), -interp * np.sin(turn)
        rows.append(np.concatenate([re, im], 1))
        rows.append(np.concatenate([-im, re], 1))
    weave = np.concatenate(rows, 0)
    weave_hi, weave_lo = _split(weave)
    turn = TWO_PI * ((np.arange(16)[:, None] * (bands[None, :half] % 256)) % 256) / 256
    return dict(
        resid=resid, sample=sample, weave_hi=weave_hi, weave_lo=weave_lo,
        turn_c=np.cos(turn).astype(np.float32), turn_s=np.sin(turn).astype(np.float32),
    )


COL_A, COL_SC8, COL_CF8, COL_ROW = 0, 16, 24, 32
CHUNKS = 24


def _angle(product):
    turns = lax.bitwise_and(product + NIMG, 2 * NIMG - 1) - NIMG
    return turns.astype(f32) * (math.pi / NIMG)


def _offset_row(order_ref, offsets_ref, which):
    slots = lax.broadcasted_iota(jnp.int32, (64, 64), 0)
    offsets = _to_column(offsets_ref[which:which + 1, :].astype(f32))
    return jnp.sum(jnp.where(slots == order_ref[...], offsets, 0.0), axis=0, keepdims=True)


def _to_column(row):
    at = lax.broadcasted_iota(jnp.int32, (64, 64), 0) == lax.broadcasted_iota(jnp.int32, (64, 64), 1)
    return jnp.sum(jnp.where(at, row, 0.0), axis=1, keepdims=True)


def _pick(row, index):
    lane = lax.broadcasted_iota(jnp.int32, row.shape, 1)
    return jnp.sum(jnp.where(lane == index, row, 0.0), axis=1, keepdims=True)


def _prepare(slot, half, order_ref, offsets_ref, cols_ref, rows_ref, band_ref,
             lc_ref, ls_ref, pc_ref, ps_ref, mc_ref, ms_ref, combine_ref, wc_ref, ws_ref):
    cf_row = _offset_row(order_ref, offsets_ref, 0)
    own_cf = _pick(cf_row, slot).astype(jnp.int32)
    cf = _to_column(cf_row).astype(jnp.int32)
    sc = _to_column(cols_ref[...].astype(f32)).astype(jnp.int32)
    sr = _to_column(rows_ref[...].astype(f32)).astype(jnp.int32)
    lane = lax.broadcasted_iota(jnp.int32, (64, 128), 1)
    row = lax.bitwise_and(4 * half + 4 * lax.bitwise_and(lane // 8, 1) + lax.bitwise_and(lane, 3), 7)
    odd = 2 * row - 7
    factor = jnp.where(
        lane < COL_SC8, 2 * (own_cf + 1024 * lane),
        jnp.where(lane < COL_CF8, 256 * (lane - COL_SC8), jnp.where(lane < COL_ROW, 256 * (lane - COL_CF8), odd)),
    )
    other = jnp.where(lane < COL_CF8, sc, jnp.where(lane < COL_ROW, cf, sr + 512))
    angle = _angle(factor * other)
    mc, ms = jnp.cos(angle), jnp.sin(angle)
    mc_ref[...] = mc
    ms_ref[...] = ms
    angle = _angle(2 * lane * sc)
    low_c, low_s = jnp.cos(angle), jnp.sin(angle)
    for i in range(8):
        c, s = mc[:, COL_SC8 + i:COL_SC8 + i + 1], ms[:, COL_SC8 + i:COL_SC8 + i + 1]
        lc_ref[:, i * 128:(i + 1) * 128] = c * low_c - s * low_s
        ls_ref[:, i * 128:(i + 1) * 128] = s * low_c + c * low_s
    angle = _angle(2 * lane * cf)
    low_c, low_s = jnp.cos(angle), jnp.sin(angle)
    for i in range(8):
        c, s = mc[:, COL_CF8 + i:COL_CF8 + i + 1], ms[:, COL_CF8 + i:COL_CF8 + i + 1]
        band = band_ref[:, i * 128:(i + 1) * 128]
        pc_ref[:, i * 128:(i + 1) * 128] = (c * low_c - s * low_s) * band
        ps_ref[:, i * 128:(i + 1) * 128] = (s * low_c + c * low_s) * band
    rho = odd.astype(f32) * (0.5 / ROW_SCALE)
    power = jnp.ones((64, 128), f32)
    first = lax.bitwise_and(lane, 4) == 0
    to_re, to_im = jnp.where(first, mc, ms), jnp.where(first, -ms, mc)
    for n in range(RANK):
        wc_ref[n] = mc * power
        ws_ref[n] = ms * power
        if n < ERANK:
            for part, value in ((0, to_re), (1, to_im)):
                base = part * 128 + n * 64
                combine_ref[base:base + 64, :] = (value * power)[:, COL_ROW:COL_ROW + 16].astype(bf16)
        power = power * rho


def _exact_kernel(order_hbm, offsets_hbm, cols_hbm, rows_hbm, band_hbm, data_hbm, window_hbm, sample_hbm,
                  lc_ref, ls_ref, pc_ref, ps_ref, mc_ref, ms_ref, combine_ref, out_ref,
                  order_ref, offsets_ref, cols_ref, rows_ref, band_ref, data_ref, window_ref, sample_ref,
                  wc_ref, ws_ref, even_ref, odd_ref, acc_ref, sems):
    loads = [
        pltpu.make_async_copy(source, target, sems.at[i])
        for i, (source, target) in enumerate((
            (order_hbm, order_ref), (offsets_hbm, offsets_ref), (cols_hbm, cols_ref), (rows_hbm, rows_ref),
            (band_hbm, band_ref), (data_hbm, data_ref), (window_hbm, window_ref), (sample_hbm, sample_ref),
        ))
    ]
    for load in loads:
        load.start()
    for load in loads[:5]:
        load.wait()
    acc_ref[...] = jnp.zeros_like(acc_ref)
    _prepare(lax.axis_index("facet"), lax.axis_index("rows"), order_ref, offsets_ref, cols_ref, rows_ref, band_ref,
             lc_ref, ls_ref, pc_ref, ps_ref, mc_ref, ms_ref, combine_ref, wc_ref, ws_ref)
    for load in loads[5:]:
        load.wait()

    def build(block, x_ref, bc, bs, i):
        cols = slice(i * 256, (i + 1) * 256)
        here = pl.ds(pl.multiple_of(block * BLOCK + i * 256, 256), 256)
        window = window_ref[:, here]
        re_rows = data_ref[0, 0, :, here] * window
        im_rows = data_ref[0, 1, :, here] * window
        for g in range(4):
            rows = slice(g * 16, (g + 1) * 16)
            lc, ls = lc_ref[rows, cols], ls_ref[rows, cols]
            c, s = bc[rows], bs[rows]
            ec = c * lc - s * ls
            es = s * lc + c * ls
            for r in range(4):
                dr, di = re_rows[r:r + 1], im_rows[r:r + 1]
                at = r * 64 + g * 16
                x_ref[at:at + 16, cols] = (dr * ec + di * es).astype(bf16)
                x_ref[256 + at:256 + at + 16, cols] = (di * ec - dr * es).astype(bf16)

    def turns(block):
        return _pick(mc_ref[...], block), _pick(ms_ref[...], block)

    def stage(block, x_ref, following, next_ref):
        bc, bs = turns(following)
        rows = pl.ds(pl.multiple_of(lax.rem(block, 4) * BLOCK, BLOCK), BLOCK)
        span = block // 4
        for p in range(2):
            half = slice(p * 256, (p + 1) * 256)
            part = jnp.dot(x_ref[half, :], sample_ref[rows, :], preferred_element_type=f32)
            build(following, next_ref, bc, bs, 2 * p)
            build(following, next_ref, bc, bs, 2 * p + 1)
            acc_ref[span, half, :] = acc_ref[span, half, :] + part

    bc, bs = turns(0)
    for i in range(4):
        build(0, even_ref, bc, bs, i)

    def body(pair, carry):
        stage(2 * pair, even_ref, 2 * pair + 1, odd_ref)
        stage(2 * pair + 1, odd_ref, lax.rem(2 * pair + 2, 16), even_ref)
        return carry

    lax.fori_loop(0, 8, body, 0)

    lane = lax.broadcasted_iota(jnp.int32, (64, 128), 1)
    sign = jnp.where(lax.bitwise_and(lane, 32) == 0, -1.0, 1.0).astype(f32)
    sums = [[None] * 4 for _ in range(RANK)]
    for span in range(4):
        for r in range(4):
            re = acc_ref[span, r * 64:(r + 1) * 64]
            im = acc_ref[span, 256 + r * 64:256 + (r + 1) * 64]
            re = re + pltpu.roll(re, 64, 1)
            im = im + pltpu.roll(im, 64, 1)
            value = re + sign * pltpu.roll(im, 32, 1)
            turned = sign * pltpu.roll(value, 32, 1)
            for n in range(RANK):
                col = slice(COL_ROW + r, COL_ROW + r + 1)
                term = wc_ref[n, :, col] * value - ws_ref[n, :, col] * turned
                sums[n][span] = term if sums[n][span] is None else sums[n][span] + term
    for n in range(RANK):
        out_ref[:, n * 256:n * 256 + 128] = jnp.where(lane < 64, sums[n][0], sums[n][1])
        out_ref[:, n * 256 + 128:n * 256 + 256] = jnp.where(lane < 64, sums[n][2], sums[n][3])


def _residual_kernel(own_hbm, peer_hbm, window_hbm, lc_hbm, ls_hbm, mc_hbm, ms_hbm, combine_hbm,
                     table_hbm, tc_hbm, ts_hbm, nodes_hbm, out_ref,
                     own_ref, peer_ref, window_ref, lc_ref, ls_ref, mc_ref, ms_ref, combine_ref,
                     table_ref, tc_ref, ts_ref, nodes_ref, even_ref, odd_ref, sum_ref, sems):
    loads = [
        pltpu.make_async_copy(source, target, sems.at[i])
        for i, (source, target) in enumerate((
            (own_hbm, own_ref), (peer_hbm, peer_ref), (window_hbm, window_ref), (lc_hbm, lc_ref), (ls_hbm, ls_ref),
            (mc_hbm, mc_ref), (ms_hbm, ms_ref), (combine_hbm, combine_ref),
            (table_hbm.at[lax.axis_index("rows")], table_ref), (tc_hbm, tc_ref), (ts_hbm, ts_ref),
            (nodes_hbm, nodes_ref),
        ))
    ]
    for load in loads:
        load.start()
    sum_ref[...] = jnp.zeros_like(sum_ref)
    for load in loads[:3]:
        load.wait()
    largest = jnp.zeros((4, 2048), f32)
    for i in range(8):
        here = slice(i * 2048, (i + 1) * 2048)
        window = window_ref[:, here]
        for ref in (own_ref, peer_ref):
            for part in range(2):
                largest = jnp.maximum(largest, jnp.abs(ref[0, part, :, here] * window))
    largest = jnp.maximum(jnp.max(jnp.max(largest, axis=1, keepdims=True), axis=0, keepdims=True), 1e-30)
    scale_in = DATA_SCALE / largest
    scale_out = largest * (1.0 / (DATA_SCALE * TABLE_SCALE))
    for load in loads[3:8]:
        load.wait()

    def mix(block, i):
        here = pl.ds(pl.multiple_of(block * BLOCK + i * 256, 256), 256)
        window = window_ref[:, here] * scale_in
        data = jnp.concatenate(
            [own_ref[0, 0, :, here], own_ref[0, 1, :, here], peer_ref[0, 0, :, here], peer_ref[0, 1, :, here]], 0
        )
        return jnp.dot(combine_ref[...], (data * window).astype(bf16), preferred_element_type=f32)

    def build(z_ref, j, i, rows, bc, bs):
        cols = slice(i * 256, (i + 1) * 256)
        lc, ls = lc_ref[:, cols], ls_ref[:, cols]
        ec = bc * lc - bs * ls
        es = bs * lc + bc * ls
        for n in range(ERANK):
            gr, gi = rows[n * 64:(n + 1) * 64], rows[128 + n * 64:128 + (n + 1) * 64]
            at = j * 256 + n * 64
            z_ref[at:at + 64, cols] = (gr * ec + gi * es).astype(z_ref.dtype)
            z_ref[at + 128:at + 192, cols] = (gi * ec - gr * es).astype(z_ref.dtype)

    def turns(block):
        return _pick(mc_ref[...], block), _pick(ms_ref[...], block)

    def stage(group, z_ref, following, next_ref):
        tasks = [(j, i) for j in range(2) for i in range(4)]
        spins = [turns(following * 2 + j) for j in range(2)]
        ready = mix(following * 2, 0)
        at = 0
        for j in range(2):
            for kc in range(2):
                cols = slice(kc * 256, (kc + 1) * 256)
                z = z_ref[j * 256:(j + 1) * 256, :]
                by_c = jnp.dot(z, table_ref[:, cols], preferred_element_type=f32)
                by_s = jnp.dot(z, table_ref[:, 512 + kc * 256:768 + kc * 256], preferred_element_type=f32)
                for _ in range(2):
                    bj, bi = tasks[at]
                    at += 1
                    coming = mix(following * 2 + tasks[at][0], tasks[at][1]) if at < 8 else None
                    build(next_ref, bj, bi, ready, *spins[bj])
                    ready = coming
                re = by_c[0:128] + by_s[128:256]
                im = by_c[128:256] - by_s[0:128]
                tc = tc_ref[pl.ds(group * 2 + j, 1), cols]
                ts = ts_ref[pl.ds(group * 2 + j, 1), cols]
                sum_ref[0, :, cols] = sum_ref[0, :, cols] + (re * tc + im * ts)
                sum_ref[1, :, cols] = sum_ref[1, :, cols] + (im * tc - re * ts)

    for j in range(2):
        spin = turns(j)
        for i in range(4):
            build(even_ref, j, i, mix(j, i), *spin)
    for load in loads[8:]:
        load.wait()

    def body(pair, carry):
        stage(2 * pair, even_ref, 2 * pair + 1, odd_ref)
        stage(2 * pair + 1, odd_ref, lax.rem(2 * pair + 2, 8), even_ref)
        return carry

    lax.fori_loop(0, 4, body, 0)

    for copy in range(2):
        for i in range(8):
            out_ref[pl.ds(copy * CHUNKS + 16 + i, 64, stride=2 * CHUNKS), :] = nodes_ref[:, i * 128:(i + 1) * 128]
        for n in range(ERANK):
            for part in range(2):
                for kc in range(4):
                    at = copy * CHUNKS + n * 8 + part * 4 + kc
                    out_ref[pl.ds(at, 64, stride=2 * CHUNKS), :] = (
                        sum_ref[part, n * 64:(n + 1) * 64, kc * 128:(kc + 1) * 128] * scale_out
                    )


def _halves(value):
    high = value.astype(bf16)
    return high, (value - high.astype(f32)).astype(bf16)


def _phase_kernel(order_ref, offsets_ref, rows_ref, left_ref, gram_ref, all_ref, turned_ref):
    slot, half = lax.axis_index("facet"), lax.axis_index("rows")
    rf = _offset_row(order_ref, offsets_ref, 1).astype(jnp.int32)
    own_sr = _pick(rows_ref[...].astype(f32), slot).astype(jnp.int32)
    odd = jnp.concatenate([2 * rf + 7, 2 * rf + 7], 1)
    lane = lax.broadcasted_iota(jnp.int32, (128, 128), 1)
    quarter = jnp.where(lane < 64, 0, -(NIMG // 2))
    sign = jnp.where(lane < 64, -1.0, 1.0).astype(f32)
    for i in range(8):
        here = slice(i * 128, (i + 1) * 128)
        q = lax.broadcasted_iota(jnp.int32, (128, 128), 0) + i * 128 + half * 512
        q = lax.bitwise_and(q, 1023)
        turn = jnp.cos(_angle(odd * (own_sr + q) + quarter))
        other = sign * pltpu.roll(turn, 64, 1)
        g = (q - 512).astype(f32) * (TWO_PI / NIMG * ROW_SCALE)
        g2, g3 = g * g * 0.5, g * g * g * (1.0 / 6.0)
        for n, value in enumerate((turn, g * other, -g2 * turn, -g3 * other)):
            high, low = _halves(value)
            cols = slice(n * 128, (n + 1) * 128)
            all_ref[0, here, cols] = high
            all_ref[1, here, cols] = low
            high_t, low_t = _halves(sign * pltpu.roll(value, 64, 1))
            turned_ref[0, here, cols] = high_t
            turned_ref[1, here, cols] = low_t
            if i < 4 and n < 2:
                left_ref[here, n * 128:(n + 1) * 128] = high
                left_ref[here, 256 + n * 128:256 + (n + 1) * 128] = high
                left_ref[here, 512 + n * 128:512 + (n + 1) * 128] = low
            elif i < 4:
                left_ref[here, 512 + n * 128:512 + (n + 1) * 128] = high
    over_rows = (((0,), (0,)), ((), ()))
    gram = None
    for ref in (all_ref, turned_ref):
        for a, b in ((0, 0), (0, 1), (1, 0)):
            part = lax.dot_general(ref[a], ref[b], over_rows, preferred_element_type=f32)
            gram = part if gram is None else gram + part
    high, low = _halves(gram)
    gram_ref[:, 0:256] = high[:, 0:256]
    gram_ref[:, 256:512] = high[:, 0:256]
    gram_ref[:, 512:768] = low[:, 0:256]
    gram_ref[:, 768:1024] = high[:, 256:512]


def _rows_kernel(got_any, wh_hbm, wl_hbm, pc_hbm, ps_hbm, gram_hbm, left_hbm, out_hbm,
                 got_ref, wh_ref, wl_ref, pc_ref, ps_ref, gram_ref, left_ref, right_ref, value_ref, high_ref, low_ref,
                 out_ref, sems, out_sems):
    loads = [
        pltpu.make_async_copy(source, target, sems.at[i])
        for i, (source, target) in enumerate((
            (got_any, got_ref), (wh_hbm, wh_ref), (wl_hbm, wl_ref), (pc_hbm, pc_ref), (ps_hbm, ps_ref),
            (gram_hbm, gram_ref), (left_hbm, left_ref),
        ))
    ]
    for load in loads:
        load.start()
    loads[0].wait()
    for n in range(RANK):
        for i in range(2):
            chunk = 16 + n * 2 + i
            value = (
                got_ref[pl.ds(chunk, 64, stride=2 * CHUNKS), :]
                + got_ref[pl.ds(CHUNKS + chunk, 64, stride=2 * CHUNKS), :]
            )
            high, low = _halves(value)
            high_ref[n * 64:(n + 1) * 64, i * 128:(i + 1) * 128] = high
            if n < 2:
                low_ref[n * 64:(n + 1) * 64, i * 128:(i + 1) * 128] = low
    for load in loads[1:5]:
        load.wait()
    for i in range(4):
        cols = slice(i * 256, (i + 1) * 256)
        vals = []
        for part in range(2):
            wcols = slice(part * 1024 + i * 256, part * 1024 + (i + 1) * 256)
            wh, wl = wh_ref[:, wcols], wl_ref[:, wcols]
            main = jnp.dot(high_ref[...], wh, preferred_element_type=f32)
            rest = (
                jnp.dot(high_ref[0:128], wl, preferred_element_type=f32)
                + jnp.dot(low_ref[...], wh, preferred_element_type=f32)
            )
            vals.append((main, rest))
        pc, ps = pc_ref[:, cols], ps_ref[:, cols]
        for n in range(RANK):
            rows = slice(n * 64, (n + 1) * 64)
            vr, vi = vals[0][0][rows], vals[1][0][rows]
            if n < ERANK:
                parts = []
                for part in range(2):
                    at = (i // 2) * CHUNKS + n * 8 + part * 4 + 2 * (i % 2)
                    parts.append(jnp.concatenate(
                        [got_ref[pl.ds(at + m, 64, stride=2 * CHUNKS), :] for m in range(2)], 1))
                vr = vr + vals[0][1][rows] + parts[0]
                vi = vi + vals[1][1][rows] + parts[1]
            cr = vr * pc + vi * ps
            ci = vi * pc - vr * ps
            at = n * 128
            value_ref[at:at + 64, cols] = cr
            value_ref[at + 64:at + 128, cols] = ci
            turned = slice(1024 + i * 256, 1024 + (i + 1) * 256)
            cr_high, ci_high = cr.astype(bf16), ci.astype(bf16)
            bases = (0, 512) if n < 2 else (512,)
            for base in bases:
                right_ref[base + at:base + at + 64, cols] = cr_high
                right_ref[base + at + 64:base + at + 128, cols] = ci_high
                right_ref[base + at:base + at + 64, turned] = ci_high
                right_ref[base + at + 64:base + at + 128, turned] = -cr_high
            if n < 2:
                cr_low = (cr - cr_high.astype(f32)).astype(bf16)
                ci_low = (ci - ci_high.astype(f32)).astype(bf16)
                right_ref[256 + at:256 + at + 64, cols] = cr_low
                right_ref[256 + at + 64:256 + at + 128, cols] = ci_low
                right_ref[256 + at:256 + at + 64, turned] = ci_low
                right_ref[256 + at + 64:256 + at + 128, turned] = -cr_low

    loads[5].wait()
    total = jnp.zeros((8, 256), f32)
    for i in range(4):
        cols = slice(i * 256, (i + 1) * 256)
        product = jnp.dot(gram_ref[...], right_ref[:, cols], preferred_element_type=f32) * value_ref[:, cols]
        total = total + jnp.sum(product.reshape(64, 8, 256), 0)
    mean = jnp.maximum(jnp.sum(total), 0.0) / (2.0 * SUBROWS * M)
    factor = lax.rsqrt(jnp.full((8, 128), mean, f32) + 1e-06)[0:1, 0:1]

    loads[6].wait()
    stores = []
    for part in range(2):
        for i in range(4):
            cols = slice(i * 256, (i + 1) * 256)
            right = right_ref[:, part * 1024 + i * 256:part * 1024 + (i + 1) * 256]
            out_ref[part, :, cols] = jnp.dot(left_ref[...], right, preferred_element_type=f32) * factor
            store = pltpu.make_async_copy(
                out_ref.at[part, :, cols], out_hbm.at[0, part, :, cols], out_sems.at[part * 4 + i])
            store.start()
            stores.append(store)
    for store in stores:
        store.wait()


def per_device(facets, facet_window, band_window, facet_order, facet_offsets, sub_cols, sub_rows):
    tables = _tables()
    peer = lax.ppermute(facets, "rows", [(0, 1), (1, 0)])
    order, cols, rows = (v.reshape(1, 64) for v in (facet_order, sub_cols, sub_rows))
    offsets = facet_offsets.T
    window = facet_window.reshape(1, 16384)
    hbm = pl.BlockSpec(memory_space=pltpu.HBM)
    anywhere = pl.BlockSpec(memory_space=pl.ANY)
    vmem = pl.BlockSpec(memory_space=pltpu.VMEM)
    shape = jax.ShapeDtypeStruct

    def params(mib):
        return pltpu.CompilerParams(vmem_limit_bytes=mib * 1024 * 1024)

    wide, narrow = shape((64, 1024), f32), shape((64, 128), f32)
    lc, ls, pc, ps, mc, ms, combine, nodes = pl.pallas_call(
        _exact_kernel,
        in_specs=[hbm] * 8,
        out_shape=[wide, wide, wide, wide, narrow, narrow, shape((256, 16), bf16), wide],
        scratch_shapes=[
            pltpu.VMEM((1, 64), jnp.int32), pltpu.VMEM((2, 64), jnp.int32), pltpu.VMEM((1, 64), jnp.int32),
            pltpu.VMEM((1, 64), jnp.int32), pltpu.VMEM((1, M), f32), pltpu.VMEM((1, 2, 4, 16384), f32),
            pltpu.VMEM((1, 16384), f32), pltpu.VMEM((SPAN, 128), bf16),
            pltpu.VMEM((RANK, 64, 128), f32), pltpu.VMEM((RANK, 64, 128), f32),
            pltpu.VMEM((512, BLOCK), bf16), pltpu.VMEM((512, BLOCK), bf16), pltpu.VMEM((4, 512, 128), f32),
            pltpu.SemaphoreType.DMA((8,)),
        ],
        compiler_params=params(60),
        cost_estimate=pl.CostEstimate(flops=8 * 10**9, bytes_accessed=2 * 10**6, transcendentals=0),
        name="exact_part",
    )(order, offsets, cols, rows, band_window.reshape(1, M), facets, window, jnp.asarray(tables["sample"]))

    send = pl.pallas_call(
        _residual_kernel,
        in_specs=[hbm, anywhere] + [hbm] * 10,
        out_shape=shape((128 * CHUNKS, 128), f32),
        scratch_shapes=[
            pltpu.VMEM((1, 2, 4, 16384), f32), pltpu.VMEM((1, 2, 4, 16384), f32), pltpu.VMEM((1, 16384), f32),
            pltpu.VMEM((64, 1024), f32), pltpu.VMEM((64, 1024), f32), pltpu.VMEM((64, 128), f32),
            pltpu.VMEM((64, 128), f32), pltpu.VMEM((256, 16), bf16),
            pltpu.VMEM((1024, 1024), f8), pltpu.VMEM((16, 512), f32), pltpu.VMEM((16, 512), f32),
            pltpu.VMEM((64, 1024), f32),
            pltpu.VMEM((512, 1024), f8), pltpu.VMEM((512, 1024), f8), pltpu.VMEM((2, 128, 512), f32),
            pltpu.SemaphoreType.DMA((12,)),
        ],
        compiler_params=params(60),
        cost_estimate=pl.CostEstimate(flops=9 * 10**9, bytes_accessed=4 * 10**6, transcendentals=0),
        name="residual_part",
    )(
        facets, peer, window, lc, ls, mc, ms, combine, jnp.asarray(tables["resid"]), jnp.asarray(tables["turn_c"]),
        jnp.asarray(tables["turn_s"]), nodes,
    )

    got = lax.all_to_all(send.reshape(128, CHUNKS, 128), ("facet", "rows"), split_axis=0, concat_axis=0, tiled=True)
    left, gram = pl.pallas_call(
        _phase_kernel,
        in_specs=[vmem] * 3,
        out_shape=[shape((512, 1024), bf16), shape((512, 1024), bf16)],
        scratch_shapes=[pltpu.VMEM((2, 1024, 512), bf16), pltpu.VMEM((2, 1024, 512), bf16)],
        compiler_params=params(60),
        cost_estimate=pl.CostEstimate(flops=3 * 10**9, bytes_accessed=2 * 10**6, transcendentals=2 * 10**5),
        name="row_phases",
    )(order, offsets, rows)

    return pl.pallas_call(
        _rows_kernel,
        in_specs=[anywhere] + [hbm] * 6,
        out_specs=hbm,
        out_shape=shape((1, 2, 512, 1024), f32),
        scratch_shapes=[
            pltpu.VMEM((128 * CHUNKS, 128), f32), pltpu.VMEM((256, 2048), bf16), pltpu.VMEM((256, 2048), bf16),
            pltpu.VMEM((64, 1024), f32), pltpu.VMEM((64, 1024), f32), pltpu.VMEM((512, 1024), bf16),
            pltpu.VMEM((512, 1024), bf16), pltpu.VMEM((1024, 2048), bf16), pltpu.VMEM((512, 1024), f32),
            pltpu.VMEM((256, 256), bf16), pltpu.VMEM((128, 256), bf16), pltpu.VMEM((2, 512, 1024), f32),
            pltpu.SemaphoreType.DMA((7,)), pltpu.SemaphoreType.DMA((8,)),
        ],
        compiler_params=params(60),
        cost_estimate=pl.CostEstimate(flops=5 * 10**9, bytes_accessed=12 * 10**6, transcendentals=0),
        name="row_transform",
    )(got.reshape(128 * CHUNKS, 128), jnp.asarray(tables["weave_hi"]), jnp.asarray(tables["weave_lo"]), pc, ps, gram, left)


def solution(mesh):
    return jax.shard_map(
        per_device,
        mesh=mesh,
        in_specs=(P("facet", None, "rows", None), P(), P(), P(), P(), P(), P()),
        out_specs=P("facet", None, "rows", None),
        check_vma=False,
    )
```

```python
import functools
import math

import jax
import jax.numpy as jnp
import ml_dtypes
import numpy as np
from jax import lax
from jax.experimental import pallas as pl
from jax.experimental.pallas import tpu as pltpu
from jax.sharding import PartitionSpec as P

NIMG = 262144
M = 1024
SUBROWS = 1024
TWO_PI = 2.0 * math.pi

BLOCK = 1024
SPAN = 4096
NODES = 32
RANK = 4
ERANK = 2
ROW_SCALE = 4.0
TABLE_SCALE = 32768.0
DATA_SCALE = 16.0

f32 = jnp.float32
bf16 = jnp.bfloat16
f8 = jnp.float8_e4m3fn


def _split(values):
    high = values.astype(np.float32).astype(ml_dtypes.bfloat16)
    low = (values - high.astype(np.float64)).astype(np.float32).astype(ml_dtypes.bfloat16)
    return high, low


def _kernel_sum(x, count):
    den = np.sin(np.pi * x / NIMG)
    zero = np.abs(den) < 1e-14
    return np.where(zero, float(count), np.sin(np.pi * x * count / NIMG) / np.where(zero, 1.0, den))


def _solve(gram, right):
    gram, right = gram.copy(), right.copy()
    n = len(gram)
    for i in range(n):
        for j in range(i + 1, n):
            factor = gram[j, i] / gram[i, i]
            gram[j] = gram[j] - factor * gram[i]
            right[j] = right[j] - factor * right[i]
    out = np.zeros_like(right)
    for i in range(n - 1, -1, -1):
        total = right[i].copy()
        for j in range(i + 1, n):
            total = total - gram[i, j] * out[j]
        out[i] = total / gram[i, i]
    return out


@functools.lru_cache(maxsize=None)
def _tables():
    scale = TWO_PI / NIMG
    bands = np.arange(M)
    product = (np.arange(BLOCK)[:, None] * bands[None, :]) % NIMG
    angle = (np.float32(scale) * product.astype(np.float32)).astype(np.float64)
    exact = scale * product
    resid_c = np.cos(angle).astype(np.float32).astype(ml_dtypes.bfloat16).astype(np.float64) - np.cos(exact)
    resid_s = np.sin(angle).astype(np.float32).astype(ml_dtypes.bfloat16).astype(np.float64) - np.sin(exact)
    half = M // 2
    resid = np.stack(
        [np.concatenate([resid_c[:, h * half:(h + 1) * half], resid_s[:, h * half:(h + 1) * half]], 1) for h in range(2)]
    )
    resid = (resid * TABLE_SCALE).astype(np.float32).astype(ml_dtypes.float8_e4m3fn)
    i = np.arange(NODES)
    nodes = 511.5 + 512 * 1.05 * (0.25 * ((2 * i + 1) / NODES - 1) - 0.75 * np.cos(np.pi * (i + 0.5) / NODES))
    gram = _kernel_sum(nodes[:, None] - nodes[None, :], SPAN) + 1e-13 * SPAN * np.eye(NODES)
    interp = _solve(gram, _kernel_sum(nodes[:, None] - bands[None, :], SPAN))
    centre = (SPAN - 1) / 2
    at = scale * (np.arange(SPAN) - centre)[:, None] * nodes[None, :]
    sample = np.concatenate([np.cos(at), -np.sin(at)], 1)
    sample = np.concatenate(_split(sample), 1)
    rows = []
    for span in range(16384 // SPAN):
        turn = scale * (span * SPAN + centre) * bands
        rows += [interp * np.cos(turn), interp * np.sin(turn)]
    weave = np.concatenate(rows, 0)
    weave_hi, weave_lo = _split(weave)
    turn = TWO_PI * ((np.arange(16)[:, None] * (bands[None, :half] % 256)) % 256) / 256
    return dict(
        resid=resid, sample=sample, weave_hi=weave_hi, weave_lo=weave_lo,
        turn_c=np.cos(turn).astype(np.float32), turn_s=np.sin(turn).astype(np.float32),
    )


COL_A, COL_SC8, COL_CF8, COL_ROW = 0, 16, 24, 32
CHUNKS = 24


def _angle(product):
    turns = lax.bitwise_and(product + NIMG, 2 * NIMG - 1) - NIMG
    return turns.astype(f32) * (math.pi / NIMG)


def _offset_row(order_ref, offsets_ref, which):
    slots = lax.broadcasted_iota(jnp.int32, (64, 64), 0)
    offsets = _to_column(offsets_ref[which:which + 1, :].astype(f32))
    return jnp.sum(jnp.where(slots == order_ref[...], offsets, 0.0), axis=0, keepdims=True)


def _to_column(row):
    at = lax.broadcasted_iota(jnp.int32, (64, 64), 0) == lax.broadcasted_iota(jnp.int32, (64, 64), 1)
    return jnp.sum(jnp.where(at, row, 0.0), axis=1, keepdims=True)


def _pick(row, index):
    lane = lax.broadcasted_iota(jnp.int32, row.shape, 1)
    return jnp.sum(jnp.where(lane == index, row, 0.0), axis=1, keepdims=True)


def _prepare(slot, half, order_ref, offsets_ref, cols_ref, rows_ref, band_ref,
             lc_ref, ls_ref, pc_ref, ps_ref, mc_ref, ms_ref, combine_ref):
    cf_row = _offset_row(order_ref, offsets_ref, 0)
    own_cf = _pick(cf_row, slot).astype(jnp.int32)
    cf = _to_column(cf_row).astype(jnp.int32)
    sc = _to_column(cols_ref[...].astype(f32)).astype(jnp.int32)
    sr = _to_column(rows_ref[...].astype(f32)).astype(jnp.int32)
    lane = lax.broadcasted_iota(jnp.int32, (64, 128), 1)
    row = lax.bitwise_and(4 * half + 4 * lax.bitwise_and(lane // 8, 1) + lax.bitwise_and(lane, 3), 7)
    odd = 2 * row - 7
    factor = jnp.where(
        lane < COL_SC8, 2 * (own_cf + 1024 * lane),
        jnp.where(lane < COL_CF8, 256 * (lane - COL_SC8), jnp.where(lane < COL_ROW, 256 * (lane - COL_CF8), odd)),
    )
    other = jnp.where(lane < COL_CF8, sc, jnp.where(lane < COL_ROW, cf, sr + 512))
    angle = _angle(factor * other)
    mc, ms = jnp.cos(angle), jnp.sin(angle)
    mc_ref[...] = mc
    ms_ref[...] = ms
    angle = _angle(2 * lane * sc)
    low_c, low_s = jnp.cos(angle), jnp.sin(angle)
    for i in range(8):
        c, s = mc[:, COL_SC8 + i:COL_SC8 + i + 1], ms[:, COL_SC8 + i:COL_SC8 + i + 1]
        lc_ref[:, i * 128:(i + 1) * 128] = c * low_c - s * low_s
        ls_ref[:, i * 128:(i + 1) * 128] = s * low_c + c * low_s
    angle = _angle(2 * lane * cf)
    low_c, low_s = jnp.cos(angle), jnp.sin(angle)
    for i in range(8):
        c, s = mc[:, COL_CF8 + i:COL_CF8 + i + 1], ms[:, COL_CF8 + i:COL_CF8 + i + 1]
        band = band_ref[:, i * 128:(i + 1) * 128]
        pc_ref[:, i * 128:(i + 1) * 128] = (c * low_c - s * low_s) * band
        ps_ref[:, i * 128:(i + 1) * 128] = (s * low_c + c * low_s) * band
    rho = odd.astype(f32) * (0.5 / ROW_SCALE)
    power = jnp.ones((64, 128), f32)
    first = lax.bitwise_and(lane, 4) == 0
    to_re, to_im = jnp.where(first, mc, ms), jnp.where(first, -ms, mc)
    for n in range(ERANK):
        for part, value in ((0, to_re), (1, to_im)):
            base = part * 128 + n * 64
            combine_ref[base:base + 64, :] = (value * power)[:, COL_ROW:COL_ROW + 16].astype(bf16)
        power = power * rho


def _exact_kernel(order_hbm, offsets_hbm, cols_hbm, rows_hbm, band_hbm, data_hbm, window_hbm, sample_hbm,
                  lc_hbm, ls_hbm, pc_hbm, ps_hbm, mc_hbm, ms_hbm, combine_hbm, out_ref,
                  order_ref, offsets_ref, cols_ref, rows_ref, band_ref, data_ref, window_ref, sample_ref,
                  lc_ref, ls_ref, pc_ref, ps_ref, mc_ref, ms_ref, combine_ref,
                  even_ref, odd_ref, acc_ref, sems, out_sems):
    loads = [
        pltpu.make_async_copy(source, target, sems.at[i])
        for i, (source, target) in enumerate((
            (order_hbm, order_ref), (offsets_hbm, offsets_ref), (cols_hbm, cols_ref), (rows_hbm, rows_ref),
            (band_hbm, band_ref), (data_hbm, data_ref), (window_hbm, window_ref), (sample_hbm, sample_ref),
        ))
    ]
    for load in loads:
        load.start()
    for load in loads[:5]:
        load.wait()
    acc_ref[...] = jnp.zeros_like(acc_ref)
    _prepare(lax.axis_index("facet"), lax.axis_index("rows"), order_ref, offsets_ref, cols_ref, rows_ref, band_ref,
             lc_ref, ls_ref, pc_ref, ps_ref, mc_ref, ms_ref, combine_ref)
    stores = [
        pltpu.make_async_copy(source, target, out_sems.at[i])
        for i, (source, target) in enumerate((
            (lc_ref, lc_hbm), (ls_ref, ls_hbm), (pc_ref, pc_hbm), (ps_ref, ps_hbm), (mc_ref, mc_hbm), (ms_ref, ms_hbm),
            (combine_ref, combine_hbm),
        ))
    ]
    for store in stores:
        store.start()
    for load in loads[5:]:
        load.wait()

    def build(block, x_ref, bc, bs, i):
        cols = slice(i * 256, (i + 1) * 256)
        here = pl.ds(pl.multiple_of(block * BLOCK + i * 256, 256), 256)
        window = window_ref[:, here]
        re_rows = data_ref[0, 0, :, here] * window
        im_rows = data_ref[0, 1, :, here] * window
        for g in range(4):
            rows = slice(g * 16, (g + 1) * 16)
            lc, ls = lc_ref[rows, cols], ls_ref[rows, cols]
            c, s = bc[rows], bs[rows]
            ec = c * lc - s * ls
            es = s * lc + c * ls
            for r in range(4):
                dr, di = re_rows[r:r + 1], im_rows[r:r + 1]
                at = r * 64 + g * 16
                x_ref[at:at + 16, cols] = (dr * ec + di * es).astype(bf16)
                x_ref[256 + at:256 + at + 16, cols] = (di * ec - dr * es).astype(bf16)

    def turns(block):
        return _pick(mc_ref[...], block), _pick(ms_ref[...], block)

    def stage(block, x_ref, following, next_ref):
        bc, bs = turns(following)
        span = block // 4
        for i in range(4):
            rows = pl.ds(pl.multiple_of(lax.rem(block, 4) * BLOCK + i * 256, 256), 256)
            part = jnp.dot(x_ref[:, i * 256:(i + 1) * 256], sample_ref[rows, :], preferred_element_type=f32)
            build(following, next_ref, bc, bs, i)
            acc_ref[span] = acc_ref[span] + part

    bc, bs = turns(0)
    for i in range(4):
        build(0, even_ref, bc, bs, i)

    def body(pair, carry):
        stage(2 * pair, even_ref, 2 * pair + 1, odd_ref)
        stage(2 * pair + 1, odd_ref, lax.rem(2 * pair + 2, 16), even_ref)
        return carry

    lax.fori_loop(0, 8, body, 0)

    first = lax.broadcasted_iota(jnp.int32, (64, 128), 1) < 64
    lane = lax.broadcasted_iota(jnp.int32, (64, 128), 1)
    sign = jnp.where(lax.bitwise_and(lane, 32) == 0, -1.0, 1.0).astype(f32)
    half = lax.axis_index("rows")
    places = [(8 * half + 2 * r - 7).astype(f32) * (0.5 / ROW_SCALE) for r in range(4)]
    spins = [
        [jnp.broadcast_to(ref[:, COL_ROW + r:COL_ROW + r + 1], (64, 128)) for ref in (mc_ref, ms_ref)] for r in range(4)
    ]
    for pair in range(2):
        sums = []
        for span in (2 * pair, 2 * pair + 1):
            direct, across = [None] * RANK, [None] * RANK
            for r in range(4):
                c, s = spins[r]
                re = acc_ref[span, r * 64:(r + 1) * 64]
                im = acc_ref[span, 256 + r * 64:256 + (r + 1) * 64]
                one, two = c * re + s * im, c * im - s * re
                for n in range(RANK):
                    direct[n] = one if r == 0 else direct[n] + one
                    across[n] = two if r == 0 else across[n] + two
                    one, two = one * places[r], two * places[r]
            sums.append((direct, across))
        for n in range(RANK):
            folded = []
            for which in range(2):
                a, b = sums[0][which][n], sums[1][which][n]
                folded.append(jnp.where(first, a, b) + pltpu.roll(jnp.where(first, b, a), 64, 1))
            at = n * 256 + pair * 128
            out_ref[:, at:at + 128] = folded[0] + jnp.where(
                sign < 0, -pltpu.roll(folded[1], 96, 1), pltpu.roll(folded[1], 32, 1))
    for store in stores:
        store.wait()


def _residual_kernel(own_hbm, peer_any, window_hbm, lc_hbm, ls_hbm, mc_hbm, ms_hbm, combine_hbm,
                     table_hbm, tc_hbm, ts_hbm, nodes_hbm, out_ref,
                     own_ref, peer_ref, window_ref, lc_ref, ls_ref, mc_ref, ms_ref, combine_ref,
                     table_ref, tc_ref, ts_ref, nodes_ref, cos_ref, sin_ref, even_ref, odd_ref, sum_ref, sems):
    loads = [
        pltpu.make_async_copy(source, target, sems.at[i])
        for i, (source, target) in enumerate((
            (own_hbm, own_ref), (peer_any, peer_ref), (window_hbm, window_ref), (lc_hbm, lc_ref), (ls_hbm, ls_ref),
            (mc_hbm, mc_ref), (ms_hbm, ms_ref), (combine_hbm, combine_ref),
            (table_hbm.at[lax.axis_index("rows")], table_ref), (tc_hbm, tc_ref), (ts_hbm, ts_ref),
            (nodes_hbm, nodes_ref),
        ))
    ]
    for load in loads:
        load.start()
    sum_ref[...] = jnp.zeros_like(sum_ref)
    for load in loads[:3]:
        load.wait()
    largest = jnp.zeros((4, 2048), f32)
    for i in range(8):
        here = slice(i * 2048, (i + 1) * 2048)
        window = window_ref[:, here]
        for ref in (own_ref, peer_ref):
            for part in range(2):
                largest = jnp.maximum(largest, jnp.abs(ref[0, part, :, here] * window))
    largest = jnp.maximum(jnp.max(jnp.max(largest, axis=1, keepdims=True), axis=0, keepdims=True), 1e-30)
    scale_in = DATA_SCALE / largest
    scale_out = largest * (1.0 / (DATA_SCALE * TABLE_SCALE))
    for load in loads[3:8]:
        load.wait()
    cos_ref[...] = lc_ref[...].astype(bf16)
    sin_ref[...] = ls_ref[...].astype(bf16)

    def mix(block, i):
        here = pl.ds(pl.multiple_of(block * BLOCK + i * 256, 256), 256)
        window = window_ref[:, here] * scale_in
        data = jnp.concatenate(
            [own_ref[0, 0, :, here], own_ref[0, 1, :, here], peer_ref[0, 0, :, here], peer_ref[0, 1, :, here]], 0
        )
        return jnp.dot(combine_ref[...], (data * window).astype(bf16), preferred_element_type=f32)

    def build(z_ref, j, i, rows, bc, bs):
        cols = slice(i * 256, (i + 1) * 256)
        lc, ls = cos_ref[:, cols], sin_ref[:, cols]
        ec = bc * lc - bs * ls
        es = bs * lc + bc * ls
        rows = rows.astype(bf16)
        for n in range(ERANK):
            gr, gi = rows[n * 64:(n + 1) * 64], rows[128 + n * 64:128 + (n + 1) * 64]
            at = j * 256 + n * 64
            z_ref[at:at + 64, cols] = (gr * ec + gi * es).astype(z_ref.dtype)
            z_ref[at + 128:at + 192, cols] = (gi * ec - gr * es).astype(z_ref.dtype)

    def turns(block):
        return tuple(
            jnp.broadcast_to(_pick(ref[...], block), (64, 256)).astype(bf16) for ref in (mc_ref, ms_ref)
        )

    def stage(group, z_ref, following, next_ref):
        tasks = [(j, i) for j in range(2) for i in range(4)]
        spins = [turns(following * 2 + j) for j in range(2)]
        ready = mix(following * 2, 0)
        at = 0
        for j in range(2):
            for kc in range(2):
                cols = slice(kc * 256, (kc + 1) * 256)
                z = z_ref[j * 256:(j + 1) * 256, :]
                by_c = jnp.dot(z, table_ref[:, cols], preferred_element_type=f32)
                by_s = jnp.dot(z, table_ref[:, 512 + kc * 256:768 + kc * 256], preferred_element_type=f32)
                for _ in range(2):
                    bj, bi = tasks[at]
                    at += 1
                    coming = mix(following * 2 + tasks[at][0], tasks[at][1]) if at < 8 else None
                    build(next_ref, bj, bi, ready, *spins[bj])
                    ready = coming
                re = by_c[0:128] + by_s[128:256]
                im = by_c[128:256] - by_s[0:128]
                tc = tc_ref[pl.ds(group * 2 + j, 1), cols]
                ts = ts_ref[pl.ds(group * 2 + j, 1), cols]
                sum_ref[0, :, cols] = sum_ref[0, :, cols] + (re * tc + im * ts)
                sum_ref[1, :, cols] = sum_ref[1, :, cols] + (im * tc - re * ts)

    for j in range(2):
        spin = turns(j)
        for i in range(4):
            build(even_ref, j, i, mix(j, i), *spin)
    for load in loads[8:]:
        load.wait()

    def body(pair, carry):
        stage(2 * pair, even_ref, 2 * pair + 1, odd_ref)
        stage(2 * pair + 1, odd_ref, lax.rem(2 * pair + 2, 8), even_ref)
        return carry

    lax.fori_loop(0, 4, body, 0)

    for copy in range(2):
        for i in range(8):
            out_ref[pl.ds(copy * CHUNKS + 16 + i, 64, stride=2 * CHUNKS), :] = nodes_ref[:, i * 128:(i + 1) * 128]
        for n in range(ERANK):
            for part in range(2):
                for kc in range(4):
                    at = copy * CHUNKS + n * 8 + part * 4 + kc
                    out_ref[pl.ds(at, 64, stride=2 * CHUNKS), :] = (
                        sum_ref[part, n * 64:(n + 1) * 64, kc * 128:(kc + 1) * 128] * scale_out
                    )


def _halves(value):
    high = value.astype(bf16)
    return high, (value - high.astype(f32)).astype(bf16)


def _phase_kernel(order_ref, offsets_ref, rows_ref, left_ref, gram_ref, all_ref, turned_ref):
    slot, half = lax.axis_index("facet"), lax.axis_index("rows")
    rf = _offset_row(order_ref, offsets_ref, 1).astype(jnp.int32)
    own_sr = _pick(rows_ref[...].astype(f32), slot).astype(jnp.int32)
    odd = jnp.concatenate([2 * rf + 7, 2 * rf + 7], 1)
    lane = lax.broadcasted_iota(jnp.int32, (128, 128), 1)
    quarter = jnp.where(lane < 64, 0, -(NIMG // 2))
    sign = jnp.where(lane < 64, -1.0, 1.0).astype(f32)
    for i in range(8):
        here = slice(i * 128, (i + 1) * 128)
        q = lax.broadcasted_iota(jnp.int32, (128, 128), 0) + i * 128 + half * 512
        q = lax.bitwise_and(q, 1023)
        turn = jnp.cos(_angle(odd * (own_sr + q) + quarter))
        other = sign * pltpu.roll(turn, 64, 1)
        g = (q - 512).astype(f32) * (TWO_PI / NIMG * ROW_SCALE)
        g2, g3 = g * g * 0.5, g * g * g * (1.0 / 6.0)
        for n, value in enumerate((turn, g * other, -g2 * turn, -g3 * other)):
            high, low = _halves(value)
            cols = slice(n * 128, (n + 1) * 128)
            all_ref[0, here, cols] = high
            all_ref[1, here, cols] = low
            high_t, low_t = _halves(sign * pltpu.roll(value, 64, 1))
            turned_ref[0, here, cols] = high_t
            turned_ref[1, here, cols] = low_t
            if i < 4 and n < 2:
                left_ref[here, n * 128:(n + 1) * 128] = high
                left_ref[here, 256 + n * 128:256 + (n + 1) * 128] = high
                left_ref[here, 512 + n * 128:512 + (n + 1) * 128] = low
            elif i < 4:
                left_ref[here, 512 + n * 128:512 + (n + 1) * 128] = high
    over_rows = (((0,), (0,)), ((), ()))
    gram = None
    for ref in (all_ref, turned_ref):
        for a, b in ((0, 0), (0, 1), (1, 0)):
            part = lax.dot_general(ref[a], ref[b], over_rows, preferred_element_type=f32)
            gram = part if gram is None else gram + part
    high, low = _halves(gram)
    gram_ref[:, 0:256] = high[:, 0:256]
    gram_ref[:, 256:512] = high[:, 0:256]
    gram_ref[:, 512:768] = low[:, 0:256]
    gram_ref[:, 768:1024] = high[:, 256:512]


def _rows_kernel(got_any, wh_hbm, wl_hbm, pc_hbm, ps_hbm, gram_hbm, left_hbm, out_hbm,
                 got_ref, wh_ref, wl_ref, pc_ref, ps_ref, gram_ref, left_ref, right_ref, value_ref, high_ref, low_ref,
                 out_ref, sems, out_sems):
    loads = [
        pltpu.make_async_copy(source, target, sems.at[i])
        for i, (source, target) in enumerate((
            (got_any, got_ref), (wh_hbm, wh_ref), (wl_hbm, wl_ref), (pc_hbm, pc_ref), (ps_hbm, ps_ref),
            (gram_hbm, gram_ref), (left_hbm, left_ref),
        ))
    ]
    for load in loads:
        load.start()
    loads[0].wait()
    second = lax.bitwise_and(lax.broadcasted_iota(jnp.int32, (64, 128), 1), 32) != 0
    for n in range(RANK):
        for i in range(2):
            chunk = 16 + n * 2 + i
            value = (
                got_ref[pl.ds(chunk, 64, stride=2 * CHUNKS), :]
                + got_ref[pl.ds(CHUNKS + chunk, 64, stride=2 * CHUNKS), :]
            )
            high, low = _halves(value)
            for part in range(2):
                high_ref[part, n * 64:(n + 1) * 64, i * 128:(i + 1) * 128] = high.astype(bf16)
                if n < 2:
                    low_ref[part, n * 64:(n + 1) * 64, i * 128:(i + 1) * 128] = low.astype(bf16)
                high, low = (
                    jnp.where(second, -pltpu.roll(v.astype(f32), 32, 1), pltpu.roll(v.astype(f32), 96, 1)) for v in (high, low)
                )
    for load in loads[1:5]:
        load.wait()
    for i in range(4):
        cols = slice(i * 256, (i + 1) * 256)
        vals = []
        for part in range(2):
            wh, wl = wh_ref[:, cols], wl_ref[:, cols]
            main = jnp.dot(high_ref[part], wh, preferred_element_type=f32)
            rest = (
                jnp.dot(high_ref[part, 0:128], wl, preferred_element_type=f32)
                + jnp.dot(low_ref[part], wh, preferred_element_type=f32)
            )
            vals.append((main, rest))
        pc, ps = pc_ref[:, cols], ps_ref[:, cols]
        for n in range(RANK):
            rows = slice(n * 64, (n + 1) * 64)
            vr, vi = vals[0][0][rows], vals[1][0][rows]
            if n < ERANK:
                parts = []
                for part in range(2):
                    at = (i // 2) * CHUNKS + n * 8 + part * 4 + 2 * (i % 2)
                    parts.append(jnp.concatenate(
                        [got_ref[pl.ds(at + m, 64, stride=2 * CHUNKS), :] for m in range(2)], 1))
                vr = vr + vals[0][1][rows] + parts[0]
                vi = vi + vals[1][1][rows] + parts[1]
            cr = vr * pc + vi * ps
            ci = vi * pc - vr * ps
            at = n * 128
            value_ref[at:at + 64, cols] = cr
            value_ref[at + 64:at + 128, cols] = ci
            turned = slice(1024 + i * 256, 1024 + (i + 1) * 256)
            cr_high, ci_high = cr.astype(bf16), ci.astype(bf16)
            bases = (0, 512) if n < 2 else (512,)
            for base in bases:
                right_ref[base + at:base + at + 64, cols] = cr_high
                right_ref[base + at + 64:base + at + 128, cols] = ci_high
                right_ref[base + at:base + at + 64, turned] = ci_high
                right_ref[base + at + 64:base + at + 128, turned] = -cr_high
            if n < 2:
                cr_low = (cr - cr_high.astype(f32)).astype(bf16)
                ci_low = (ci - ci_high.astype(f32)).astype(bf16)
                right_ref[256 + at:256 + at + 64, cols] = cr_low
                right_ref[256 + at + 64:256 + at + 128, cols] = ci_low
                right_ref[256 + at:256 + at + 64, turned] = ci_low
                right_ref[256 + at + 64:256 + at + 128, turned] = -cr_low

    loads[5].wait()
    total = jnp.zeros((8, 256), f32)
    for i in range(4):
        cols = slice(i * 256, (i + 1) * 256)
        product = jnp.dot(gram_ref[...], right_ref[:, cols], preferred_element_type=f32) * value_ref[:, cols]
        total = total + jnp.sum(product.reshape(64, 8, 256), 0)
    mean = jnp.maximum(jnp.sum(total), 0.0) / (2.0 * SUBROWS * M)
    factor = lax.rsqrt(jnp.full((8, 128), mean, f32) + 1e-06)[0:1, 0:1]

    loads[6].wait()
    stores = []
    for part in range(2):
        for i in range(4):
            cols = slice(i * 256, (i + 1) * 256)
            right = right_ref[:, part * 1024 + i * 256:part * 1024 + (i + 1) * 256]
            out_ref[part, :, cols] = jnp.dot(left_ref[...], right, preferred_element_type=f32) * factor
            store = pltpu.make_async_copy(
                out_ref.at[part, :, cols], out_hbm.at[0, part, :, cols], out_sems.at[part * 4 + i])
            store.start()
            stores.append(store)
    for store in stores:
        store.wait()


def per_device(facets, facet_window, band_window, facet_order, facet_offsets, sub_cols, sub_rows):
    tables = _tables()
    peer = lax.ppermute(facets, "rows", [(0, 1), (1, 0)])
    order, cols, rows = (v.reshape(1, 64) for v in (facet_order, sub_cols, sub_rows))
    offsets = facet_offsets.T
    window = facet_window.reshape(1, 16384)
    hbm = pl.BlockSpec(memory_space=pltpu.HBM)
    anywhere = pl.BlockSpec(memory_space=pl.ANY)
    vmem = pl.BlockSpec(memory_space=pltpu.VMEM)
    shape = jax.ShapeDtypeStruct

    def params(mib):
        return pltpu.CompilerParams(vmem_limit_bytes=mib * 1024 * 1024)

    wide, narrow = shape((64, 1024), f32), shape((64, 128), f32)
    lc, ls, pc, ps, mc, ms, combine, nodes = pl.pallas_call(
        _exact_kernel,
        in_specs=[hbm] * 8,
        out_specs=[hbm] * 7 + [vmem],
        out_shape=[wide, wide, wide, wide, narrow, narrow, shape((256, 16), bf16), wide],
        scratch_shapes=[
            pltpu.VMEM((1, 64), jnp.int32), pltpu.VMEM((2, 64), jnp.int32), pltpu.VMEM((1, 64), jnp.int32),
            pltpu.VMEM((1, 64), jnp.int32), pltpu.VMEM((1, M), f32), pltpu.VMEM((1, 2, 4, 16384), f32),
            pltpu.VMEM((1, 16384), f32), pltpu.VMEM((SPAN, 128), bf16),
            pltpu.VMEM((64, 1024), f32), pltpu.VMEM((64, 1024), f32), pltpu.VMEM((64, 1024), f32),
            pltpu.VMEM((64, 1024), f32), pltpu.VMEM((64, 128), f32), pltpu.VMEM((64, 128), f32),
            pltpu.VMEM((256, 16), bf16),
            pltpu.VMEM((512, BLOCK), bf16), pltpu.VMEM((512, BLOCK), bf16), pltpu.VMEM((4, 512, 128), f32),
            pltpu.SemaphoreType.DMA((8,)), pltpu.SemaphoreType.DMA((7,)),
        ],
        compiler_params=params(60),
        cost_estimate=pl.CostEstimate(flops=8 * 10**9, bytes_accessed=2 * 10**6, transcendentals=0),
        name="exact_part",
    )(order, offsets, cols, rows, band_window.reshape(1, M), facets, window, jnp.asarray(tables["sample"]))

    send = pl.pallas_call(
        _residual_kernel,
        in_specs=[hbm, anywhere] + [hbm] * 10,
        out_shape=shape((128 * CHUNKS, 128), f32),
        scratch_shapes=[
            pltpu.VMEM((1, 2, 4, 16384), f32), pltpu.VMEM((1, 2, 4, 16384), f32), pltpu.VMEM((1, 16384), f32),
            pltpu.VMEM((64, 1024), f32), pltpu.VMEM((64, 1024), f32), pltpu.VMEM((64, 128), f32),
            pltpu.VMEM((64, 128), f32), pltpu.VMEM((256, 16), bf16),
            pltpu.VMEM((1024, 1024), f8), pltpu.VMEM((16, 512), f32), pltpu.VMEM((16, 512), f32),
            pltpu.VMEM((64, 1024), f32), pltpu.VMEM((64, 1024), bf16), pltpu.VMEM((64, 1024), bf16),
            pltpu.VMEM((512, 1024), f8), pltpu.VMEM((512, 1024), f8), pltpu.VMEM((2, 128, 512), f32),
            pltpu.SemaphoreType.DMA((12,)),
        ],
        compiler_params=params(60),
        cost_estimate=pl.CostEstimate(flops=9 * 10**9, bytes_accessed=4 * 10**6, transcendentals=0),
        name="residual_part",
    )(
        facets, peer, window, lc, ls, mc, ms, combine, jnp.asarray(tables["resid"]), jnp.asarray(tables["turn_c"]),
        jnp.asarray(tables["turn_s"]), nodes,
    )

    got = lax.all_to_all(send.reshape(128, CHUNKS, 128), ("facet", "rows"), split_axis=0, concat_axis=0, tiled=True)
    left, gram = pl.pallas_call(
        _phase_kernel,
        in_specs=[vmem] * 3,
        out_shape=[shape((512, 1024), bf16), shape((512, 1024), bf16)],
        scratch_shapes=[pltpu.VMEM((2, 1024, 512), bf16), pltpu.VMEM((2, 1024, 512), bf16)],
        compiler_params=params(60),
        cost_estimate=pl.CostEstimate(flops=3 * 10**9, bytes_accessed=2 * 10**6, transcendentals=2 * 10**5),
        name="row_phases",
    )(order, offsets, rows)

    return pl.pallas_call(
        _rows_kernel,
        in_specs=[anywhere] + [hbm] * 6,
        out_specs=hbm,
        out_shape=shape((1, 2, 512, 1024), f32),
        scratch_shapes=[
            pltpu.VMEM((128 * CHUNKS, 128), f32), pltpu.VMEM((256, 1024), bf16), pltpu.VMEM((256, 1024), bf16),
            pltpu.VMEM((64, 1024), f32), pltpu.VMEM((64, 1024), f32), pltpu.VMEM((512, 1024), bf16),
            pltpu.VMEM((512, 1024), bf16), pltpu.VMEM((1024, 2048), bf16), pltpu.VMEM((512, 1024), f32),
            pltpu.VMEM((2, 256, 256), bf16), pltpu.VMEM((2, 128, 256), bf16), pltpu.VMEM((2, 512, 1024), f32),
            pltpu.SemaphoreType.DMA((7,)), pltpu.SemaphoreType.DMA((8,)),
        ],
        compiler_params=params(60),
        cost_estimate=pl.CostEstimate(flops=5 * 10**9, bytes_accessed=12 * 10**6, transcendentals=0),
        name="row_transform",
    )(got.reshape(128 * CHUNKS, 128), jnp.asarray(tables["weave_hi"]), jnp.asarray(tables["weave_lo"]), pc, ps, gram, left)


def solution(mesh):
    return jax.shard_map(
        per_device,
        mesh=mesh,
        in_specs=(P("facet", None, "rows", None), P(), P(), P(), P(), P(), P()),
        out_specs=P("facet", None, "rows", None),
        check_vma=False,
    )
```

```python
import functools
import math

import jax
import jax.numpy as jnp
import ml_dtypes
import numpy as np
from jax import lax
from jax.experimental import pallas as pl
from jax.experimental.pallas import tpu as pltpu
from jax.sharding import PartitionSpec as P

NIMG = 262144
M = 1024
SUBROWS = 1024
TWO_PI = 2.0 * math.pi

BLOCK = 1024
SPAN = 4096
NODES = 32
RANK = 4
OWN_RANK = 3
ERANK = 2
ROW_SCALE = 4.0
TABLE_SCALE = 32768.0
DATA_SCALE = 16.0

f32 = jnp.float32
bf16 = jnp.bfloat16
f8 = jnp.float8_e4m3fn


def _split(values):
    high = values.astype(np.float32).astype(ml_dtypes.bfloat16)
    low = (values - high.astype(np.float64)).astype(np.float32).astype(ml_dtypes.bfloat16)
    return high, low


def _kernel_sum(x, count):
    den = np.sin(np.pi * x / NIMG)
    zero = np.abs(den) < 1e-14
    return np.where(zero, float(count), np.sin(np.pi * x * count / NIMG) / np.where(zero, 1.0, den))


def _solve(gram, right):
    gram, right = gram.copy(), right.copy()
    n = len(gram)
    for i in range(n):
        for j in range(i + 1, n):
            factor = gram[j, i] / gram[i, i]
            gram[j] = gram[j] - factor * gram[i]
            right[j] = right[j] - factor * right[i]
    out = np.zeros_like(right)
    for i in range(n - 1, -1, -1):
        total = right[i].copy()
        for j in range(i + 1, n):
            total = total - gram[i, j] * out[j]
        out[i] = total / gram[i, i]
    return out


@functools.lru_cache(maxsize=None)
def _tables():
    scale = TWO_PI / NIMG
    bands = np.arange(M)
    product = (np.arange(BLOCK)[:, None] * bands[None, :]) % NIMG
    angle = (np.float32(scale) * product.astype(np.float32)).astype(np.float64)
    exact = scale * product
    resid_c = np.cos(angle).astype(np.float32).astype(ml_dtypes.bfloat16).astype(np.float64) - np.cos(exact)
    resid_s = np.sin(angle).astype(np.float32).astype(ml_dtypes.bfloat16).astype(np.float64) - np.sin(exact)
    half = M // 2
    resid = np.stack(
        [np.concatenate([resid_c[:, h * half:(h + 1) * half], resid_s[:, h * half:(h + 1) * half]], 1) for h in range(2)]
    )
    resid = (resid * TABLE_SCALE).astype(np.float32).astype(ml_dtypes.float8_e4m3fn)
    i = np.arange(NODES)
    nodes = 511.5 + 512 * 1.05 * (0.25 * ((2 * i + 1) / NODES - 1) - 0.75 * np.cos(np.pi * (i + 0.5) / NODES))
    gram = _kernel_sum(nodes[:, None] - nodes[None, :], SPAN) + 1e-13 * SPAN * np.eye(NODES)
    interp = _solve(gram, _kernel_sum(nodes[:, None] - bands[None, :], SPAN))
    centre = (SPAN - 1) / 2
    at = scale * (np.arange(SPAN) - centre)[:, None] * nodes[None, :]
    sample = np.concatenate([np.cos(at), -np.sin(at)], 1)
    sample = np.concatenate(_split(sample), 1)
    rows = []
    for span in range(16384 // SPAN):
        turn = scale * (span * SPAN + centre) * bands
        rows += [interp * np.cos(turn), interp * np.sin(turn)]
    weave = np.concatenate(rows, 0)
    weave_hi, weave_lo = _split(weave)
    turn = TWO_PI * ((np.arange(16)[:, None] * (bands[None, :half] % 256)) % 256) / 256
    return dict(
        resid=resid, sample=sample, weave_hi=weave_hi, weave_lo=weave_lo,
        turn_c=np.cos(turn).astype(np.float32), turn_s=np.sin(turn).astype(np.float32),
    )


COL_A, COL_SC8, COL_CF8, COL_ROW = 0, 16, 24, 32
CHUNKS = 22


def _angle(product):
    turns = lax.bitwise_and(product + NIMG, 2 * NIMG - 1) - NIMG
    return turns.astype(f32) * (math.pi / NIMG)


def _offset_row(order_ref, offsets_ref, which):
    slots = lax.broadcasted_iota(jnp.int32, (64, 64), 0)
    offsets = _to_column(offsets_ref[which:which + 1, :].astype(f32))
    return jnp.sum(jnp.where(slots == order_ref[...], offsets, 0.0), axis=0, keepdims=True)


def _to_column(row):
    at = lax.broadcasted_iota(jnp.int32, (64, 64), 0) == lax.broadcasted_iota(jnp.int32, (64, 64), 1)
    return jnp.sum(jnp.where(at, row, 0.0), axis=1, keepdims=True)


def _pick(row, index):
    lane = lax.broadcasted_iota(jnp.int32, row.shape, 1)
    return jnp.sum(jnp.where(lane == index, row, 0.0), axis=1, keepdims=True)


def _prepare(slot, half, order_ref, offsets_ref, cols_ref, rows_ref, band_ref,
             lc_ref, ls_ref, pc_ref, ps_ref, mc_ref, ms_ref, combine_ref):
    cf_row = _offset_row(order_ref, offsets_ref, 0)
    own_cf = _pick(cf_row, slot).astype(jnp.int32)
    cf = _to_column(cf_row).astype(jnp.int32)
    sc = _to_column(cols_ref[...].astype(f32)).astype(jnp.int32)
    sr = _to_column(rows_ref[...].astype(f32)).astype(jnp.int32)
    lane = lax.broadcasted_iota(jnp.int32, (64, 128), 1)
    row = lax.bitwise_and(4 * half + 4 * lax.bitwise_and(lane // 8, 1) + lax.bitwise_and(lane, 3), 7)
    odd = 2 * row - 7
    factor = jnp.where(
        lane < COL_SC8, 2 * (own_cf + 1024 * lane),
        jnp.where(lane < COL_CF8, 256 * (lane - COL_SC8), jnp.where(lane < COL_ROW, 256 * (lane - COL_CF8), odd)),
    )
    other = jnp.where(lane < COL_CF8, sc, jnp.where(lane < COL_ROW, cf, sr + 512))
    angle = _angle(factor * other)
    mc, ms = jnp.cos(angle), jnp.sin(angle)
    mc_ref[...] = mc
    ms_ref[...] = ms
    angle = _angle(2 * lane * sc)
    low_c, low_s = jnp.cos(angle), jnp.sin(angle)
    for i in range(8):
        c, s = mc[:, COL_SC8 + i:COL_SC8 + i + 1], ms[:, COL_SC8 + i:COL_SC8 + i + 1]
        lc_ref[:, i * 128:(i + 1) * 128] = c * low_c - s * low_s
        ls_ref[:, i * 128:(i + 1) * 128] = s * low_c + c * low_s
    angle = _angle(2 * lane * cf)
    low_c, low_s = jnp.cos(angle), jnp.sin(angle)
    for i in range(8):
        c, s = mc[:, COL_CF8 + i:COL_CF8 + i + 1], ms[:, COL_CF8 + i:COL_CF8 + i + 1]
        band = band_ref[:, i * 128:(i + 1) * 128]
        pc_ref[:, i * 128:(i + 1) * 128] = (c * low_c - s * low_s) * band
        ps_ref[:, i * 128:(i + 1) * 128] = (s * low_c + c * low_s) * band
    rho = odd.astype(f32) * (0.5 / ROW_SCALE)
    power = jnp.ones((64, 128), f32)
    first = lax.bitwise_and(lane, 4) == 0
    to_re, to_im = jnp.where(first, mc, ms), jnp.where(first, -ms, mc)
    for n in range(ERANK):
        for part, value in ((0, to_re), (1, to_im)):
            base = part * 128 + n * 64
            combine_ref[base:base + 64, :] = (value * power)[:, COL_ROW:COL_ROW + 16].astype(bf16)
        power = power * rho


def _exact_kernel(order_hbm, offsets_hbm, cols_hbm, rows_hbm, band_hbm, data_hbm, window_hbm, sample_hbm,
                  lc_hbm, ls_hbm, pc_hbm, ps_hbm, mc_hbm, ms_hbm, combine_hbm, out_ref,
                  order_ref, offsets_ref, cols_ref, rows_ref, band_ref, data_ref, window_ref, sample_ref,
                  lc_ref, ls_ref, lc16_ref, ls16_ref, pc_ref, ps_ref, mc_ref, ms_ref, combine_ref,
                  even_ref, odd_ref, acc_ref, sems, out_sems):
    loads = [
        pltpu.make_async_copy(source, target, sems.at[i])
        for i, (source, target) in enumerate((
            (order_hbm, order_ref), (offsets_hbm, offsets_ref), (cols_hbm, cols_ref), (rows_hbm, rows_ref),
            (band_hbm, band_ref), (data_hbm, data_ref), (window_hbm, window_ref), (sample_hbm, sample_ref),
        ))
    ]
    for load in loads:
        load.start()
    for load in loads[:5]:
        load.wait()
    acc_ref[...] = jnp.zeros_like(acc_ref)
    _prepare(lax.axis_index("facet"), lax.axis_index("rows"), order_ref, offsets_ref, cols_ref, rows_ref, band_ref,
             lc_ref, ls_ref, pc_ref, ps_ref, mc_ref, ms_ref, combine_ref)
    lc16_ref[...] = lc_ref[...].astype(bf16)
    ls16_ref[...] = ls_ref[...].astype(bf16)
    stores = [
        pltpu.make_async_copy(source, target, out_sems.at[i])
        for i, (source, target) in enumerate((
            (lc16_ref, lc_hbm), (ls16_ref, ls_hbm), (pc_ref, pc_hbm), (ps_ref, ps_hbm), (mc_ref, mc_hbm), (ms_ref, ms_hbm),
            (combine_ref, combine_hbm),
        ))
    ]
    for store in stores:
        store.start()
    for load in loads[5:]:
        load.wait()

    def build(block, x_ref, bc, bs, i):
        cols = slice(i * 256, (i + 1) * 256)
        here = pl.ds(pl.multiple_of(block * BLOCK + i * 256, 256), 256)
        window = window_ref[:, here]
        re_rows = data_ref[0, 0, :, here] * window
        im_rows = data_ref[0, 1, :, here] * window
        for g in range(4):
            rows = slice(g * 16, (g + 1) * 16)
            lc, ls = lc_ref[rows, cols], ls_ref[rows, cols]
            c, s = bc[rows], bs[rows]
            ec = c * lc - s * ls
            es = s * lc + c * ls
            for r in range(4):
                dr, di = re_rows[r:r + 1], im_rows[r:r + 1]
                at = r * 64 + g * 16
                x_ref[at:at + 16, cols] = (dr * ec + di * es).astype(bf16)
                x_ref[256 + at:256 + at + 16, cols] = (di * ec - dr * es).astype(bf16)

    def turns(block):
        return _pick(mc_ref[...], block), _pick(ms_ref[...], block)

    def stage(block, x_ref, following, next_ref):
        bc, bs = turns(following)
        span = block // 4
        for i in range(4):
            rows = pl.ds(pl.multiple_of(lax.rem(block, 4) * BLOCK + i * 256, 256), 256)
            part = jnp.dot(x_ref[:, i * 256:(i + 1) * 256], sample_ref[rows, :], preferred_element_type=f32)
            build(following, next_ref, bc, bs, i)
            acc_ref[span] = acc_ref[span] + part

    bc, bs = turns(0)
    for i in range(4):
        build(0, even_ref, bc, bs, i)

    def body(pair, carry):
        stage(2 * pair, even_ref, 2 * pair + 1, odd_ref)
        stage(2 * pair + 1, odd_ref, lax.rem(2 * pair + 2, 16), even_ref)
        return carry

    lax.fori_loop(0, 8, body, 0)

    first = lax.broadcasted_iota(jnp.int32, (64, 128), 1) < 64
    lane = lax.broadcasted_iota(jnp.int32, (64, 128), 1)
    sign = jnp.where(lax.bitwise_and(lane, 32) == 0, -1.0, 1.0).astype(f32)
    places = [(r - 1.5) / ROW_SCALE for r in range(4)]
    spins = [
        [jnp.broadcast_to(ref[:, COL_ROW + r:COL_ROW + r + 1], (64, 128)) for ref in (mc_ref, ms_ref)] for r in range(4)
    ]
    for pair in range(2):
        sums = []
        for span in (2 * pair, 2 * pair + 1):
            direct, across = [None] * OWN_RANK, [None] * OWN_RANK
            for r in range(4):
                c, s = spins[r]
                re = acc_ref[span, r * 64:(r + 1) * 64]
                im = acc_ref[span, 256 + r * 64:256 + (r + 1) * 64]
                one, two = c * re + s * im, c * im - s * re
                for n in range(OWN_RANK):
                    direct[n] = one if r == 0 else direct[n] + one
                    across[n] = two if r == 0 else across[n] + two
                    one, two = one * places[r], two * places[r]
            sums.append((direct, across))
        for n in range(OWN_RANK):
            folded = []
            for which in range(2):
                a, b = sums[0][which][n], sums[1][which][n]
                folded.append(jnp.where(first, a, b) + pltpu.roll(jnp.where(first, b, a), 64, 1))
            at = n * 256 + pair * 128
            out_ref[:, at:at + 128] = folded[0] + jnp.where(
                sign < 0, -pltpu.roll(folded[1], 96, 1), pltpu.roll(folded[1], 32, 1))
    for store in stores:
        store.wait()


def _residual_kernel(own_hbm, peer_any, window_hbm, lc_hbm, ls_hbm, mc_hbm, ms_hbm, combine_hbm,
                     table_hbm, tc_hbm, ts_hbm, nodes_hbm, out_ref,
                     own_ref, peer_ref, window_ref, lc_ref, ls_ref, mc_ref, ms_ref, combine_ref,
                     table_ref, tc_ref, ts_ref, nodes_ref, even_ref, odd_ref, sum_ref, sems):
    loads = [
        pltpu.make_async_copy(source, target, sems.at[i])
        for i, (source, target) in enumerate((
            (own_hbm, own_ref), (peer_any, peer_ref), (window_hbm, window_ref), (lc_hbm, lc_ref), (ls_hbm, ls_ref),
            (mc_hbm, mc_ref), (ms_hbm, ms_ref), (combine_hbm, combine_ref),
            (table_hbm.at[lax.axis_index("rows")], table_ref), (tc_hbm, tc_ref), (ts_hbm, ts_ref),
            (nodes_hbm, nodes_ref),
        ))
    ]
    for load in loads:
        load.start()
    sum_ref[...] = jnp.zeros_like(sum_ref)
    for load in loads[:3]:
        load.wait()
    largest = jnp.zeros((4, 2048), f32)
    for i in range(8):
        here = slice(i * 2048, (i + 1) * 2048)
        window = window_ref[:, here]
        for ref in (own_ref, peer_ref):
            for part in range(2):
                largest = jnp.maximum(largest, jnp.abs(ref[0, part, :, here] * window))
    largest = jnp.maximum(jnp.max(jnp.max(largest, axis=1, keepdims=True), axis=0, keepdims=True), 1e-30)
    scale_in = DATA_SCALE / largest
    scale_out = largest * (1.0 / (DATA_SCALE * TABLE_SCALE))
    for load in loads[3:8]:
        load.wait()

    def mix(block, i):
        here = pl.ds(pl.multiple_of(block * BLOCK + i * 256, 256), 256)
        window = window_ref[:, here] * scale_in
        data = jnp.concatenate(
            [own_ref[0, 0, :, here], own_ref[0, 1, :, here], peer_ref[0, 0, :, here], peer_ref[0, 1, :, here]], 0
        )
        return jnp.dot(combine_ref[...], (data * window).astype(bf16), preferred_element_type=f32)

    def build(z_ref, j, i, rows, bc, bs):
        cols = slice(i * 256, (i + 1) * 256)
        lc, ls = lc_ref[:, cols], ls_ref[:, cols]
        ec = bc * lc - bs * ls
        es = bs * lc + bc * ls
        rows = rows.astype(bf16)
        for n in range(ERANK):
            gr, gi = rows[n * 64:(n + 1) * 64], rows[128 + n * 64:128 + (n + 1) * 64]
            at = j * 256 + n * 64
            z_ref[at:at + 64, cols] = (gr * ec + gi * es).astype(z_ref.dtype)
            z_ref[at + 128:at + 192, cols] = (gi * ec - gr * es).astype(z_ref.dtype)

    def turns(block):
        return tuple(
            jnp.broadcast_to(_pick(ref[...], block), (64, 256)).astype(bf16) for ref in (mc_ref, ms_ref)
        )

    def stage(group, z_ref, following, next_ref):
        tasks = [(j, i) for j in range(2) for i in range(4)]
        building = following is not None
        if building:
            spins = [turns(following * 2 + j) for j in range(2)]
            ready = mix(following * 2, 0)
        at = 0
        for j in range(2):
            for kc in range(2):
                cols = slice(kc * 256, (kc + 1) * 256)
                z = z_ref[j * 256:(j + 1) * 256, :]
                by_c = jnp.dot(z, table_ref[:, cols], preferred_element_type=f32)
                by_s = jnp.dot(z, table_ref[:, 512 + kc * 256:768 + kc * 256], preferred_element_type=f32)
                for _ in range(2 if building else 0):
                    bj, bi = tasks[at]
                    at += 1
                    coming = mix(following * 2 + tasks[at][0], tasks[at][1]) if at < 8 else None
                    build(next_ref, bj, bi, ready, *spins[bj])
                    ready = coming
                re = by_c[0:128] + by_s[128:256]
                im = by_c[128:256] - by_s[0:128]
                tc = tc_ref[pl.ds(group * 2 + j, 1), cols]
                ts = ts_ref[pl.ds(group * 2 + j, 1), cols]
                sum_ref[0, :, cols] = sum_ref[0, :, cols] + (re * tc + im * ts)
                sum_ref[1, :, cols] = sum_ref[1, :, cols] + (im * tc - re * ts)

    for j in range(2):
        spin = turns(j)
        for i in range(4):
            build(even_ref, j, i, mix(j, i), *spin)
    for load in loads[8:]:
        load.wait()

    def body(pair, carry):
        stage(2 * pair, even_ref, 2 * pair + 1, odd_ref)
        stage(2 * pair + 1, odd_ref, 2 * pair + 2, even_ref)
        return carry

    lax.fori_loop(0, 3, body, 0)
    stage(6, even_ref, 7, odd_ref)
    stage(7, odd_ref, None, None)

    for copy in range(2):
        for i in range(CHUNKS - 16):
            out_ref[pl.ds(copy * CHUNKS + 16 + i, 64, stride=2 * CHUNKS), :] = nodes_ref[:, i * 128:(i + 1) * 128]
        for n in range(ERANK):
            for part in range(2):
                for kc in range(4):
                    at = copy * CHUNKS + n * 8 + part * 4 + kc
                    out_ref[pl.ds(at, 64, stride=2 * CHUNKS), :] = (
                        sum_ref[part, n * 64:(n + 1) * 64, kc * 128:(kc + 1) * 128] * scale_out
                    )


def _halves(value):
    high = value.astype(bf16)
    return high, (value - high.astype(f32)).astype(bf16)


def _phase_kernel(order_ref, offsets_ref, rows_ref, out_ref, all_ref, turned_ref):
    left_ref, gram_ref = out_ref.at[0:512], out_ref.at[512:1024]
    slot, half = lax.axis_index("facet"), lax.axis_index("rows")
    rf = _offset_row(order_ref, offsets_ref, 1).astype(jnp.int32)
    own_sr = _pick(rows_ref[...].astype(f32), slot).astype(jnp.int32)
    odd = jnp.concatenate([2 * rf + 7, 2 * rf + 7], 1)
    lane = lax.broadcasted_iota(jnp.int32, (128, 128), 1)
    quarter = jnp.where(lane < 64, 0, -(NIMG // 2))
    sign = jnp.where(lane < 64, -1.0, 1.0).astype(f32)
    for i in range(8):
        here = slice(i * 128, (i + 1) * 128)
        q = lax.broadcasted_iota(jnp.int32, (128, 128), 0) + i * 128 + half * 512
        q = lax.bitwise_and(q, 1023)
        turn = jnp.cos(_angle(odd * (own_sr + q) + quarter))
        other = sign * pltpu.roll(turn, 64, 1)
        g = (q - 512).astype(f32) * (TWO_PI / NIMG * ROW_SCALE)
        g2, g3 = g * g * 0.5, g * g * g * (1.0 / 6.0)
        for n, value in enumerate((turn, g * other, -g2 * turn, -g3 * other)):
            high, low = _halves(value)
            cols = slice(n * 128, (n + 1) * 128)
            all_ref[0, here, cols] = high
            all_ref[1, here, cols] = low
            high_t, low_t = _halves(sign * pltpu.roll(value, 64, 1))
            turned_ref[0, here, cols] = high_t
            turned_ref[1, here, cols] = low_t
            if i < 4 and n < 2:
                left_ref[here, n * 128:(n + 1) * 128] = high
                left_ref[here, 256 + n * 128:256 + (n + 1) * 128] = high
                left_ref[here, 512 + n * 128:512 + (n + 1) * 128] = low
            elif i < 4:
                left_ref[here, 512 + n * 128:512 + (n + 1) * 128] = high
    over_rows = (((0,), (0,)), ((), ()))
    gram = None
    for ref in (all_ref, turned_ref):
        for a, b in ((0, 0), (0, 1), (1, 0)):
            part = lax.dot_general(ref[a], ref[b], over_rows, preferred_element_type=f32)
            gram = part if gram is None else gram + part
    high, low = _halves(gram)
    gram_ref[:, 0:256] = high[:, 0:256]
    gram_ref[:, 256:512] = high[:, 0:256]
    gram_ref[:, 512:768] = low[:, 0:256]
    gram_ref[:, 768:1024] = high[:, 256:512]


def _rows_kernel(got_any, wh_hbm, wl_hbm, pc_hbm, ps_hbm, phases_any, out_hbm,
                 got_ref, wh_ref, wl_ref, pc_ref, ps_ref, gram_ref, left_ref, right_ref, value_ref, high_ref, low_ref,
                 out_ref, sems, out_sems):
    loads = [
        pltpu.make_async_copy(source, target, sems.at[i])
        for i, (source, target) in enumerate((
            (got_any, got_ref), (wh_hbm, wh_ref), (wl_hbm, wl_ref), (pc_hbm, pc_ref), (ps_hbm, ps_ref),
            (phases_any.at[512:1024], gram_ref), (phases_any.at[0:512], left_ref),
        ))
    ]
    for load in loads:
        load.start()
    loads[0].wait()
    second = lax.bitwise_and(lax.broadcasted_iota(jnp.int32, (64, 128), 1), 32) != 0
    for i in range(2):
        sums, diffs = [], []
        for n in range(OWN_RANK):
            parts = [got_ref[pl.ds(h * CHUNKS + 16 + n * 2 + i, 64, stride=2 * CHUNKS), :] for h in range(2)]
            sums.append(parts[0] + parts[1])
            diffs.append(parts[1] - parts[0])
        d = 2.0 / ROW_SCALE
        cube = 2.05 / (ROW_SCALE * ROW_SCALE)
        terms = (
            sums[0],
            sums[1] + d * diffs[0],
            sums[2] + (2 * d) * diffs[1] + (d * d) * sums[0],
            (cube + 3 * d * d) * sums[1] + (3 * d) * diffs[2] + (d * d * d) * diffs[0],
        )
        cols = slice(i * 128, (i + 1) * 128)
        for n, value in enumerate(terms):
            for part in range(2):
                rows = slice(n * 64, (n + 1) * 64)
                high, low = _halves(value)
                high_ref[part, rows, cols] = high
                if n < 2:
                    low_ref[part, rows, cols] = low
                value = jnp.where(second, -pltpu.roll(value, 32, 1), pltpu.roll(value, 96, 1))
    for load in loads[1:5]:
        load.wait()
    for i in range(4):
        cols = slice(i * 256, (i + 1) * 256)
        vals = []
        for part in range(2):
            wh, wl = wh_ref[:, cols], wl_ref[:, cols]
            main = jnp.dot(high_ref[part], wh, preferred_element_type=f32)
            rest = (
                jnp.dot(high_ref[part, 0:128], wl, preferred_element_type=f32)
                + jnp.dot(low_ref[part], wh, preferred_element_type=f32)
            )
            vals.append((main, rest))
        pc, ps = pc_ref[:, cols], ps_ref[:, cols]
        for n in range(RANK):
            rows = slice(n * 64, (n + 1) * 64)
            vr, vi = vals[0][0][rows], vals[1][0][rows]
            if n < ERANK:
                parts = []
                for part in range(2):
                    at = (i // 2) * CHUNKS + n * 8 + part * 4 + 2 * (i % 2)
                    parts.append(jnp.concatenate(
                        [got_ref[pl.ds(at + m, 64, stride=2 * CHUNKS), :] for m in range(2)], 1))
                vr = vr + vals[0][1][rows] + parts[0]
                vi = vi + vals[1][1][rows] + parts[1]
            cr = vr * pc + vi * ps
            ci = vi * pc - vr * ps
            at = n * 128
            value_ref[at:at + 64, cols] = cr
            value_ref[at + 64:at + 128, cols] = ci
            turned = slice(1024 + i * 256, 1024 + (i + 1) * 256)
            cr_high, ci_high = cr.astype(bf16), ci.astype(bf16)
            bases = (0, 512) if n < 2 else (512,)
            for base in bases:
                right_ref[base + at:base + at + 64, cols] = cr_high
                right_ref[base + at + 64:base + at + 128, cols] = ci_high
                right_ref[base + at:base + at + 64, turned] = ci_high
                right_ref[base + at + 64:base + at + 128, turned] = -cr_high
            if n < 2:
                cr_low = (cr - cr_high.astype(f32)).astype(bf16)
                ci_low = (ci - ci_high.astype(f32)).astype(bf16)
                right_ref[256 + at:256 + at + 64, cols] = cr_low
                right_ref[256 + at + 64:256 + at + 128, cols] = ci_low
                right_ref[256 + at:256 + at + 64, turned] = ci_low
                right_ref[256 + at + 64:256 + at + 128, turned] = -cr_low

    loads[5].wait()
    total = jnp.zeros((8, 256), f32)
    for i in range(4):
        cols = slice(i * 256, (i + 1) * 256)
        product = jnp.dot(gram_ref[...], right_ref[:, cols], preferred_element_type=f32) * value_ref[:, cols]
        total = total + jnp.sum(product.reshape(64, 8, 256), 0)
    mean = jnp.maximum(jnp.sum(total), 0.0) / (2.0 * SUBROWS * M)
    factor = lax.rsqrt(jnp.full((8, 128), mean, f32) + 1e-06)[0:1, 0:1]

    loads[6].wait()
    stores = []
    for part in range(2):
        for i in range(4):
            cols = slice(i * 256, (i + 1) * 256)
            right = right_ref[:, part * 1024 + i * 256:part * 1024 + (i + 1) * 256]
            out_ref[part, :, cols] = jnp.dot(left_ref[...], right, preferred_element_type=f32) * factor
            store = pltpu.make_async_copy(
                out_ref.at[part, :, cols], out_hbm.at[0, part, :, cols], out_sems.at[part * 4 + i])
            store.start()
            stores.append(store)
    for store in stores:
        store.wait()


def per_device(facets, facet_window, band_window, facet_order, facet_offsets, sub_cols, sub_rows):
    tables = _tables()
    peer = lax.ppermute(facets, "rows", [(0, 1), (1, 0)])
    order, cols, rows = (v.reshape(1, 64) for v in (facet_order, sub_cols, sub_rows))
    offsets = facet_offsets.T
    window = facet_window.reshape(1, 16384)
    hbm = pl.BlockSpec(memory_space=pltpu.HBM)
    anywhere = pl.BlockSpec(memory_space=pl.ANY)
    vmem = pl.BlockSpec(memory_space=pltpu.VMEM)
    shape = jax.ShapeDtypeStruct

    def params(mib):
        return pltpu.CompilerParams(vmem_limit_bytes=mib * 1024 * 1024)

    wide, wide16, narrow = shape((64, 1024), f32), shape((64, 1024), bf16), shape((64, 128), f32)
    lc, ls, pc, ps, mc, ms, combine, nodes = pl.pallas_call(
        _exact_kernel,
        in_specs=[hbm] * 8,
        out_specs=[hbm] * 7 + [vmem],
        out_shape=[wide16, wide16, wide, wide, narrow, narrow, shape((256, 16), bf16),
                   shape((64, 128 * (CHUNKS - 16)), f32)],
        scratch_shapes=[
            pltpu.VMEM((1, 64), jnp.int32), pltpu.VMEM((2, 64), jnp.int32), pltpu.VMEM((1, 64), jnp.int32),
            pltpu.VMEM((1, 64), jnp.int32), pltpu.VMEM((1, M), f32), pltpu.VMEM((1, 2, 4, 16384), f32),
            pltpu.VMEM((1, 16384), f32), pltpu.VMEM((SPAN, 128), bf16),
            pltpu.VMEM((64, 1024), f32), pltpu.VMEM((64, 1024), f32), pltpu.VMEM((64, 1024), bf16),
            pltpu.VMEM((64, 1024), bf16), pltpu.VMEM((64, 1024), f32), pltpu.VMEM((64, 1024), f32),
            pltpu.VMEM((64, 128), f32), pltpu.VMEM((64, 128), f32), pltpu.VMEM((256, 16), bf16),
            pltpu.VMEM((512, BLOCK), bf16), pltpu.VMEM((512, BLOCK), bf16), pltpu.VMEM((4, 512, 128), f32),
            pltpu.SemaphoreType.DMA((8,)), pltpu.SemaphoreType.DMA((7,)),
        ],
        compiler_params=params(60),
        cost_estimate=pl.CostEstimate(flops=8 * 10**9, bytes_accessed=2 * 10**6, transcendentals=0),
        name="exact_part",
    )(order, offsets, cols, rows, band_window.reshape(1, M), facets, window, jnp.asarray(tables["sample"]))

    send = pl.pallas_call(
        _residual_kernel,
        in_specs=[hbm, anywhere] + [hbm] * 10,
        out_shape=shape((128 * CHUNKS, 128), f32),
        scratch_shapes=[
            pltpu.VMEM((1, 2, 4, 16384), f32), pltpu.VMEM((1, 2, 4, 16384), f32), pltpu.VMEM((1, 16384), f32),
            pltpu.VMEM((64, 1024), bf16), pltpu.VMEM((64, 1024), bf16), pltpu.VMEM((64, 128), f32),
            pltpu.VMEM((64, 128), f32), pltpu.VMEM((256, 16), bf16),
            pltpu.VMEM((1024, 1024), f8), pltpu.VMEM((16, 512), f32), pltpu.VMEM((16, 512), f32),
            pltpu.VMEM((64, 128 * (CHUNKS - 16)), f32),
            pltpu.VMEM((512, 1024), f8), pltpu.VMEM((512, 1024), f8), pltpu.VMEM((2, 128, 512), f32),
            pltpu.SemaphoreType.DMA((12,)),
        ],
        compiler_params=params(60),
        cost_estimate=pl.CostEstimate(flops=9 * 10**9, bytes_accessed=4 * 10**6, transcendentals=0),
        name="residual_part",
    )(
        facets, peer, window, lc, ls, mc, ms, combine, jnp.asarray(tables["resid"]), jnp.asarray(tables["turn_c"]),
        jnp.asarray(tables["turn_s"]), nodes,
    )

    got = lax.all_to_all(send.reshape(128, CHUNKS // 2, 2, 128), ("facet", "rows"), split_axis=0, concat_axis=0, tiled=True)
    phases = pl.pallas_call(
        _phase_kernel,
        in_specs=[vmem] * 3,
        out_shape=shape((1024, 1024), bf16),
        scratch_shapes=[pltpu.VMEM((2, 1024, 512), bf16), pltpu.VMEM((2, 1024, 512), bf16)],
        compiler_params=params(60),
        cost_estimate=pl.CostEstimate(flops=3 * 10**9, bytes_accessed=2 * 10**6, transcendentals=2 * 10**5),
        name="row_phases",
    )(order, offsets, rows)

    return pl.pallas_call(
        _rows_kernel,
        in_specs=[anywhere] + [hbm] * 4 + [anywhere],
        out_specs=hbm,
        out_shape=shape((1, 2, 512, 1024), f32),
        scratch_shapes=[
            pltpu.VMEM((128 * CHUNKS, 128), f32), pltpu.VMEM((256, 1024), bf16), pltpu.VMEM((256, 1024), bf16),
            pltpu.VMEM((64, 1024), f32), pltpu.VMEM((64, 1024), f32), pltpu.VMEM((512, 1024), bf16),
            pltpu.VMEM((512, 1024), bf16), pltpu.VMEM((1024, 2048), bf16), pltpu.VMEM((512, 1024), f32),
            pltpu.VMEM((2, 256, 256), bf16), pltpu.VMEM((2, 128, 256), bf16), pltpu.VMEM((2, 512, 1024), f32),
            pltpu.SemaphoreType.DMA((7,)), pltpu.SemaphoreType.DMA((8,)),
        ],
        compiler_params=params(60),
        cost_estimate=pl.CostEstimate(flops=5 * 10**9, bytes_accessed=12 * 10**6, transcendentals=0),
        name="row_transform",
    )(got.reshape(128 * CHUNKS, 128), jnp.asarray(tables["weave_hi"]), jnp.asarray(tables["weave_lo"]), pc, ps, phases)


def solution(mesh):
    return jax.shard_map(
        per_device,
        mesh=mesh,
        in_specs=(P("facet", None, "rows", None), P(), P(), P(), P(), P(), P()),
        out_specs=P("facet", None, "rows", None),
        check_vma=False,
    )
```

```python
import functools
import math

import jax
import jax.numpy as jnp
import ml_dtypes
import numpy as np
from jax import lax
from jax.experimental import pallas as pl
from jax.experimental.pallas import tpu as pltpu
from jax.sharding import PartitionSpec as P

NIMG = 262144
M = 1024
SUBROWS = 1024
TWO_PI = 2.0 * math.pi

BLOCK = 1024
SPAN = 4096
NODES = 32
WIDTH = 16384
ALL_NODES = 85
RANK = 4
OWN_RANK = 3
ERANK = 2
ROW_SCALE = 4.0
TABLE_SCALE = 32768.0
DATA_SCALE = 16.0

f32 = jnp.float32
bf16 = jnp.bfloat16
f8 = jnp.float8_e4m3fn


def _split(values):
    high = values.astype(np.float32).astype(ml_dtypes.bfloat16)
    low = (values - high.astype(np.float64)).astype(np.float32).astype(ml_dtypes.bfloat16)
    return high, low


def _kernel_sum(x, count):
    den = np.sin(np.pi * x / NIMG)
    zero = np.abs(den) < 1e-14
    return np.where(zero, float(count), np.sin(np.pi * x * count / NIMG) / np.where(zero, 1.0, den))


def _solve(gram, right):
    gram, right = gram.copy(), right.copy()
    n = len(gram)
    for i in range(n):
        for j in range(i + 1, n):
            factor = gram[j, i] / gram[i, i]
            gram[j] = gram[j] - factor * gram[i]
            right[j] = right[j] - factor * right[i]
    out = np.zeros_like(right)
    for i in range(n - 1, -1, -1):
        total = right[i].copy()
        for j in range(i + 1, n):
            total = total - gram[i, j] * out[j]
        out[i] = total / gram[i, i]
    return out


@functools.lru_cache(maxsize=None)
def _tables():
    scale = TWO_PI / NIMG
    bands = np.arange(M)
    product = (np.arange(BLOCK)[:, None] * bands[None, :]) % NIMG
    angle = (np.float32(scale) * product.astype(np.float32)).astype(np.float64)
    exact = scale * product
    resid_c = np.cos(angle).astype(np.float32).astype(ml_dtypes.bfloat16).astype(np.float64) - np.cos(exact)
    resid_s = np.sin(angle).astype(np.float32).astype(ml_dtypes.bfloat16).astype(np.float64) - np.sin(exact)
    half = M // 2
    resid = np.stack(
        [np.concatenate([resid_c[:, h * half:(h + 1) * half], resid_s[:, h * half:(h + 1) * half]], 1) for h in range(2)]
    )
    resid = (resid * TABLE_SCALE).astype(np.float32).astype(ml_dtypes.float8_e4m3fn)
    def spread(count, width, even):
        i = np.arange(count)
        return 511.5 + 512 * width * (even * ((2 * i + 1) / count - 1) - (1 - even) * np.cos(np.pi * (i + 0.5) / count))

    def interpolate(nodes, targets, columns):
        gram = _kernel_sum(nodes[:, None] - nodes[None, :], columns) + 1e-13 * columns * np.eye(len(nodes))
        return _solve(gram, _kernel_sum(nodes[:, None] - targets[None, :], columns))

    nodes, all_nodes = spread(NODES, 1.05, 0.25), spread(ALL_NODES, 1.04, 0.6)
    centre = (SPAN - 1) / 2
    at = scale * (np.arange(SPAN) - centre)[:, None] * nodes[None, :]
    sample = np.concatenate([np.cos(at), -np.sin(at)], 1)
    sample = np.concatenate(_split(sample), 1)
    middle = (WIDTH - 1) / 2
    interp = interpolate(nodes, all_nodes, SPAN)
    rows = []
    for span in range(WIDTH // SPAN):
        turn = scale * (span * SPAN + centre - middle) * all_nodes
        re, im = interp * np.cos(turn), -interp * np.sin(turn)
        rows += [np.concatenate([re, im], 1), np.concatenate([-im, re], 1)]
    joined = np.concatenate(rows, 0)
    join = np.zeros((OWN_RANK * 256, 512))
    for n in range(OWN_RANK):
        join[n * 256:(n + 1) * 256, n * 2 * ALL_NODES:(n + 1) * 2 * ALL_NODES] = joined
    join_hi, join_lo = _split(join)
    interp = interpolate(all_nodes, bands.astype(np.float64), WIDTH)
    turn = scale * middle * bands
    weave = np.zeros((256, M))
    weave[:2 * ALL_NODES] = np.concatenate([interp * np.cos(turn), interp * np.sin(turn)], 0)
    weave_hi, weave_lo = _split(weave)
    turn = TWO_PI * ((np.arange(16)[:, None] * (bands[None, :half] % 256)) % 256) / 256
    return dict(
        resid=resid, sample=sample, join_hi=join_hi, join_lo=join_lo, weave_hi=weave_hi, weave_lo=weave_lo,
        turn_c=np.cos(turn).astype(np.float32), turn_s=np.sin(turn).astype(np.float32),
    )


COL_A, COL_SC8, COL_CF8, COL_ROW = 0, 16, 24, 32
CHUNKS = 20


def _angle(product):
    turns = lax.bitwise_and(product + NIMG, 2 * NIMG - 1) - NIMG
    return turns.astype(f32) * (math.pi / NIMG)


def _offset_row(order_ref, offsets_ref, which):
    slots = lax.broadcasted_iota(jnp.int32, (64, 64), 0)
    offsets = _to_column(offsets_ref[which:which + 1, :].astype(f32))
    return jnp.sum(jnp.where(slots == order_ref[...], offsets, 0.0), axis=0, keepdims=True)


def _to_column(row):
    at = lax.broadcasted_iota(jnp.int32, (64, 64), 0) == lax.broadcasted_iota(jnp.int32, (64, 64), 1)
    return jnp.sum(jnp.where(at, row, 0.0), axis=1, keepdims=True)


def _pick(row, index):
    lane = lax.broadcasted_iota(jnp.int32, row.shape, 1)
    return jnp.sum(jnp.where(lane == index, row, 0.0), axis=1, keepdims=True)


def _prepare(slot, half, order_ref, offsets_ref, cols_ref, rows_ref, band_ref,
             lc_ref, ls_ref, pc_ref, ps_ref, mc_ref, ms_ref, combine_ref):
    cf_row = _offset_row(order_ref, offsets_ref, 0)
    own_cf = _pick(cf_row, slot).astype(jnp.int32)
    cf = _to_column(cf_row).astype(jnp.int32)
    sc = _to_column(cols_ref[...].astype(f32)).astype(jnp.int32)
    sr = _to_column(rows_ref[...].astype(f32)).astype(jnp.int32)
    lane = lax.broadcasted_iota(jnp.int32, (64, 128), 1)
    row = lax.bitwise_and(4 * half + 4 * lax.bitwise_and(lane // 8, 1) + lax.bitwise_and(lane, 3), 7)
    odd = 2 * row - 7
    factor = jnp.where(
        lane < COL_SC8, 2 * (own_cf + 1024 * lane),
        jnp.where(lane < COL_CF8, 256 * (lane - COL_SC8), jnp.where(lane < COL_ROW, 256 * (lane - COL_CF8), odd)),
    )
    other = jnp.where(lane < COL_CF8, sc, jnp.where(lane < COL_ROW, cf, sr + 512))
    angle = _angle(factor * other)
    mc, ms = jnp.cos(angle), jnp.sin(angle)
    mc_ref[...] = mc
    ms_ref[...] = ms
    angle = _angle(2 * lane * sc)
    low_c, low_s = jnp.cos(angle), jnp.sin(angle)
    for i in range(8):
        c, s = mc[:, COL_SC8 + i:COL_SC8 + i + 1], ms[:, COL_SC8 + i:COL_SC8 + i + 1]
        lc_ref[:, i * 128:(i + 1) * 128] = c * low_c - s * low_s
        ls_ref[:, i * 128:(i + 1) * 128] = s * low_c + c * low_s
    angle = _angle(2 * lane * cf)
    low_c, low_s = jnp.cos(angle), jnp.sin(angle)
    for i in range(8):
        c, s = mc[:, COL_CF8 + i:COL_CF8 + i + 1], ms[:, COL_CF8 + i:COL_CF8 + i + 1]
        band = band_ref[:, i * 128:(i + 1) * 128]
        pc_ref[:, i * 128:(i + 1) * 128] = (c * low_c - s * low_s) * band
        ps_ref[:, i * 128:(i + 1) * 128] = (s * low_c + c * low_s) * band
    rho = odd.astype(f32) * (0.5 / ROW_SCALE)
    power = jnp.ones((64, 128), f32)
    first = lax.bitwise_and(lane, 4) == 0
    to_re, to_im = jnp.where(first, mc, ms), jnp.where(first, -ms, mc)
    for n in range(ERANK):
        for part, value in ((0, to_re), (1, to_im)):
            base = part * 128 + n * 64
            combine_ref[base:base + 64, :] = (value * power)[:, COL_ROW:COL_ROW + 16].astype(bf16)
        power = power * rho


def _exact_kernel(order_hbm, offsets_hbm, cols_hbm, rows_hbm, band_hbm, data_hbm, window_hbm, sample_hbm, jh_hbm, jl_hbm,
                  lc_hbm, ls_hbm, pc_hbm, ps_hbm, mc_hbm, ms_hbm, combine_hbm, out_ref,
                  order_ref, offsets_ref, cols_ref, rows_ref, band_ref, data_ref, window_ref, sample_ref, jh_ref, jl_ref,
                  lc_ref, ls_ref, lc16_ref, ls16_ref, pc_ref, ps_ref, mc_ref, ms_ref, combine_ref,
                  even_ref, odd_ref, acc_ref, terms_ref, sems, out_sems):
    loads = [
        pltpu.make_async_copy(source, target, sems.at[i])
        for i, (source, target) in enumerate((
            (order_hbm, order_ref), (offsets_hbm, offsets_ref), (cols_hbm, cols_ref), (rows_hbm, rows_ref),
            (band_hbm, band_ref), (data_hbm, data_ref), (window_hbm, window_ref), (sample_hbm, sample_ref),
            (jh_hbm, jh_ref), (jl_hbm, jl_ref),
        ))
    ]
    for load in loads:
        load.start()
    for load in loads[:5]:
        load.wait()
    acc_ref[...] = jnp.zeros_like(acc_ref)
    _prepare(lax.axis_index("facet"), lax.axis_index("rows"), order_ref, offsets_ref, cols_ref, rows_ref, band_ref,
             lc_ref, ls_ref, pc_ref, ps_ref, mc_ref, ms_ref, combine_ref)
    lc16_ref[...] = lc_ref[...].astype(bf16)
    ls16_ref[...] = ls_ref[...].astype(bf16)
    stores = [
        pltpu.make_async_copy(source, target, out_sems.at[i])
        for i, (source, target) in enumerate((
            (lc16_ref, lc_hbm), (ls16_ref, ls_hbm), (pc_ref, pc_hbm), (ps_ref, ps_hbm), (mc_ref, mc_hbm), (ms_ref, ms_hbm),
            (combine_ref, combine_hbm),
        ))
    ]
    for store in stores:
        store.start()
    for load in loads[5:8]:
        load.wait()

    def build(block, x_ref, bc, bs, i):
        cols = slice(i * 256, (i + 1) * 256)
        here = pl.ds(pl.multiple_of(block * BLOCK + i * 256, 256), 256)
        window = window_ref[:, here]
        re_rows = data_ref[0, 0, :, here] * window
        im_rows = data_ref[0, 1, :, here] * window
        for g in range(4):
            rows = slice(g * 16, (g + 1) * 16)
            lc, ls = lc_ref[rows, cols], ls_ref[rows, cols]
            c, s = bc[rows], bs[rows]
            ec = c * lc - s * ls
            es = s * lc + c * ls
            for r in range(4):
                dr, di = re_rows[r:r + 1], im_rows[r:r + 1]
                at = r * 64 + g * 16
                x_ref[at:at + 16, cols] = (dr * ec + di * es).astype(bf16)
                x_ref[256 + at:256 + at + 16, cols] = (di * ec - dr * es).astype(bf16)

    def turns(block):
        return _pick(mc_ref[...], block), _pick(ms_ref[...], block)

    def stage(block, x_ref, following, next_ref):
        bc, bs = turns(following)
        span = block // 4
        for i in range(4):
            rows = pl.ds(pl.multiple_of(lax.rem(block, 4) * BLOCK + i * 256, 256), 256)
            part = jnp.dot(x_ref[:, i * 256:(i + 1) * 256], sample_ref[rows, :], preferred_element_type=f32)
            build(following, next_ref, bc, bs, i)
            acc_ref[span] = acc_ref[span] + part

    bc, bs = turns(0)
    for i in range(4):
        build(0, even_ref, bc, bs, i)

    def body(pair, carry):
        stage(2 * pair, even_ref, 2 * pair + 1, odd_ref)
        stage(2 * pair + 1, odd_ref, lax.rem(2 * pair + 2, 16), even_ref)
        return carry

    lax.fori_loop(0, 8, body, 0)

    first = lax.broadcasted_iota(jnp.int32, (64, 128), 1) < 64
    lane = lax.broadcasted_iota(jnp.int32, (64, 128), 1)
    sign = jnp.where(lax.bitwise_and(lane, 32) == 0, -1.0, 1.0).astype(f32)
    places = [(r - 1.5) / ROW_SCALE for r in range(4)]
    spins = [
        [jnp.broadcast_to(ref[:, COL_ROW + r:COL_ROW + r + 1], (64, 128)) for ref in (mc_ref, ms_ref)] for r in range(4)
    ]
    for pair in range(2):
        sums = []
        for span in (2 * pair, 2 * pair + 1):
            direct, across = [None] * OWN_RANK, [None] * OWN_RANK
            for r in range(4):
                c, s = spins[r]
                re = acc_ref[span, r * 64:(r + 1) * 64]
                im = acc_ref[span, 256 + r * 64:256 + (r + 1) * 64]
                one, two = c * re + s * im, c * im - s * re
                for n in range(OWN_RANK):
                    direct[n] = one if r == 0 else direct[n] + one
                    across[n] = two if r == 0 else across[n] + two
                    one, two = one * places[r], two * places[r]
            sums.append((direct, across))
        for n in range(OWN_RANK):
            folded = []
            for which in range(2):
                a, b = sums[0][which][n], sums[1][which][n]
                folded.append(jnp.where(first, a, b) + pltpu.roll(jnp.where(first, b, a), 64, 1))
            at = n * 256 + pair * 128
            terms_ref[:, at:at + 128] = folded[0] + jnp.where(
                sign < 0, -pltpu.roll(folded[1], 96, 1), pltpu.roll(folded[1], 32, 1))
    for load in loads[8:]:
        load.wait()
    high, low = _halves(terms_ref[...])
    out_ref[...] = (
        jnp.dot(high, jh_ref[...], preferred_element_type=f32)
        + (jnp.dot(high, jl_ref[...], preferred_element_type=f32) + jnp.dot(low, jh_ref[...], preferred_element_type=f32))
    )
    for store in stores:
        store.wait()


def _residual_kernel(own_hbm, peer_any, window_hbm, lc_hbm, ls_hbm, mc_hbm, ms_hbm, combine_hbm,
                     table_hbm, tc_hbm, ts_hbm, nodes_hbm, out_ref,
                     own_ref, peer_ref, window_ref, lc_ref, ls_ref, mc_ref, ms_ref, combine_ref,
                     table_ref, tc_ref, ts_ref, nodes_ref, even_ref, odd_ref, sum_ref, sems):
    loads = [
        pltpu.make_async_copy(source, target, sems.at[i])
        for i, (source, target) in enumerate((
            (own_hbm, own_ref), (peer_any, peer_ref), (window_hbm, window_ref), (lc_hbm, lc_ref), (ls_hbm, ls_ref),
            (mc_hbm, mc_ref), (ms_hbm, ms_ref), (combine_hbm, combine_ref),
            (table_hbm.at[lax.axis_index("rows")], table_ref), (tc_hbm, tc_ref), (ts_hbm, ts_ref),
            (nodes_hbm, nodes_ref),
        ))
    ]
    for load in loads:
        load.start()
    sum_ref[...] = jnp.zeros_like(sum_ref)
    for load in loads[:3]:
        load.wait()
    largest = jnp.zeros((4, 2048), f32)
    for i in range(8):
        here = slice(i * 2048, (i + 1) * 2048)
        window = window_ref[:, here]
        for ref in (own_ref, peer_ref):
            for part in range(2):
                largest = jnp.maximum(largest, jnp.abs(ref[0, part, :, here] * window))
    largest = jnp.maximum(jnp.max(jnp.max(largest, axis=1, keepdims=True), axis=0, keepdims=True), 1e-30)
    scale_in = DATA_SCALE / largest
    scale_out = largest * (1.0 / (DATA_SCALE * TABLE_SCALE))
    for load in loads[3:8]:
        load.wait()

    def mix(block, i):
        here = pl.ds(pl.multiple_of(block * BLOCK + i * 256, 256), 256)
        window = window_ref[:, here] * scale_in
        data = jnp.concatenate(
            [own_ref[0, 0, :, here], own_ref[0, 1, :, here], peer_ref[0, 0, :, here], peer_ref[0, 1, :, here]], 0
        )
        return jnp.dot(combine_ref[...], (data * window).astype(bf16), preferred_element_type=f32)

    def build(z_ref, j, i, rows, bc, bs):
        cols = slice(i * 256, (i + 1) * 256)
        lc, ls = lc_ref[:, cols], ls_ref[:, cols]
        ec = bc * lc - bs * ls
        es = bs * lc + bc * ls
        rows = rows.astype(bf16)
        for n in range(ERANK):
            gr, gi = rows[n * 64:(n + 1) * 64], rows[128 + n * 64:128 + (n + 1) * 64]
            at = j * 256 + n * 64
            z_ref[at:at + 64, cols] = (gr * ec + gi * es).astype(z_ref.dtype)
            z_ref[at + 128:at + 192, cols] = (gi * ec - gr * es).astype(z_ref.dtype)

    def turns(block):
        return tuple(
            jnp.broadcast_to(_pick(ref[...], block), (64, 256)).astype(bf16) for ref in (mc_ref, ms_ref)
        )

    def stage(group, z_ref, following, next_ref):
        tasks = [(j, i) for j in range(2) for i in range(4)]
        building = following is not None
        if building:
            spins = [turns(following * 2 + j) for j in range(2)]
            ready = mix(following * 2, 0)
        at = 0
        for j in range(2):
            for kc in range(2):
                cols = slice(kc * 256, (kc + 1) * 256)
                z = z_ref[j * 256:(j + 1) * 256, :]
                by_c = jnp.dot(z, table_ref[:, cols], preferred_element_type=f32)
                by_s = jnp.dot(z, table_ref[:, 512 + kc * 256:768 + kc * 256], preferred_element_type=f32)
                for _ in range(2 if building else 0):
                    bj, bi = tasks[at]
                    at += 1
                    coming = mix(following * 2 + tasks[at][0], tasks[at][1]) if at < 8 else None
                    build(next_ref, bj, bi, ready, *spins[bj])
                    ready = coming
                re = by_c[0:128] + by_s[128:256]
                im = by_c[128:256] - by_s[0:128]
                tc = tc_ref[pl.ds(group * 2 + j, 1), cols]
                ts = ts_ref[pl.ds(group * 2 + j, 1), cols]
                sum_ref[0, :, cols] = sum_ref[0, :, cols] + (re * tc + im * ts)
                sum_ref[1, :, cols] = sum_ref[1, :, cols] + (im * tc - re * ts)

    for j in range(2):
        spin = turns(j)
        for i in range(4):
            build(even_ref, j, i, mix(j, i), *spin)
    for load in loads[8:]:
        load.wait()

    def body(pair, carry):
        stage(2 * pair, even_ref, 2 * pair + 1, odd_ref)
        stage(2 * pair + 1, odd_ref, 2 * pair + 2, even_ref)
        return carry

    lax.fori_loop(0, 3, body, 0)
    stage(6, even_ref, 7, odd_ref)
    stage(7, odd_ref, None, None)

    for copy in range(2):
        for i in range(CHUNKS - 16):
            out_ref[pl.ds(copy * CHUNKS + 16 + i, 64, stride=2 * CHUNKS), :] = nodes_ref[:, i * 128:(i + 1) * 128]
        for n in range(ERANK):
            for part in range(2):
                for kc in range(4):
                    at = copy * CHUNKS + n * 8 + part * 4 + kc
                    out_ref[pl.ds(at, 64, stride=2 * CHUNKS), :] = (
                        sum_ref[part, n * 64:(n + 1) * 64, kc * 128:(kc + 1) * 128] * scale_out
                    )


def _halves(value):
    high = value.astype(bf16)
    return high, (value - high.astype(f32)).astype(bf16)


def _phase_kernel(order_ref, offsets_ref, rows_ref, out_ref, all_ref, turned_ref):
    left_ref, gram_ref = out_ref.at[0:512], out_ref.at[512:1024]
    slot, half = lax.axis_index("facet"), lax.axis_index("rows")
    rf = _offset_row(order_ref, offsets_ref, 1).astype(jnp.int32)
    own_sr = _pick(rows_ref[...].astype(f32), slot).astype(jnp.int32)
    odd = jnp.concatenate([2 * rf + 7, 2 * rf + 7], 1)
    lane = lax.broadcasted_iota(jnp.int32, (128, 128), 1)
    quarter = jnp.where(lane < 64, 0, -(NIMG // 2))
    sign = jnp.where(lane < 64, -1.0, 1.0).astype(f32)
    for i in range(8):
        here = slice(i * 128, (i + 1) * 128)
        q = lax.broadcasted_iota(jnp.int32, (128, 128), 0) + i * 128 + half * 512
        q = lax.bitwise_and(q, 1023)
        turn = jnp.cos(_angle(odd * (own_sr + q) + quarter))
        other = sign * pltpu.roll(turn, 64, 1)
        g = (q - 512).astype(f32) * (TWO_PI / NIMG * ROW_SCALE)
        g2, g3 = g * g * 0.5, g * g * g * (1.0 / 6.0)
        for n, value in enumerate((turn, g * other, -g2 * turn, -g3 * other)):
            high, low = _halves(value)
            cols = slice(n * 128, (n + 1) * 128)
            all_ref[0, here, cols] = high
            all_ref[1, here, cols] = low
            high_t, low_t = _halves(sign * pltpu.roll(value, 64, 1))
            turned_ref[0, here, cols] = high_t
            turned_ref[1, here, cols] = low_t
            if i < 4 and n < 2:
                left_ref[here, n * 128:(n + 1) * 128] = high
                left_ref[here, 256 + n * 128:256 + (n + 1) * 128] = high
                left_ref[here, 512 + n * 128:512 + (n + 1) * 128] = low
            elif i < 4:
                left_ref[here, 512 + n * 128:512 + (n + 1) * 128] = high
    over_rows = (((0,), (0,)), ((), ()))
    gram = None
    for ref in (all_ref, turned_ref):
        for a, b in ((0, 0), (0, 1), (1, 0)):
            part = lax.dot_general(ref[a], ref[b], over_rows, preferred_element_type=f32)
            gram = part if gram is None else gram + part
    high, low = _halves(gram)
    gram_ref[:, 0:256] = high[:, 0:256]
    gram_ref[:, 256:512] = high[:, 0:256]
    gram_ref[:, 512:768] = low[:, 0:256]
    gram_ref[:, 768:1024] = high[:, 256:512]


def _rows_kernel(got_any, wh_hbm, wl_hbm, pc_hbm, ps_hbm, phases_any, out_hbm,
                 got_ref, wh_ref, wl_ref, pc_ref, ps_ref, gram_ref, left_ref, right_ref, value_ref, high_ref, low_ref,
                 out_ref, sems, out_sems):
    loads = [
        pltpu.make_async_copy(source, target, sems.at[i])
        for i, (source, target) in enumerate((
            (got_any, got_ref), (wh_hbm, wh_ref), (wl_hbm, wl_ref), (pc_hbm, pc_ref), (ps_hbm, ps_ref),
            (phases_any.at[512:1024], gram_ref), (phases_any.at[0:512], left_ref),
        ))
    ]
    for load in loads:
        load.start()
    loads[0].wait()
    parts = [
        jnp.concatenate([got_ref[pl.ds(h * CHUNKS + 16 + i, 64, stride=2 * CHUNKS), :] for i in range(4)], 1)
        for h in range(2)
    ]
    both, between = parts[0] + parts[1], parts[1] - parts[0]
    sums, diffs = [
        [(pltpu.roll(v, 512 - n * 2 * ALL_NODES, 1) if n else v)[:, 0:256] for n in range(OWN_RANK)]
        for v in (both, between)
    ]
    d = 2.0 / ROW_SCALE
    cube = 2.05 / (ROW_SCALE * ROW_SCALE)
    terms = (
        sums[0],
        sums[1] + d * diffs[0],
        sums[2] + (2 * d) * diffs[1] + (d * d) * sums[0],
        (cube + 3 * d * d) * sums[1] + (3 * d) * diffs[2] + (d * d * d) * diffs[0],
    )
    lane = lax.broadcasted_iota(jnp.int32, (64, 256), 1)
    for n, value in enumerate(terms):
        rows = slice(n * 64, (n + 1) * 64)
        value = jnp.where(lane < 2 * ALL_NODES, value, 0.0)
        for part in range(2):
            high, low = _halves(value)
            high_ref[part, rows, :] = high
            if n < 2:
                low_ref[part, rows, :] = low
            value = jnp.where(
                lane < ALL_NODES, pltpu.roll(value, 256 - ALL_NODES, 1), -pltpu.roll(value, ALL_NODES, 1))
    for load in loads[1:5]:
        load.wait()
    for i in range(4):
        cols = slice(i * 256, (i + 1) * 256)
        vals = []
        for part in range(2):
            wh, wl = wh_ref[:, cols], wl_ref[:, cols]
            main = jnp.dot(high_ref[part], wh, preferred_element_type=f32)
            rest = (
                jnp.dot(high_ref[part, 0:128], wl, preferred_element_type=f32)
                + jnp.dot(low_ref[part], wh, preferred_element_type=f32)
            )
            vals.append((main, rest))
        pc, ps = pc_ref[:, cols], ps_ref[:, cols]
        for n in range(RANK):
            rows = slice(n * 64, (n + 1) * 64)
            vr, vi = vals[0][0][rows], vals[1][0][rows]
            if n < ERANK:
                parts = []
                for part in range(2):
                    at = (i // 2) * CHUNKS + n * 8 + part * 4 + 2 * (i % 2)
                    parts.append(jnp.concatenate(
                        [got_ref[pl.ds(at + m, 64, stride=2 * CHUNKS), :] for m in range(2)], 1))
                vr = vr + vals[0][1][rows] + parts[0]
                vi = vi + vals[1][1][rows] + parts[1]
            cr = vr * pc + vi * ps
            ci = vi * pc - vr * ps
            at = n * 128
            value_ref[at:at + 64, cols] = cr
            value_ref[at + 64:at + 128, cols] = ci
            turned = slice(1024 + i * 256, 1024 + (i + 1) * 256)
            cr_high, ci_high = cr.astype(bf16), ci.astype(bf16)
            bases = (0, 512) if n < 2 else (512,)
            for base in bases:
                right_ref[base + at:base + at + 64, cols] = cr_high
                right_ref[base + at + 64:base + at + 128, cols] = ci_high
                right_ref[base + at:base + at + 64, turned] = ci_high
                right_ref[base + at + 64:base + at + 128, turned] = -cr_high
            if n < 2:
                cr_low = (cr - cr_high.astype(f32)).astype(bf16)
                ci_low = (ci - ci_high.astype(f32)).astype(bf16)
                right_ref[256 + at:256 + at + 64, cols] = cr_low
                right_ref[256 + at + 64:256 + at + 128, cols] = ci_low
                right_ref[256 + at:256 + at + 64, turned] = ci_low
                right_ref[256 + at + 64:256 + at + 128, turned] = -cr_low

    loads[5].wait()
    total = jnp.zeros((8, 256), f32)
    for i in range(4):
        cols = slice(i * 256, (i + 1) * 256)
        product = jnp.dot(gram_ref[...], right_ref[:, cols], preferred_element_type=f32) * value_ref[:, cols]
        total = total + jnp.sum(product.reshape(64, 8, 256), 0)
    mean = jnp.maximum(jnp.sum(total), 0.0) / (2.0 * SUBROWS * M)
    factor = lax.rsqrt(jnp.full((8, 128), mean, f32) + 1e-06)[0:1, 0:1]

    loads[6].wait()
    stores = []
    for part in range(2):
        for i in range(4):
            cols = slice(i * 256, (i + 1) * 256)
            right = right_ref[:, part * 1024 + i * 256:part * 1024 + (i + 1) * 256]
            out_ref[part, :, cols] = jnp.dot(left_ref[...], right, preferred_element_type=f32) * factor
            store = pltpu.make_async_copy(
                out_ref.at[part, :, cols], out_hbm.at[0, part, :, cols], out_sems.at[part * 4 + i])
            store.start()
            stores.append(store)
    for store in stores:
        store.wait()


def per_device(facets, facet_window, band_window, facet_order, facet_offsets, sub_cols, sub_rows):
    tables = _tables()
    peer = lax.ppermute(facets, "rows", [(0, 1), (1, 0)])
    order, cols, rows = (v.reshape(1, 64) for v in (facet_order, sub_cols, sub_rows))
    offsets = facet_offsets.T
    window = facet_window.reshape(1, 16384)
    hbm = pl.BlockSpec(memory_space=pltpu.HBM)
    anywhere = pl.BlockSpec(memory_space=pl.ANY)
    vmem = pl.BlockSpec(memory_space=pltpu.VMEM)
    shape = jax.ShapeDtypeStruct

    def params(mib):
        return pltpu.CompilerParams(vmem_limit_bytes=mib * 1024 * 1024)

    wide, wide16, narrow = shape((64, 1024), f32), shape((64, 1024), bf16), shape((64, 128), f32)
    lc, ls, pc, ps, mc, ms, combine, nodes = pl.pallas_call(
        _exact_kernel,
        in_specs=[hbm] * 10,
        out_specs=[hbm] * 7 + [vmem],
        out_shape=[wide16, wide16, wide, wide, narrow, narrow, shape((256, 16), bf16),
                   shape((64, 128 * (CHUNKS - 16)), f32)],
        scratch_shapes=[
            pltpu.VMEM((1, 64), jnp.int32), pltpu.VMEM((2, 64), jnp.int32), pltpu.VMEM((1, 64), jnp.int32),
            pltpu.VMEM((1, 64), jnp.int32), pltpu.VMEM((1, M), f32), pltpu.VMEM((1, 2, 4, 16384), f32),
            pltpu.VMEM((1, 16384), f32), pltpu.VMEM((SPAN, 128), bf16),
            pltpu.VMEM((OWN_RANK * 256, 512), bf16), pltpu.VMEM((OWN_RANK * 256, 512), bf16),
            pltpu.VMEM((64, 1024), f32), pltpu.VMEM((64, 1024), f32), pltpu.VMEM((64, 1024), bf16),
            pltpu.VMEM((64, 1024), bf16), pltpu.VMEM((64, 1024), f32), pltpu.VMEM((64, 1024), f32),
            pltpu.VMEM((64, 128), f32), pltpu.VMEM((64, 128), f32), pltpu.VMEM((256, 16), bf16),
            pltpu.VMEM((512, BLOCK), bf16), pltpu.VMEM((512, BLOCK), bf16), pltpu.VMEM((4, 512, 128), f32),
            pltpu.VMEM((64, OWN_RANK * 256), f32),
            pltpu.SemaphoreType.DMA((10,)), pltpu.SemaphoreType.DMA((7,)),
        ],
        compiler_params=params(60),
        cost_estimate=pl.CostEstimate(flops=8 * 10**9, bytes_accessed=2 * 10**6, transcendentals=0),
        name="exact_part",
    )(order, offsets, cols, rows, band_window.reshape(1, M), facets, window, jnp.asarray(tables["sample"]),
      jnp.asarray(tables["join_hi"]), jnp.asarray(tables["join_lo"]))

    send = pl.pallas_call(
        _residual_kernel,
        in_specs=[hbm, anywhere] + [hbm] * 10,
        out_shape=shape((128 * CHUNKS, 128), f32),
        scratch_shapes=[
            pltpu.VMEM((1, 2, 4, 16384), f32), pltpu.VMEM((1, 2, 4, 16384), f32), pltpu.VMEM((1, 16384), f32),
            pltpu.VMEM((64, 1024), bf16), pltpu.VMEM((64, 1024), bf16), pltpu.VMEM((64, 128), f32),
            pltpu.VMEM((64, 128), f32), pltpu.VMEM((256, 16), bf16),
            pltpu.VMEM((1024, 1024), f8), pltpu.VMEM((16, 512), f32), pltpu.VMEM((16, 512), f32),
            pltpu.VMEM((64, 128 * (CHUNKS - 16)), f32),
            pltpu.VMEM((512, 1024), f8), pltpu.VMEM((512, 1024), f8), pltpu.VMEM((2, 128, 512), f32),
            pltpu.SemaphoreType.DMA((12,)),
        ],
        compiler_params=params(60),
        cost_estimate=pl.CostEstimate(flops=9 * 10**9, bytes_accessed=4 * 10**6, transcendentals=0),
        name="residual_part",
    )(
        facets, peer, window, lc, ls, mc, ms, combine, jnp.asarray(tables["resid"]), jnp.asarray(tables["turn_c"]),
        jnp.asarray(tables["turn_s"]), nodes,
    )

    got = lax.all_to_all(send.reshape(128, CHUNKS // 4, 4, 128), ("facet", "rows"), split_axis=0, concat_axis=0, tiled=True)
    phases = pl.pallas_call(
        _phase_kernel,
        in_specs=[vmem] * 3,
        out_shape=shape((1024, 1024), bf16),
        scratch_shapes=[pltpu.VMEM((2, 1024, 512), bf16), pltpu.VMEM((2, 1024, 512), bf16)],
        compiler_params=params(60),
        cost_estimate=pl.CostEstimate(flops=3 * 10**9, bytes_accessed=2 * 10**6, transcendentals=2 * 10**5),
        name="row_phases",
    )(order, offsets, rows)

    return pl.pallas_call(
        _rows_kernel,
        in_specs=[anywhere] + [hbm] * 4 + [anywhere],
        out_specs=hbm,
        out_shape=shape((1, 2, 512, 1024), f32),
        scratch_shapes=[
            pltpu.VMEM((128 * CHUNKS, 128), f32), pltpu.VMEM((256, 1024), bf16), pltpu.VMEM((256, 1024), bf16),
            pltpu.VMEM((64, 1024), f32), pltpu.VMEM((64, 1024), f32), pltpu.VMEM((512, 1024), bf16),
            pltpu.VMEM((512, 1024), bf16), pltpu.VMEM((1024, 2048), bf16), pltpu.VMEM((512, 1024), f32),
            pltpu.VMEM((2, 256, 256), bf16), pltpu.VMEM((2, 128, 256), bf16), pltpu.VMEM((2, 512, 1024), f32),
            pltpu.SemaphoreType.DMA((7,)), pltpu.SemaphoreType.DMA((8,)),
        ],
        compiler_params=params(60),
        cost_estimate=pl.CostEstimate(flops=5 * 10**9, bytes_accessed=12 * 10**6, transcendentals=0),
        name="row_transform",
    )(got.reshape(128 * CHUNKS, 128), jnp.asarray(tables["weave_hi"]), jnp.asarray(tables["weave_lo"]), pc, ps, phases)


def solution(mesh):
    return jax.shard_map(
        per_device,
        mesh=mesh,
        in_specs=(P("facet", None, "rows", None), P(), P(), P(), P(), P(), P()),
        out_specs=P("facet", None, "rows", None),
        check_vma=False,
    )
```

```python
import functools
import math

import jax
import jax.numpy as jnp
import ml_dtypes
import numpy as np
from jax import lax
from jax.experimental import pallas as pl
from jax.experimental.pallas import tpu as pltpu
from jax.sharding import PartitionSpec as P

NIMG = 262144
M = 1024
SUBROWS = 1024
TWO_PI = 2.0 * math.pi

BLOCK = 1024
SPAN = 4096
NODES = 32
WIDTH = 16384
ALL_NODES = 85
RANK = 4
OWN_RANK = 3
ERANK = 2
ROW_SCALE = 4.0
TABLE_SCALE = 32768.0
DATA_SCALE = 16.0

f32 = jnp.float32
bf16 = jnp.bfloat16
f8 = jnp.float8_e4m3fn


def _split(values):
    high = values.astype(np.float32).astype(ml_dtypes.bfloat16)
    low = (values - high.astype(np.float64)).astype(np.float32).astype(ml_dtypes.bfloat16)
    return high, low


def _kernel_sum(x, count):
    den = np.sin(np.pi * x / NIMG)
    zero = np.abs(den) < 1e-14
    return np.where(zero, float(count), np.sin(np.pi * x * count / NIMG) / np.where(zero, 1.0, den))


def _solve(gram, right):
    gram, right = gram.copy(), right.copy()
    n = len(gram)
    for i in range(n):
        for j in range(i + 1, n):
            factor = gram[j, i] / gram[i, i]
            gram[j] = gram[j] - factor * gram[i]
            right[j] = right[j] - factor * right[i]
    out = np.zeros_like(right)
    for i in range(n - 1, -1, -1):
        total = right[i].copy()
        for j in range(i + 1, n):
            total = total - gram[i, j] * out[j]
        out[i] = total / gram[i, i]
    return out


@functools.lru_cache(maxsize=None)
def _tables():
    scale = TWO_PI / NIMG
    bands = np.arange(M)
    product = (np.arange(BLOCK)[:, None] * bands[None, :]) % NIMG
    angle = (np.float32(scale) * product.astype(np.float32)).astype(np.float64)
    exact = scale * product
    resid_c = np.cos(angle).astype(np.float32).astype(ml_dtypes.bfloat16).astype(np.float64) - np.cos(exact)
    resid_s = np.sin(angle).astype(np.float32).astype(ml_dtypes.bfloat16).astype(np.float64) - np.sin(exact)
    half = M // 2
    resid = np.stack(
        [np.concatenate([resid_c[:, h * half:(h + 1) * half], resid_s[:, h * half:(h + 1) * half]], 1) for h in range(2)]
    )
    resid = (resid * TABLE_SCALE).astype(np.float32).astype(ml_dtypes.float8_e4m3fn)
    def spread(count, width, even):
        i = np.arange(count)
        return 511.5 + 512 * width * (even * ((2 * i + 1) / count - 1) - (1 - even) * np.cos(np.pi * (i + 0.5) / count))

    def interpolate(nodes, targets, columns):
        gram = _kernel_sum(nodes[:, None] - nodes[None, :], columns) + 1e-13 * columns * np.eye(len(nodes))
        return _solve(gram, _kernel_sum(nodes[:, None] - targets[None, :], columns))

    nodes, all_nodes = spread(NODES, 1.05, 0.25), spread(ALL_NODES, 1.04, 0.6)
    centre = (SPAN - 1) / 2
    at = scale * (np.arange(SPAN) - centre)[:, None] * nodes[None, :]
    sample = np.concatenate([np.cos(at), -np.sin(at)], 1)
    sample = np.concatenate(_split(sample), 1)
    middle = (WIDTH - 1) / 2
    interp = interpolate(nodes, all_nodes, SPAN)
    rows = []
    for span in range(WIDTH // SPAN):
        turn = scale * (span * SPAN + centre - middle) * all_nodes
        re, im = interp * np.cos(turn), -interp * np.sin(turn)
        rows += [np.concatenate([re, im], 1), np.concatenate([-im, re], 1)]
    joined = np.concatenate(rows, 0)
    join = np.zeros((OWN_RANK * 256, 512))
    for n in range(OWN_RANK):
        join[n * 256:(n + 1) * 256, n * 2 * ALL_NODES:(n + 1) * 2 * ALL_NODES] = joined
    join_hi, join_lo = _split(join)
    interp = interpolate(all_nodes, bands.astype(np.float64), WIDTH)
    turn = scale * middle * bands
    weave = np.zeros((256, M))
    weave[:2 * ALL_NODES] = np.concatenate([interp * np.cos(turn), interp * np.sin(turn)], 0)
    weave_hi, weave_lo = _split(weave)
    turn = TWO_PI * ((np.arange(16)[:, None] * (bands[None, :half] % 256)) % 256) / 256
    return dict(
        resid=resid, sample=sample, join_hi=join_hi, join_lo=join_lo, weave_hi=weave_hi, weave_lo=weave_lo,
        turn_c=np.cos(turn).astype(np.float32), turn_s=np.sin(turn).astype(np.float32),
    )


COL_A, COL_SC8, COL_CF8, COL_ROW = 0, 16, 24, 32
CHUNKS = 20


def _angle(product):
    turns = lax.bitwise_and(product + NIMG, 2 * NIMG - 1) - NIMG
    return turns.astype(f32) * (math.pi / NIMG)


def _offset_row(order_ref, offsets_ref, which):
    slots = lax.broadcasted_iota(jnp.int32, (64, 64), 0)
    offsets = _to_column(offsets_ref[which:which + 1, :].astype(f32))
    return jnp.sum(jnp.where(slots == order_ref[...], offsets, 0.0), axis=0, keepdims=True)


def _to_column(row):
    at = lax.broadcasted_iota(jnp.int32, (64, 64), 0) == lax.broadcasted_iota(jnp.int32, (64, 64), 1)
    return jnp.sum(jnp.where(at, row, 0.0), axis=1, keepdims=True)


def _pick(row, index):
    lane = lax.broadcasted_iota(jnp.int32, row.shape, 1)
    return jnp.sum(jnp.where(lane == index, row, 0.0), axis=1, keepdims=True)


def _prepare(slot, half, order_ref, offsets_ref, cols_ref, rows_ref, band_ref,
             lc_ref, ls_ref, pc_ref, ps_ref, mc_ref, ms_ref, combine_ref):
    cf_row = _offset_row(order_ref, offsets_ref, 0)
    own_cf = _pick(cf_row, slot).astype(jnp.int32)
    cf = _to_column(cf_row).astype(jnp.int32)
    sc = _to_column(cols_ref[...].astype(f32)).astype(jnp.int32)
    sr = _to_column(rows_ref[...].astype(f32)).astype(jnp.int32)
    lane = lax.broadcasted_iota(jnp.int32, (64, 128), 1)
    row = lax.bitwise_and(4 * half + 4 * lax.bitwise_and(lane // 8, 1) + lax.bitwise_and(lane, 3), 7)
    odd = 2 * row - 7
    factor = jnp.where(
        lane < COL_SC8, 2 * (own_cf + 1024 * lane),
        jnp.where(lane < COL_CF8, 256 * (lane - COL_SC8), jnp.where(lane < COL_ROW, 256 * (lane - COL_CF8), odd)),
    )
    other = jnp.where(lane < COL_CF8, sc, jnp.where(lane < COL_ROW, cf, sr + 512))
    angle = _angle(factor * other)
    mc, ms = jnp.cos(angle), jnp.sin(angle)
    mc_ref[...] = mc
    ms_ref[...] = ms
    angle = _angle(2 * lane * sc)
    low_c, low_s = jnp.cos(angle), jnp.sin(angle)
    for i in range(8):
        c, s = mc[:, COL_SC8 + i:COL_SC8 + i + 1], ms[:, COL_SC8 + i:COL_SC8 + i + 1]
        lc_ref[:, i * 128:(i + 1) * 128] = c * low_c - s * low_s
        ls_ref[:, i * 128:(i + 1) * 128] = s * low_c + c * low_s
    angle = _angle(2 * lane * cf)
    low_c, low_s = jnp.cos(angle), jnp.sin(angle)
    for i in range(8):
        c, s = mc[:, COL_CF8 + i:COL_CF8 + i + 1], ms[:, COL_CF8 + i:COL_CF8 + i + 1]
        band = band_ref[:, i * 128:(i + 1) * 128]
        pc_ref[:, i * 128:(i + 1) * 128] = (c * low_c - s * low_s) * band
        ps_ref[:, i * 128:(i + 1) * 128] = (s * low_c + c * low_s) * band
    rho = odd.astype(f32) * (0.5 / ROW_SCALE)
    power = jnp.ones((64, 128), f32)
    first = lax.bitwise_and(lane, 4) == 0
    to_re, to_im = jnp.where(first, mc, ms), jnp.where(first, -ms, mc)
    for n in range(ERANK):
        for part, value in ((0, to_re), (1, to_im)):
            base = part * 128 + n * 64
            combine_ref[base:base + 64, :] = (value * power)[:, COL_ROW:COL_ROW + 16].astype(bf16)
        power = power * rho


def _exact_kernel(order_hbm, offsets_hbm, cols_hbm, rows_hbm, band_hbm, data_hbm, window_hbm, sample_hbm, jh_hbm, jl_hbm,
                  lc_hbm, ls_hbm, pc_hbm, ps_hbm, mc_hbm, ms_hbm, combine_hbm, out_ref,
                  order_ref, offsets_ref, cols_ref, rows_ref, band_ref, data_ref, window_ref, sample_ref, jh_ref, jl_ref,
                  lc_ref, ls_ref, lc16_ref, ls16_ref, pc_ref, ps_ref, mc_ref, ms_ref, combine_ref,
                  even_ref, odd_ref, acc_ref, terms_ref, sems, out_sems):
    loads = [
        pltpu.make_async_copy(source, target, sems.at[i])
        for i, (source, target) in enumerate((
            (order_hbm, order_ref), (offsets_hbm, offsets_ref), (cols_hbm, cols_ref), (rows_hbm, rows_ref),
            (band_hbm, band_ref), (data_hbm, data_ref), (window_hbm, window_ref), (sample_hbm, sample_ref),
            (jh_hbm, jh_ref), (jl_hbm, jl_ref),
        ))
    ]
    for load in loads:
        load.start()
    for load in loads[:5]:
        load.wait()
    acc_ref[...] = jnp.zeros_like(acc_ref)
    _prepare(lax.axis_index("facet"), lax.axis_index("rows"), order_ref, offsets_ref, cols_ref, rows_ref, band_ref,
             lc_ref, ls_ref, pc_ref, ps_ref, mc_ref, ms_ref, combine_ref)
    lc16_ref[...] = lc_ref[...].astype(bf16)
    ls16_ref[...] = ls_ref[...].astype(bf16)
    stores = [
        pltpu.make_async_copy(source, target, out_sems.at[i])
        for i, (source, target) in enumerate((
            (lc16_ref, lc_hbm), (ls16_ref, ls_hbm), (pc_ref, pc_hbm), (ps_ref, ps_hbm), (mc_ref, mc_hbm), (ms_ref, ms_hbm),
            (combine_ref, combine_hbm),
        ))
    ]
    for store in stores:
        store.start()
    for load in loads[5:8]:
        load.wait()

    def build(block, x_ref, bc, bs, i):
        cols = slice(i * 256, (i + 1) * 256)
        here = pl.ds(pl.multiple_of(block * BLOCK + i * 256, 256), 256)
        window = window_ref[:, here]
        re_rows = data_ref[0, 0, :, here] * window
        im_rows = data_ref[0, 1, :, here] * window
        for g in range(4):
            rows = slice(g * 16, (g + 1) * 16)
            lc, ls = lc_ref[rows, cols], ls_ref[rows, cols]
            c, s = bc[rows], bs[rows]
            ec = c * lc - s * ls
            es = s * lc + c * ls
            for r in range(4):
                dr, di = re_rows[r:r + 1], im_rows[r:r + 1]
                at = r * 64 + g * 16
                x_ref[at:at + 16, cols] = (dr * ec + di * es).astype(bf16)
                x_ref[256 + at:256 + at + 16, cols] = (di * ec - dr * es).astype(bf16)

    def turns(block):
        return _pick(mc_ref[...], block), _pick(ms_ref[...], block)

    def stage(block, x_ref, following, next_ref):
        bc, bs = turns(following)
        span = block // 4
        for i in range(4):
            rows = pl.ds(pl.multiple_of(lax.rem(block, 4) * BLOCK + i * 256, 256), 256)
            part = jnp.dot(x_ref[:, i * 256:(i + 1) * 256], sample_ref[rows, :], preferred_element_type=f32)
            build(following, next_ref, bc, bs, i)
            acc_ref[span] = acc_ref[span] + part

    bc, bs = turns(0)
    for i in range(4):
        build(0, even_ref, bc, bs, i)

    def body(pair, carry):
        stage(2 * pair, even_ref, 2 * pair + 1, odd_ref)
        stage(2 * pair + 1, odd_ref, lax.rem(2 * pair + 2, 16), even_ref)
        return carry

    lax.fori_loop(0, 8, body, 0)

    first = lax.broadcasted_iota(jnp.int32, (64, 128), 1) < 64
    lane = lax.broadcasted_iota(jnp.int32, (64, 128), 1)
    sign = jnp.where(lax.bitwise_and(lane, 32) == 0, -1.0, 1.0).astype(f32)
    places = [(r - 1.5) / ROW_SCALE for r in range(4)]
    spins = [
        [jnp.broadcast_to(ref[:, COL_ROW + r:COL_ROW + r + 1], (64, 128)) for ref in (mc_ref, ms_ref)] for r in range(4)
    ]
    for pair in range(2):
        sums = []
        for span in (2 * pair, 2 * pair + 1):
            direct, across = [None] * OWN_RANK, [None] * OWN_RANK
            for r in range(4):
                c, s = spins[r]
                re = acc_ref[span, r * 64:(r + 1) * 64]
                im = acc_ref[span, 256 + r * 64:256 + (r + 1) * 64]
                one, two = c * re + s * im, c * im - s * re
                for n in range(OWN_RANK):
                    direct[n] = one if r == 0 else direct[n] + one
                    across[n] = two if r == 0 else across[n] + two
                    one, two = one * places[r], two * places[r]
            sums.append((direct, across))
        for n in range(OWN_RANK):
            folded = []
            for which in range(2):
                a, b = sums[0][which][n], sums[1][which][n]
                folded.append(jnp.where(first, a, b) + pltpu.roll(jnp.where(first, b, a), 64, 1))
            at = n * 256 + pair * 128
            terms_ref[:, at:at + 128] = folded[0] + jnp.where(
                sign < 0, -pltpu.roll(folded[1], 96, 1), pltpu.roll(folded[1], 32, 1))
    for load in loads[8:]:
        load.wait()
    high, low = _halves(terms_ref[...])
    out_ref[...] = (
        jnp.dot(high, jh_ref[...], preferred_element_type=f32)
        + (jnp.dot(high, jl_ref[...], preferred_element_type=f32) + jnp.dot(low, jh_ref[...], preferred_element_type=f32))
    )
    for store in stores:
        store.wait()


def _residual_kernel(own_hbm, peer_any, window_hbm, lc_hbm, ls_hbm, mc_hbm, ms_hbm, combine_hbm,
                     table_hbm, tc_hbm, ts_hbm, nodes_hbm, out_ref,
                     own_ref, peer_ref, window_ref, lc_ref, ls_ref, mc_ref, ms_ref, combine_ref,
                     table_ref, tc_ref, ts_ref, nodes_ref, even_ref, odd_ref, sum_ref, sems):
    loads = [
        pltpu.make_async_copy(source, target, sems.at[i])
        for i, (source, target) in enumerate((
            (own_hbm, own_ref), (peer_any, peer_ref), (window_hbm, window_ref), (lc_hbm, lc_ref), (ls_hbm, ls_ref),
            (mc_hbm, mc_ref), (ms_hbm, ms_ref), (combine_hbm, combine_ref),
            (table_hbm.at[lax.axis_index("rows")], table_ref), (tc_hbm, tc_ref), (ts_hbm, ts_ref),
            (nodes_hbm, nodes_ref),
        ))
    ]
    for load in loads:
        load.start()
    sum_ref[...] = jnp.zeros_like(sum_ref)
    for load in loads[:3]:
        load.wait()
    largest = jnp.zeros((4, 2048), f32)
    for i in range(8):
        here = slice(i * 2048, (i + 1) * 2048)
        window = window_ref[:, here]
        for ref in (own_ref, peer_ref):
            for part in range(2):
                largest = jnp.maximum(largest, jnp.abs(ref[0, part, :, here] * window))
    largest = jnp.maximum(jnp.max(jnp.max(largest, axis=1, keepdims=True), axis=0, keepdims=True), 1e-30)
    scale_in = DATA_SCALE / largest
    scale_out = largest * (1.0 / (DATA_SCALE * TABLE_SCALE))
    for load in loads[3:8]:
        load.wait()

    def mix(block, i):
        here = pl.ds(pl.multiple_of(block * BLOCK + i * 256, 256), 256)
        window = window_ref[:, here] * scale_in
        data = jnp.concatenate(
            [own_ref[0, 0, :, here], own_ref[0, 1, :, here], peer_ref[0, 0, :, here], peer_ref[0, 1, :, here]], 0
        )
        return jnp.dot(combine_ref[...], (data * window).astype(bf16), preferred_element_type=f32)

    def build(z_ref, j, i, rows, bc, bs):
        cols = slice(i * 256, (i + 1) * 256)
        lc, ls = lc_ref[:, cols], ls_ref[:, cols]
        ec = bc * lc - bs * ls
        es = bs * lc + bc * ls
        rows = rows.astype(bf16)
        for n in range(ERANK):
            gr, gi = rows[n * 64:(n + 1) * 64], rows[128 + n * 64:128 + (n + 1) * 64]
            at = j * 256 + n * 64
            z_ref[at:at + 64, cols] = (gr * ec + gi * es).astype(z_ref.dtype)
            z_ref[at + 128:at + 192, cols] = (gi * ec - gr * es).astype(z_ref.dtype)

    def turns(block):
        return tuple(
            jnp.broadcast_to(_pick(ref[...], block), (64, 256)).astype(bf16) for ref in (mc_ref, ms_ref)
        )

    def stage(group, z_ref, following, next_ref):
        tasks = [(j, i) for j in range(2) for i in range(4)]
        building = following is not None
        if building:
            spins = [turns(following * 2 + j) for j in range(2)]
            ready = mix(following * 2, 0)
        at = 0
        for j in range(2):
            for kc in range(2):
                cols = slice(kc * 256, (kc + 1) * 256)
                z = z_ref[j * 256:(j + 1) * 256, :]
                by_c = jnp.dot(z, table_ref[:, cols], preferred_element_type=f32)
                by_s = jnp.dot(z, table_ref[:, 512 + kc * 256:768 + kc * 256], preferred_element_type=f32)
                for _ in range(2 if building else 0):
                    bj, bi = tasks[at]
                    at += 1
                    coming = mix(following * 2 + tasks[at][0], tasks[at][1]) if at < 8 else None
                    build(next_ref, bj, bi, ready, *spins[bj])
                    ready = coming
                re = by_c[0:128] + by_s[128:256]
                im = by_c[128:256] - by_s[0:128]
                tc = tc_ref[pl.ds(group * 2 + j, 1), cols]
                ts = ts_ref[pl.ds(group * 2 + j, 1), cols]
                sum_ref[0, :, cols] = sum_ref[0, :, cols] + (re * tc + im * ts)
                sum_ref[1, :, cols] = sum_ref[1, :, cols] + (im * tc - re * ts)

    for j in range(2):
        spin = turns(j)
        for i in range(4):
            build(even_ref, j, i, mix(j, i), *spin)
    for load in loads[8:]:
        load.wait()

    def body(pair, carry):
        stage(2 * pair, even_ref, 2 * pair + 1, odd_ref)
        stage(2 * pair + 1, odd_ref, 2 * pair + 2, even_ref)
        return carry

    lax.fori_loop(0, 3, body, 0)
    stage(6, even_ref, 7, odd_ref)
    stage(7, odd_ref, None, None)

    for copy in range(2):
        for i in range(CHUNKS - 16):
            out_ref[pl.ds(copy * CHUNKS + 16 + i, 64, stride=2 * CHUNKS), :] = nodes_ref[:, i * 128:(i + 1) * 128]
        for n in range(ERANK):
            for part in range(2):
                for kc in range(4):
                    at = copy * CHUNKS + n * 8 + part * 4 + kc
                    out_ref[pl.ds(at, 64, stride=2 * CHUNKS), :] = (
                        sum_ref[part, n * 64:(n + 1) * 64, kc * 128:(kc + 1) * 128] * scale_out
                    )


def _halves(value):
    high = value.astype(bf16)
    return high, (value - high.astype(f32)).astype(bf16)


def _phase_kernel(order_ref, offsets_ref, rows_ref, out_ref, all_ref, turned_ref):
    left_ref, gram_ref = out_ref.at[0:512], out_ref.at[512:1024]
    slot, half = lax.axis_index("facet"), lax.axis_index("rows")
    rf = _offset_row(order_ref, offsets_ref, 1).astype(jnp.int32)
    own_sr = _pick(rows_ref[...].astype(f32), slot).astype(jnp.int32)
    odd = jnp.concatenate([2 * rf + 7, 2 * rf + 7], 1)
    lane = lax.broadcasted_iota(jnp.int32, (128, 128), 1)
    quarter = jnp.where(lane < 64, 0, -(NIMG // 2))
    sign = jnp.where(lane < 64, -1.0, 1.0).astype(f32)
    for i in range(8):
        here = slice(i * 128, (i + 1) * 128)
        q = lax.broadcasted_iota(jnp.int32, (128, 128), 0) + i * 128 + half * 512
        q = lax.bitwise_and(q, 1023)
        turn = jnp.cos(_angle(odd * (own_sr + q) + quarter))
        other = sign * pltpu.roll(turn, 64, 1)
        g = (q - 512).astype(f32) * (TWO_PI / NIMG * ROW_SCALE)
        g2, g3 = g * g * 0.5, g * g * g * (1.0 / 6.0)
        for n, value in enumerate((turn, g * other, -g2 * turn, -g3 * other)):
            high, low = _halves(value)
            cols = slice(n * 128, (n + 1) * 128)
            all_ref[0, here, cols] = high
            all_ref[1, here, cols] = low
            high_t, low_t = _halves(sign * pltpu.roll(value, 64, 1))
            turned_ref[0, here, cols] = high_t
            turned_ref[1, here, cols] = low_t
            if i < 4 and n < 2:
                left_ref[here, n * 128:(n + 1) * 128] = high
                left_ref[here, 256 + n * 128:256 + (n + 1) * 128] = high
                left_ref[here, 512 + n * 128:512 + (n + 1) * 128] = low
            elif i < 4:
                left_ref[here, 512 + n * 128:512 + (n + 1) * 128] = high
    over_rows = (((0,), (0,)), ((), ()))
    gram = None
    for ref in (all_ref, turned_ref):
        for a, b in ((0, 0), (0, 1), (1, 0)):
            part = lax.dot_general(ref[a], ref[b], over_rows, preferred_element_type=f32)
            gram = part if gram is None else gram + part
    high, low = _halves(gram)
    gram_ref[:, 0:256] = high[:, 0:256]
    gram_ref[:, 256:512] = high[:, 0:256]
    gram_ref[:, 512:768] = low[:, 0:256]
    gram_ref[:, 768:1024] = high[:, 256:512]


def _rows_kernel(got_ref, wh_hbm, wl_hbm, pc_hbm, ps_hbm, phases_any, out_hbm,
                 wh_ref, wl_ref, pc_ref, ps_ref, gram_ref, left_ref, right_ref, value_ref, high_ref, low_ref,
                 out_ref, sems, out_sems):
    loads = [
        pltpu.make_async_copy(source, target, sems.at[i])
        for i, (source, target) in enumerate((
            (wh_hbm, wh_ref), (wl_hbm, wl_ref), (pc_hbm, pc_ref), (ps_hbm, ps_ref),
            (phases_any.at[512:1024], gram_ref), (phases_any.at[0:512], left_ref),
        ))
    ]
    for load in loads:
        load.start()
    parts = [
        jnp.concatenate([got_ref[pl.ds(h * CHUNKS + 16 + i, 64, stride=2 * CHUNKS), :] for i in range(4)], 1)
        for h in range(2)
    ]
    both, between = parts[0] + parts[1], parts[1] - parts[0]
    sums, diffs = [
        [(pltpu.roll(v, 512 - n * 2 * ALL_NODES, 1) if n else v)[:, 0:256] for n in range(OWN_RANK)]
        for v in (both, between)
    ]
    d = 2.0 / ROW_SCALE
    cube = 2.05 / (ROW_SCALE * ROW_SCALE)
    terms = (
        sums[0],
        sums[1] + d * diffs[0],
        sums[2] + (2 * d) * diffs[1] + (d * d) * sums[0],
        (cube + 3 * d * d) * sums[1] + (3 * d) * diffs[2] + (d * d * d) * diffs[0],
    )
    lane = lax.broadcasted_iota(jnp.int32, (64, 256), 1)
    for n, value in enumerate(terms):
        rows = slice(n * 64, (n + 1) * 64)
        value = jnp.where(lane < 2 * ALL_NODES, value, 0.0)
        for part in range(2):
            high, low = _halves(value)
            high_ref[part, rows, :] = high
            if n < 2:
                low_ref[part, rows, :] = low
            value = jnp.where(
                lane < ALL_NODES, pltpu.roll(value, 256 - ALL_NODES, 1), -pltpu.roll(value, ALL_NODES, 1))
    for load in loads[0:4]:
        load.wait()
    for i in range(4):
        cols = slice(i * 256, (i + 1) * 256)
        vals = []
        for part in range(2):
            wh, wl = wh_ref[:, cols], wl_ref[:, cols]
            main = jnp.dot(high_ref[part], wh, preferred_element_type=f32)
            rest = (
                jnp.dot(high_ref[part, 0:128], wl, preferred_element_type=f32)
                + jnp.dot(low_ref[part], wh, preferred_element_type=f32)
            )
            vals.append((main, rest))
        pc, ps = pc_ref[:, cols], ps_ref[:, cols]
        for n in range(RANK):
            rows = slice(n * 64, (n + 1) * 64)
            vr, vi = vals[0][0][rows], vals[1][0][rows]
            if n < ERANK:
                parts = []
                for part in range(2):
                    at = (i // 2) * CHUNKS + n * 8 + part * 4 + 2 * (i % 2)
                    parts.append(jnp.concatenate(
                        [got_ref[pl.ds(at + m, 64, stride=2 * CHUNKS), :] for m in range(2)], 1))
                vr = vr + vals[0][1][rows] + parts[0]
                vi = vi + vals[1][1][rows] + parts[1]
            cr = vr * pc + vi * ps
            ci = vi * pc - vr * ps
            at = n * 128
            value_ref[at:at + 64, cols] = cr
            value_ref[at + 64:at + 128, cols] = ci
            turned = slice(1024 + i * 256, 1024 + (i + 1) * 256)
            cr_high, ci_high = cr.astype(bf16), ci.astype(bf16)
            bases = (0, 512) if n < 2 else (512,)
            for base in bases:
                right_ref[base + at:base + at + 64, cols] = cr_high
                right_ref[base + at + 64:base + at + 128, cols] = ci_high
                right_ref[base + at:base + at + 64, turned] = ci_high
                right_ref[base + at + 64:base + at + 128, turned] = -cr_high
            if n < 2:
                cr_low = (cr - cr_high.astype(f32)).astype(bf16)
                ci_low = (ci - ci_high.astype(f32)).astype(bf16)
                right_ref[256 + at:256 + at + 64, cols] = cr_low
                right_ref[256 + at + 64:256 + at + 128, cols] = ci_low
                right_ref[256 + at:256 + at + 64, turned] = ci_low
                right_ref[256 + at + 64:256 + at + 128, turned] = -cr_low

    loads[4].wait()
    total = jnp.zeros((8, 256), f32)
    for i in range(4):
        cols = slice(i * 256, (i + 1) * 256)
        product = jnp.dot(gram_ref[...], right_ref[:, cols], preferred_element_type=f32) * value_ref[:, cols]
        total = total + jnp.sum(product.reshape(64, 8, 256), 0)
    mean = jnp.maximum(jnp.sum(total), 0.0) / (2.0 * SUBROWS * M)
    factor = lax.rsqrt(jnp.full((8, 128), mean, f32) + 1e-06)[0:1, 0:1]

    loads[5].wait()
    stores = []
    for part in range(2):
        for i in range(4):
            cols = slice(i * 256, (i + 1) * 256)
            right = right_ref[:, part * 1024 + i * 256:part * 1024 + (i + 1) * 256]
            out_ref[part, :, cols] = jnp.dot(left_ref[...], right, preferred_element_type=f32) * factor
            store = pltpu.make_async_copy(
                out_ref.at[part, :, cols], out_hbm.at[0, part, :, cols], out_sems.at[part * 4 + i])
            store.start()
            stores.append(store)
    for store in stores:
        store.wait()


def per_device(facets, facet_window, band_window, facet_order, facet_offsets, sub_cols, sub_rows):
    tables = _tables()
    peer = lax.ppermute(facets, "rows", [(0, 1), (1, 0)])
    order, cols, rows = (v.reshape(1, 64) for v in (facet_order, sub_cols, sub_rows))
    offsets = facet_offsets.T
    window = facet_window.reshape(1, 16384)
    hbm = pl.BlockSpec(memory_space=pltpu.HBM)
    anywhere = pl.BlockSpec(memory_space=pl.ANY)
    vmem = pl.BlockSpec(memory_space=pltpu.VMEM)
    shape = jax.ShapeDtypeStruct

    def params(mib):
        return pltpu.CompilerParams(vmem_limit_bytes=mib * 1024 * 1024)

    wide, wide16, narrow = shape((64, 1024), f32), shape((64, 1024), bf16), shape((64, 128), f32)
    lc, ls, pc, ps, mc, ms, combine, nodes = pl.pallas_call(
        _exact_kernel,
        in_specs=[hbm] * 10,
        out_specs=[hbm] * 7 + [vmem],
        out_shape=[wide16, wide16, wide, wide, narrow, narrow, shape((256, 16), bf16),
                   shape((64, 128 * (CHUNKS - 16)), f32)],
        scratch_shapes=[
            pltpu.VMEM((1, 64), jnp.int32), pltpu.VMEM((2, 64), jnp.int32), pltpu.VMEM((1, 64), jnp.int32),
            pltpu.VMEM((1, 64), jnp.int32), pltpu.VMEM((1, M), f32), pltpu.VMEM((1, 2, 4, 16384), f32),
            pltpu.VMEM((1, 16384), f32), pltpu.VMEM((SPAN, 128), bf16),
            pltpu.VMEM((OWN_RANK * 256, 512), bf16), pltpu.VMEM((OWN_RANK * 256, 512), bf16),
            pltpu.VMEM((64, 1024), f32), pltpu.VMEM((64, 1024), f32), pltpu.VMEM((64, 1024), bf16),
            pltpu.VMEM((64, 1024), bf16), pltpu.VMEM((64, 1024), f32), pltpu.VMEM((64, 1024), f32),
            pltpu.VMEM((64, 128), f32), pltpu.VMEM((64, 128), f32), pltpu.VMEM((256, 16), bf16),
            pltpu.VMEM((512, BLOCK), bf16), pltpu.VMEM((512, BLOCK), bf16), pltpu.VMEM((4, 512, 128), f32),
            pltpu.VMEM((64, OWN_RANK * 256), f32),
            pltpu.SemaphoreType.DMA((10,)), pltpu.SemaphoreType.DMA((7,)),
        ],
        compiler_params=params(60),
        cost_estimate=pl.CostEstimate(flops=8 * 10**9, bytes_accessed=2 * 10**6, transcendentals=0),
        name="exact_part",
    )(order, offsets, cols, rows, band_window.reshape(1, M), facets, window, jnp.asarray(tables["sample"]),
      jnp.asarray(tables["join_hi"]), jnp.asarray(tables["join_lo"]))

    send = pl.pallas_call(
        _residual_kernel,
        in_specs=[hbm, anywhere] + [hbm] * 10,
        out_shape=shape((128 * CHUNKS, 128), f32),
        scratch_shapes=[
            pltpu.VMEM((1, 2, 4, 16384), f32), pltpu.VMEM((1, 2, 4, 16384), f32), pltpu.VMEM((1, 16384), f32),
            pltpu.VMEM((64, 1024), bf16), pltpu.VMEM((64, 1024), bf16), pltpu.VMEM((64, 128), f32),
            pltpu.VMEM((64, 128), f32), pltpu.VMEM((256, 16), bf16),
            pltpu.VMEM((1024, 1024), f8), pltpu.VMEM((16, 512), f32), pltpu.VMEM((16, 512), f32),
            pltpu.VMEM((64, 128 * (CHUNKS - 16)), f32),
            pltpu.VMEM((512, 1024), f8), pltpu.VMEM((512, 1024), f8), pltpu.VMEM((2, 128, 512), f32),
            pltpu.SemaphoreType.DMA((12,)),
        ],
        compiler_params=params(60),
        cost_estimate=pl.CostEstimate(flops=9 * 10**9, bytes_accessed=4 * 10**6, transcendentals=0),
        name="residual_part",
    )(
        facets, peer, window, lc, ls, mc, ms, combine, jnp.asarray(tables["resid"]), jnp.asarray(tables["turn_c"]),
        jnp.asarray(tables["turn_s"]), nodes,
    )

    got = lax.all_to_all(send.reshape(128, CHUNKS // 4, 4, 128), ("facet", "rows"), split_axis=0, concat_axis=0, tiled=True)
    phases = pl.pallas_call(
        _phase_kernel,
        in_specs=[vmem] * 3,
        out_shape=shape((1024, 1024), bf16),
        scratch_shapes=[pltpu.VMEM((2, 1024, 512), bf16), pltpu.VMEM((2, 1024, 512), bf16)],
        compiler_params=params(60),
        cost_estimate=pl.CostEstimate(flops=3 * 10**9, bytes_accessed=2 * 10**6, transcendentals=2 * 10**5),
        name="row_phases",
    )(order, offsets, rows)

    return pl.pallas_call(
        _rows_kernel,
        in_specs=[vmem] + [hbm] * 4 + [anywhere],
        out_specs=hbm,
        out_shape=shape((1, 2, 512, 1024), f32),
        scratch_shapes=[
            pltpu.VMEM((256, 1024), bf16), pltpu.VMEM((256, 1024), bf16),
            pltpu.VMEM((64, 1024), f32), pltpu.VMEM((64, 1024), f32), pltpu.VMEM((512, 1024), bf16),
            pltpu.VMEM((512, 1024), bf16), pltpu.VMEM((1024, 2048), bf16), pltpu.VMEM((512, 1024), f32),
            pltpu.VMEM((2, 256, 256), bf16), pltpu.VMEM((2, 128, 256), bf16), pltpu.VMEM((2, 512, 1024), f32),
            pltpu.SemaphoreType.DMA((7,)), pltpu.SemaphoreType.DMA((8,)),
        ],
        compiler_params=params(50),
        cost_estimate=pl.CostEstimate(flops=5 * 10**9, bytes_accessed=12 * 10**6, transcendentals=0),
        name="row_transform",
    )(got.reshape(128 * CHUNKS, 128), jnp.asarray(tables["weave_hi"]), jnp.asarray(tables["weave_lo"]), pc, ps, phases)


def solution(mesh):
    return jax.shard_map(
        per_device,
        mesh=mesh,
        in_specs=(P("facet", None, "rows", None), P(), P(), P(), P(), P(), P()),
        out_specs=P("facet", None, "rows", None),
        check_vma=False,
    )
```

```python
import functools
import math

import jax
import jax.numpy as jnp
import ml_dtypes
import numpy as np
from jax import lax
from jax.experimental import pallas as pl
from jax.experimental.pallas import tpu as pltpu
from jax.sharding import PartitionSpec as P

NIMG = 262144
M = 1024
SUBROWS = 1024
TWO_PI = 2.0 * math.pi

BLOCK = 1024
SPAN = 4096
NODES = 32
WIDTH = 16384
ALL_NODES = 85
RANK = 4
OWN_RANK = 3
ERANK = 2
ROW_SCALE = 4.0
TABLE_SCALE = 32768.0
DATA_SCALE = 16.0

f32 = jnp.float32
bf16 = jnp.bfloat16
f8 = jnp.float8_e4m3fn


def _split(values):
    high = values.astype(np.float32).astype(ml_dtypes.bfloat16)
    low = (values - high.astype(np.float64)).astype(np.float32).astype(ml_dtypes.bfloat16)
    return high, low


def _kernel_sum(x, count):
    den = np.sin(np.pi * x / NIMG)
    zero = np.abs(den) < 1e-14
    return np.where(zero, float(count), np.sin(np.pi * x * count / NIMG) / np.where(zero, 1.0, den))


def _solve(gram, right):
    gram, right = gram.copy(), right.copy()
    n = len(gram)
    for i in range(n):
        for j in range(i + 1, n):
            factor = gram[j, i] / gram[i, i]
            gram[j] = gram[j] - factor * gram[i]
            right[j] = right[j] - factor * right[i]
    out = np.zeros_like(right)
    for i in range(n - 1, -1, -1):
        total = right[i].copy()
        for j in range(i + 1, n):
            total = total - gram[i, j] * out[j]
        out[i] = total / gram[i, i]
    return out


@functools.lru_cache(maxsize=None)
def _tables():
    scale = TWO_PI / NIMG
    bands = np.arange(M)
    product = (np.arange(BLOCK)[:, None] * bands[None, :]) % NIMG
    angle = (np.float32(scale) * product.astype(np.float32)).astype(np.float64)
    exact = scale * product
    resid_c = np.cos(angle).astype(np.float32).astype(ml_dtypes.bfloat16).astype(np.float64) - np.cos(exact)
    resid_s = np.sin(angle).astype(np.float32).astype(ml_dtypes.bfloat16).astype(np.float64) - np.sin(exact)
    half = M // 2
    resid = np.stack(
        [np.concatenate([resid_c[:, h * half:(h + 1) * half], resid_s[:, h * half:(h + 1) * half]], 1) for h in range(2)]
    )
    resid = (resid * TABLE_SCALE).astype(np.float32).astype(ml_dtypes.float8_e4m3fn)
    def spread(count, width, even):
        i = np.arange(count)
        return 511.5 + 512 * width * (even * ((2 * i + 1) / count - 1) - (1 - even) * np.cos(np.pi * (i + 0.5) / count))

    def interpolate(nodes, targets, columns):
        gram = _kernel_sum(nodes[:, None] - nodes[None, :], columns) + 1e-13 * columns * np.eye(len(nodes))
        return _solve(gram, _kernel_sum(nodes[:, None] - targets[None, :], columns))

    nodes, all_nodes = spread(NODES, 1.05, 0.25), spread(ALL_NODES, 1.04, 0.6)
    centre = (SPAN - 1) / 2
    at = scale * (np.arange(SPAN) - centre)[:, None] * nodes[None, :]
    sample = np.concatenate([np.cos(at), -np.sin(at)], 1)
    sample = np.concatenate(_split(sample), 1)
    middle = (WIDTH - 1) / 2
    interp = interpolate(nodes, all_nodes, SPAN)
    rows = []
    for span in range(WIDTH // SPAN):
        turn = scale * (span * SPAN + centre - middle) * all_nodes
        re, im = interp * np.cos(turn), -interp * np.sin(turn)
        rows += [np.concatenate([re, im], 1), np.concatenate([-im, re], 1)]
    joined = np.concatenate(rows, 0)
    join = np.zeros((OWN_RANK * 256, 512))
    for n in range(OWN_RANK):
        join[n * 256:(n + 1) * 256, n * 2 * ALL_NODES:(n + 1) * 2 * ALL_NODES] = joined
    join_hi, join_lo = _split(join)
    interp = interpolate(all_nodes, bands.astype(np.float64), WIDTH)
    turn = scale * middle * bands
    weave = np.zeros((256, M))
    weave[:2 * ALL_NODES] = np.concatenate([interp * np.cos(turn), interp * np.sin(turn)], 0)
    weave_hi, weave_lo = _split(weave)
    turn = TWO_PI * ((np.arange(16)[:, None] * (bands[None, :half] % 256)) % 256) / 256
    return dict(
        resid=resid, sample=sample, join_hi=join_hi, join_lo=join_lo, weave_hi=weave_hi, weave_lo=weave_lo,
        turn_c=np.cos(turn).astype(np.float32), turn_s=np.sin(turn).astype(np.float32),
    )


COL_A, COL_SC8, COL_CF8, COL_ROW = 0, 16, 24, 32
PACK = ((0, 1024), (1024, 2048), (2048, 2176), (2176, 2304), (2304, 2816))
CHUNKS = 20


def _angle(product):
    turns = lax.bitwise_and(product + NIMG, 2 * NIMG - 1) - NIMG
    return turns.astype(f32) * (math.pi / NIMG)


def _offset_row(order_ref, offsets_ref, which):
    slots = lax.broadcasted_iota(jnp.int32, (64, 64), 0)
    offsets = _to_column(offsets_ref[which:which + 1, :].astype(f32))
    return jnp.sum(jnp.where(slots == order_ref[...], offsets, 0.0), axis=0, keepdims=True)


def _to_column(row):
    at = lax.broadcasted_iota(jnp.int32, (64, 64), 0) == lax.broadcasted_iota(jnp.int32, (64, 64), 1)
    return jnp.sum(jnp.where(at, row, 0.0), axis=1, keepdims=True)


def _pick(row, index):
    lane = lax.broadcasted_iota(jnp.int32, row.shape, 1)
    return jnp.sum(jnp.where(lane == index, row, 0.0), axis=1, keepdims=True)


def _prepare(slot, half, order_ref, offsets_ref, cols_ref, rows_ref, band_ref,
             lc_ref, ls_ref, pc_ref, ps_ref, mc_ref, ms_ref):
    cf_row = _offset_row(order_ref, offsets_ref, 0)
    own_cf = _pick(cf_row, slot).astype(jnp.int32)
    cf = _to_column(cf_row).astype(jnp.int32)
    sc = _to_column(cols_ref[...].astype(f32)).astype(jnp.int32)
    sr = _to_column(rows_ref[...].astype(f32)).astype(jnp.int32)
    lane = lax.broadcasted_iota(jnp.int32, (64, 128), 1)
    row = lax.bitwise_and(4 * half + 4 * lax.bitwise_and(lane // 8, 1) + lax.bitwise_and(lane, 3), 7)
    odd = 2 * row - 7
    factor = jnp.where(
        lane < COL_SC8, 2 * (own_cf + 1024 * lane),
        jnp.where(lane < COL_CF8, 256 * (lane - COL_SC8), jnp.where(lane < COL_ROW, 256 * (lane - COL_CF8), odd)),
    )
    other = jnp.where(lane < COL_CF8, sc, jnp.where(lane < COL_ROW, cf, sr + 512))
    angle = _angle(factor * other)
    mc, ms = jnp.cos(angle), jnp.sin(angle)
    mc_ref[...] = mc
    ms_ref[...] = ms
    angle = _angle(2 * lane * sc)
    low_c, low_s = jnp.cos(angle), jnp.sin(angle)
    for i in range(8):
        c, s = mc[:, COL_SC8 + i:COL_SC8 + i + 1], ms[:, COL_SC8 + i:COL_SC8 + i + 1]
        lc_ref[:, i * 128:(i + 1) * 128] = c * low_c - s * low_s
        ls_ref[:, i * 128:(i + 1) * 128] = s * low_c + c * low_s
    angle = _angle(2 * lane * cf)
    low_c, low_s = jnp.cos(angle), jnp.sin(angle)
    for i in range(8):
        c, s = mc[:, COL_CF8 + i:COL_CF8 + i + 1], ms[:, COL_CF8 + i:COL_CF8 + i + 1]
        band = band_ref[:, i * 128:(i + 1) * 128]
        pc_ref[:, i * 128:(i + 1) * 128] = (c * low_c - s * low_s) * band
        ps_ref[:, i * 128:(i + 1) * 128] = (s * low_c + c * low_s) * band


def _combine(mc, ms, combine_ref):
    lane = lax.broadcasted_iota(jnp.int32, (64, 128), 1)
    row = 4 * lax.axis_index("rows") + 4 * lax.bitwise_and(lane // 8, 1) + lax.bitwise_and(lane, 3)
    place = (2 * lax.bitwise_and(row, 7) - 7).astype(f32) * (0.5 / ROW_SCALE)
    first = lax.bitwise_and(lane, 4) == 0
    to_re, to_im = jnp.where(first, mc, ms), jnp.where(first, -ms, mc)
    for n in range(ERANK):
        for part, value in ((0, to_re), (1, to_im)):
            base = part * 128 + n * 64
            combine_ref[base:base + 64, :] = (value * place if n else value)[:, COL_ROW:COL_ROW + 16].astype(bf16)


def _exact_kernel(order_hbm, offsets_hbm, cols_hbm, rows_hbm, band_hbm, data_hbm, window_hbm, sample_hbm, jh_hbm, jl_hbm,
                  pc_hbm, ps_hbm, pack_hbm,
                  order_ref, offsets_ref, cols_ref, rows_ref, band_ref, data_ref, window_ref, sample_ref, jh_ref, jl_ref,
                  pc_ref, ps_ref, out_ref, even_ref, odd_ref, acc_ref, terms_ref, sems, out_sems):
    loads = [
        pltpu.make_async_copy(source, target, sems.at[i])
        for i, (source, target) in enumerate((
            (order_hbm, order_ref), (offsets_hbm, offsets_ref), (cols_hbm, cols_ref), (rows_hbm, rows_ref),
            (band_hbm, band_ref), (data_hbm, data_ref), (window_hbm, window_ref), (sample_hbm, sample_ref),
            (jh_hbm, jh_ref), (jl_hbm, jl_ref),
        ))
    ]
    for load in loads:
        load.start()
    for load in loads[:5]:
        load.wait()
    acc_ref[...] = jnp.zeros_like(acc_ref)
    lc_ref, ls_ref, mc_ref, ms_ref, nodes_ref = (out_ref.at[:, a:b] for a, b in PACK)
    _prepare(lax.axis_index("facet"), lax.axis_index("rows"), order_ref, offsets_ref, cols_ref, rows_ref, band_ref,
             lc_ref, ls_ref, pc_ref, ps_ref, mc_ref, ms_ref)
    stores = [
        pltpu.make_async_copy(source, target, out_sems.at[i])
        for i, (source, target) in enumerate((
            (pc_ref, pc_hbm), (ps_ref, ps_hbm),
            (out_ref.at[:, 0:PACK[-1][0]], pack_hbm.at[:, 0:PACK[-1][0]]),
        ))
    ]
    for store in stores:
        store.start()
    for load in loads[5:8]:
        load.wait()

    def build(block, x_ref, bc, bs, i):
        cols = slice(i * 256, (i + 1) * 256)
        here = pl.ds(pl.multiple_of(block * BLOCK + i * 256, 256), 256)
        window = window_ref[:, here]
        re_rows = data_ref[0, 0, :, here] * window
        im_rows = data_ref[0, 1, :, here] * window
        for g in range(4):
            rows = slice(g * 16, (g + 1) * 16)
            lc, ls = lc_ref[rows, cols], ls_ref[rows, cols]
            c, s = bc[rows], bs[rows]
            ec = c * lc - s * ls
            es = s * lc + c * ls
            for r in range(4):
                dr, di = re_rows[r:r + 1], im_rows[r:r + 1]
                at = r * 64 + g * 16
                x_ref[at:at + 16, cols] = (dr * ec + di * es).astype(bf16)
                x_ref[256 + at:256 + at + 16, cols] = (di * ec - dr * es).astype(bf16)

    def turns(block):
        return _pick(mc_ref[...], block), _pick(ms_ref[...], block)

    def stage(block, x_ref, following, next_ref):
        bc, bs = turns(following)
        span = block // 4
        for i in range(4):
            rows = pl.ds(pl.multiple_of(lax.rem(block, 4) * BLOCK + i * 256, 256), 256)
            part = jnp.dot(x_ref[:, i * 256:(i + 1) * 256], sample_ref[rows, :], preferred_element_type=f32)
            build(following, next_ref, bc, bs, i)
            acc_ref[span] = acc_ref[span] + part

    bc, bs = turns(0)
    for i in range(4):
        build(0, even_ref, bc, bs, i)

    def body(pair, carry):
        stage(2 * pair, even_ref, 2 * pair + 1, odd_ref)
        stage(2 * pair + 1, odd_ref, lax.rem(2 * pair + 2, 16), even_ref)
        return carry

    lax.fori_loop(0, 8, body, 0)

    first = lax.broadcasted_iota(jnp.int32, (64, 128), 1) < 64
    lane = lax.broadcasted_iota(jnp.int32, (64, 128), 1)
    sign = jnp.where(lax.bitwise_and(lane, 32) == 0, -1.0, 1.0).astype(f32)
    places = [(r - 1.5) / ROW_SCALE for r in range(4)]
    spins = [
        [jnp.broadcast_to(ref[:, COL_ROW + r:COL_ROW + r + 1], (64, 128)) for ref in (mc_ref, ms_ref)] for r in range(4)
    ]
    for pair in range(2):
        sums = []
        for span in (2 * pair, 2 * pair + 1):
            direct, across = [None] * OWN_RANK, [None] * OWN_RANK
            for r in range(4):
                c, s = spins[r]
                re = acc_ref[span, r * 64:(r + 1) * 64]
                im = acc_ref[span, 256 + r * 64:256 + (r + 1) * 64]
                one, two = c * re + s * im, c * im - s * re
                for n in range(OWN_RANK):
                    direct[n] = one if r == 0 else direct[n] + one
                    across[n] = two if r == 0 else across[n] + two
                    one, two = one * places[r], two * places[r]
            sums.append((direct, across))
        for n in range(OWN_RANK):
            folded = []
            for which in range(2):
                a, b = sums[0][which][n], sums[1][which][n]
                folded.append(jnp.where(first, a, b) + pltpu.roll(jnp.where(first, b, a), 64, 1))
            at = n * 256 + pair * 128
            terms_ref[:, at:at + 128] = folded[0] + jnp.where(
                sign < 0, -pltpu.roll(folded[1], 96, 1), pltpu.roll(folded[1], 32, 1))
    for load in loads[8:]:
        load.wait()
    high, low = _halves(terms_ref[...])
    nodes_ref[...] = (
        jnp.dot(high, jh_ref[...], preferred_element_type=f32)
        + (jnp.dot(high, jl_ref[...], preferred_element_type=f32) + jnp.dot(low, jh_ref[...], preferred_element_type=f32))
    )
    last = pltpu.make_async_copy(nodes_ref, pack_hbm.at[:, PACK[-1][0]:PACK[-1][1]], out_sems.at[3])
    last.start()
    for store in stores:
        store.wait()
    last.wait()


def _residual_kernel(own_hbm, peer_ref, window_hbm, pack_ref, table_hbm, tc_hbm, ts_hbm, out_ref,
                     own_ref, window_ref, lc_ref, ls_ref, combine_ref, table_ref, tc_ref, ts_ref, even_ref, odd_ref, sum_ref, sems):
    loads = [
        pltpu.make_async_copy(source, target, sems.at[i])
        for i, (source, target) in enumerate((
            (own_hbm, own_ref), (window_hbm, window_ref),
            (table_hbm.at[lax.axis_index("rows")], table_ref), (tc_hbm, tc_ref), (ts_hbm, ts_ref),
        ))
    ]
    for load in loads:
        load.start()
    sum_ref[...] = jnp.zeros_like(sum_ref)
    mc_ref, ms_ref, nodes_ref = (pack_ref.at[:, a:b] for a, b in PACK[2:])
    lc_ref[...] = pack_ref[:, PACK[0][0]:PACK[0][1]].astype(bf16)
    ls_ref[...] = pack_ref[:, PACK[1][0]:PACK[1][1]].astype(bf16)
    _combine(mc_ref[...], ms_ref[...], combine_ref)
    for load in loads[:2]:
        load.wait()
    largest = jnp.zeros((4, 2048), f32)
    for i in range(8):
        here = slice(i * 2048, (i + 1) * 2048)
        window = window_ref[:, here]
        for ref in (own_ref, peer_ref):
            for part in range(2):
                largest = jnp.maximum(largest, jnp.abs(ref[0, part, :, here] * window))
    largest = jnp.maximum(jnp.max(jnp.max(largest, axis=1, keepdims=True), axis=0, keepdims=True), 1e-30)
    scale_in = DATA_SCALE / largest
    scale_out = largest * (1.0 / (DATA_SCALE * TABLE_SCALE))

    def mix(block, i):
        here = pl.ds(pl.multiple_of(block * BLOCK + i * 256, 256), 256)
        window = window_ref[:, here] * scale_in
        data = jnp.concatenate(
            [own_ref[0, 0, :, here], own_ref[0, 1, :, here], peer_ref[0, 0, :, here], peer_ref[0, 1, :, here]], 0
        )
        return jnp.dot(combine_ref[...], (data * window).astype(bf16), preferred_element_type=f32)

    def build(z_ref, j, i, rows, bc, bs):
        cols = slice(i * 256, (i + 1) * 256)
        lc, ls = lc_ref[:, cols], ls_ref[:, cols]
        ec = bc * lc - bs * ls
        es = bs * lc + bc * ls
        rows = rows.astype(bf16)
        for n in range(ERANK):
            gr, gi = rows[n * 64:(n + 1) * 64], rows[128 + n * 64:128 + (n + 1) * 64]
            at = j * 256 + n * 64
            z_ref[at:at + 64, cols] = (gr * ec + gi * es).astype(z_ref.dtype)
            z_ref[at + 128:at + 192, cols] = (gi * ec - gr * es).astype(z_ref.dtype)

    def turns(block):
        return tuple(
            jnp.broadcast_to(_pick(ref[...], block), (64, 256)).astype(bf16) for ref in (mc_ref, ms_ref)
        )

    def stage(group, z_ref, following, next_ref):
        tasks = [(j, i) for j in range(2) for i in range(4)]
        building = following is not None
        if building:
            spins = [turns(following * 2 + j) for j in range(2)]
            ready = mix(following * 2, 0)
        at = 0
        for j in range(2):
            for kc in range(2):
                cols = slice(kc * 256, (kc + 1) * 256)
                z = z_ref[j * 256:(j + 1) * 256, :]
                by_c = jnp.dot(z, table_ref[:, cols], preferred_element_type=f32)
                by_s = jnp.dot(z, table_ref[:, 512 + kc * 256:768 + kc * 256], preferred_element_type=f32)
                for _ in range(2 if building else 0):
                    bj, bi = tasks[at]
                    at += 1
                    coming = mix(following * 2 + tasks[at][0], tasks[at][1]) if at < 8 else None
                    build(next_ref, bj, bi, ready, *spins[bj])
                    ready = coming
                re = by_c[0:128] + by_s[128:256]
                im = by_c[128:256] - by_s[0:128]
                tc = tc_ref[pl.ds(group * 2 + j, 1), cols]
                ts = ts_ref[pl.ds(group * 2 + j, 1), cols]
                sum_ref[0, :, cols] = sum_ref[0, :, cols] + (re * tc + im * ts)
                sum_ref[1, :, cols] = sum_ref[1, :, cols] + (im * tc - re * ts)

    for j in range(2):
        spin = turns(j)
        for i in range(4):
            build(even_ref, j, i, mix(j, i), *spin)
    for load in loads[2:]:
        load.wait()

    def body(pair, carry):
        stage(2 * pair, even_ref, 2 * pair + 1, odd_ref)
        stage(2 * pair + 1, odd_ref, 2 * pair + 2, even_ref)
        return carry

    lax.fori_loop(0, 3, body, 0)
    stage(6, even_ref, 7, odd_ref)
    stage(7, odd_ref, None, None)

    for copy in range(2):
        for i in range(CHUNKS - 16):
            out_ref[pl.ds(copy * CHUNKS + 16 + i, 64, stride=2 * CHUNKS), :] = nodes_ref[:, i * 128:(i + 1) * 128]
        for n in range(ERANK):
            for part in range(2):
                for kc in range(4):
                    at = copy * CHUNKS + n * 8 + part * 4 + kc
                    out_ref[pl.ds(at, 64, stride=2 * CHUNKS), :] = (
                        sum_ref[part, n * 64:(n + 1) * 64, kc * 128:(kc + 1) * 128] * scale_out
                    )


def _halves(value):
    high = value.astype(bf16)
    return high, (value - high.astype(f32)).astype(bf16)


def _phase_kernel(order_ref, offsets_ref, rows_ref, out_ref, all_ref, turned_ref):
    left_ref, gram_ref = out_ref.at[0:512], out_ref.at[512:1024]
    slot, half = lax.axis_index("facet"), lax.axis_index("rows")
    rf = _offset_row(order_ref, offsets_ref, 1).astype(jnp.int32)
    own_sr = _pick(rows_ref[...].astype(f32), slot).astype(jnp.int32)
    odd = jnp.concatenate([2 * rf + 7, 2 * rf + 7], 1)
    lane = lax.broadcasted_iota(jnp.int32, (128, 128), 1)
    quarter = jnp.where(lane < 64, 0, -(NIMG // 2))
    sign = jnp.where(lane < 64, -1.0, 1.0).astype(f32)
    for i in range(8):
        here = slice(i * 128, (i + 1) * 128)
        q = lax.broadcasted_iota(jnp.int32, (128, 128), 0) + i * 128 + half * 512
        q = lax.bitwise_and(q, 1023)
        turn = jnp.cos(_angle(odd * (own_sr + q) + quarter))
        other = sign * pltpu.roll(turn, 64, 1)
        g = (q - 512).astype(f32) * (TWO_PI / NIMG * ROW_SCALE)
        g2, g3 = g * g * 0.5, g * g * g * (1.0 / 6.0)
        for n, value in enumerate((turn, g * other, -g2 * turn, -g3 * other)):
            high, low = _halves(value)
            cols = slice(n * 128, (n + 1) * 128)
            all_ref[0, here, cols] = high
            all_ref[1, here, cols] = low
            high_t, low_t = _halves(sign * pltpu.roll(value, 64, 1))
            turned_ref[0, here, cols] = high_t
            turned_ref[1, here, cols] = low_t
            if i < 4 and n < 2:
                left_ref[here, n * 128:(n + 1) * 128] = high
                left_ref[here, 256 + n * 128:256 + (n + 1) * 128] = high
                left_ref[here, 512 + n * 128:512 + (n + 1) * 128] = low
            elif i < 4:
                left_ref[here, 512 + n * 128:512 + (n + 1) * 128] = high
    over_rows = (((0,), (0,)), ((), ()))
    gram = None
    for ref in (all_ref, turned_ref):
        for a, b in ((0, 0), (0, 1), (1, 0)):
            part = lax.dot_general(ref[a], ref[b], over_rows, preferred_element_type=f32)
            gram = part if gram is None else gram + part
    high, low = _halves(gram)
    gram_ref[:, 0:256] = high[:, 0:256]
    gram_ref[:, 256:512] = high[:, 0:256]
    gram_ref[:, 512:768] = low[:, 0:256]
    gram_ref[:, 768:1024] = high[:, 256:512]


def _rows_kernel(got_ref, wh_hbm, wl_hbm, pc_hbm, ps_hbm, phases_any, out_hbm,
                 wh_ref, wl_ref, pc_ref, ps_ref, gram_ref, left_ref, right_ref, value_ref, high_ref, low_ref,
                 out_ref, sems, out_sems):
    loads = [
        pltpu.make_async_copy(source, target, sems.at[i])
        for i, (source, target) in enumerate((
            (wh_hbm, wh_ref), (wl_hbm, wl_ref), (pc_hbm, pc_ref), (ps_hbm, ps_ref),
            (phases_any.at[512:1024], gram_ref), (phases_any.at[0:512], left_ref),
        ))
    ]
    for load in loads:
        load.start()
    parts = [
        jnp.concatenate([got_ref[pl.ds(h * CHUNKS + 16 + i, 64, stride=2 * CHUNKS), :] for i in range(4)], 1)
        for h in range(2)
    ]
    both, between = parts[0] + parts[1], parts[1] - parts[0]
    sums, diffs = [
        [(pltpu.roll(v, 512 - n * 2 * ALL_NODES, 1) if n else v)[:, 0:256] for n in range(OWN_RANK)]
        for v in (both, between)
    ]
    d = 2.0 / ROW_SCALE
    cube = 2.05 / (ROW_SCALE * ROW_SCALE)
    terms = (
        sums[0],
        sums[1] + d * diffs[0],
        sums[2] + (2 * d) * diffs[1] + (d * d) * sums[0],
        (cube + 3 * d * d) * sums[1] + (3 * d) * diffs[2] + (d * d * d) * diffs[0],
    )
    lane = lax.broadcasted_iota(jnp.int32, (64, 256), 1)
    for n, value in enumerate(terms):
        rows = slice(n * 64, (n + 1) * 64)
        value = jnp.where(lane < 2 * ALL_NODES, value, 0.0)
        for part in range(2):
            high, low = _halves(value)
            high_ref[part, rows, :] = high
            if n < 2:
                low_ref[part, rows, :] = low
            value = jnp.where(
                lane < ALL_NODES, pltpu.roll(value, 256 - ALL_NODES, 1), -pltpu.roll(value, ALL_NODES, 1))
    for load in loads[0:4]:
        load.wait()
    for i in range(4):
        cols = slice(i * 256, (i + 1) * 256)
        vals = []
        for part in range(2):
            wh, wl = wh_ref[:, cols], wl_ref[:, cols]
            main = jnp.dot(high_ref[part], wh, preferred_element_type=f32)
            rest = (
                jnp.dot(high_ref[part, 0:128], wl, preferred_element_type=f32)
                + jnp.dot(low_ref[part], wh, preferred_element_type=f32)
            )
            vals.append((main, rest))
        pc, ps = pc_ref[:, cols], ps_ref[:, cols]
        for n in range(RANK):
            rows = slice(n * 64, (n + 1) * 64)
            vr, vi = vals[0][0][rows], vals[1][0][rows]
            if n < ERANK:
                parts = []
                for part in range(2):
                    at = (i // 2) * CHUNKS + n * 8 + part * 4 + 2 * (i % 2)
                    parts.append(jnp.concatenate(
                        [got_ref[pl.ds(at + m, 64, stride=2 * CHUNKS), :] for m in range(2)], 1))
                vr = vr + vals[0][1][rows] + parts[0]
                vi = vi + vals[1][1][rows] + parts[1]
            cr = vr * pc + vi * ps
            ci = vi * pc - vr * ps
            at = n * 128
            value_ref[at:at + 64, cols] = cr
            value_ref[at + 64:at + 128, cols] = ci
            turned = slice(1024 + i * 256, 1024 + (i + 1) * 256)
            cr_high, ci_high = cr.astype(bf16), ci.astype(bf16)
            bases = (0, 512) if n < 2 else (512,)
            for base in bases:
                right_ref[base + at:base + at + 64, cols] = cr_high
                right_ref[base + at + 64:base + at + 128, cols] = ci_high
                right_ref[base + at:base + at + 64, turned] = ci_high
                right_ref[base + at + 64:base + at + 128, turned] = -cr_high
            if n < 2:
                cr_low = (cr - cr_high.astype(f32)).astype(bf16)
                ci_low = (ci - ci_high.astype(f32)).astype(bf16)
                right_ref[256 + at:256 + at + 64, cols] = cr_low
                right_ref[256 + at + 64:256 + at + 128, cols] = ci_low
                right_ref[256 + at:256 + at + 64, turned] = ci_low
                right_ref[256 + at + 64:256 + at + 128, turned] = -cr_low

    loads[4].wait()
    total = jnp.zeros((8, 256), f32)
    for i in range(4):
        cols = slice(i * 256, (i + 1) * 256)
        product = jnp.dot(gram_ref[...], right_ref[:, cols], preferred_element_type=f32) * value_ref[:, cols]
        total = total + jnp.sum(product.reshape(64, 8, 256), 0)
    mean = jnp.maximum(jnp.sum(total), 0.0) / (2.0 * SUBROWS * M)
    factor = lax.rsqrt(jnp.full((8, 128), mean, f32) + 1e-06)[0:1, 0:1]

    loads[5].wait()
    stores = []
    for part in range(2):
        for i in range(4):
            cols = slice(i * 256, (i + 1) * 256)
            right = right_ref[:, part * 1024 + i * 256:part * 1024 + (i + 1) * 256]
            out_ref[part, :, cols] = jnp.dot(left_ref[...], right, preferred_element_type=f32) * factor
            store = pltpu.make_async_copy(
                out_ref.at[part, :, cols], out_hbm.at[0, part, :, cols], out_sems.at[part * 4 + i])
            store.start()
            stores.append(store)
    for store in stores:
        store.wait()


def per_device(facets, facet_window, band_window, facet_order, facet_offsets, sub_cols, sub_rows):
    tables = _tables()
    peer = lax.ppermute(facets, "rows", [(0, 1), (1, 0)])
    order, cols, rows = (v.reshape(1, 64) for v in (facet_order, sub_cols, sub_rows))
    offsets = facet_offsets.T
    window = facet_window.reshape(1, 16384)
    hbm = pl.BlockSpec(memory_space=pltpu.HBM)
    anywhere = pl.BlockSpec(memory_space=pl.ANY)
    vmem = pl.BlockSpec(memory_space=pltpu.VMEM)
    shape = jax.ShapeDtypeStruct

    def params(mib):
        return pltpu.CompilerParams(vmem_limit_bytes=mib * 1024 * 1024)

    wide = shape((64, 1024), f32)
    pc, ps, pack = pl.pallas_call(
        _exact_kernel,
        in_specs=[hbm] * 10,
        out_specs=[hbm] * 3,
        out_shape=[wide, wide, shape((64, PACK[-1][1]), f32)],
        scratch_shapes=[
            pltpu.VMEM((1, 64), jnp.int32), pltpu.VMEM((2, 64), jnp.int32), pltpu.VMEM((1, 64), jnp.int32),
            pltpu.VMEM((1, 64), jnp.int32), pltpu.VMEM((1, M), f32), pltpu.VMEM((1, 2, 4, 16384), f32),
            pltpu.VMEM((1, 16384), f32), pltpu.VMEM((SPAN, 128), bf16),
            pltpu.VMEM((OWN_RANK * 256, 512), bf16), pltpu.VMEM((OWN_RANK * 256, 512), bf16),
            pltpu.VMEM((64, 1024), f32), pltpu.VMEM((64, 1024), f32), pltpu.VMEM((64, PACK[-1][1]), f32),
            pltpu.VMEM((512, BLOCK), bf16), pltpu.VMEM((512, BLOCK), bf16), pltpu.VMEM((4, 512, 128), f32),
            pltpu.VMEM((64, OWN_RANK * 256), f32),
            pltpu.SemaphoreType.DMA((10,)), pltpu.SemaphoreType.DMA((4,)),
        ],
        compiler_params=params(60),
        cost_estimate=pl.CostEstimate(flops=8 * 10**9, bytes_accessed=2 * 10**6, transcendentals=0),
        name="exact_part",
    )(order, offsets, cols, rows, band_window.reshape(1, M), facets, window, jnp.asarray(tables["sample"]),
      jnp.asarray(tables["join_hi"]), jnp.asarray(tables["join_lo"]))

    send = pl.pallas_call(
        _residual_kernel,
        in_specs=[hbm, vmem, hbm, vmem] + [hbm] * 3,
        out_shape=shape((128 * CHUNKS, 128), f32),
        scratch_shapes=[
            pltpu.VMEM((1, 2, 4, 16384), f32), pltpu.VMEM((1, 16384), f32),
            pltpu.VMEM((64, 1024), bf16), pltpu.VMEM((64, 1024), bf16), pltpu.VMEM((256, 16), bf16),
            pltpu.VMEM((1024, 1024), f8), pltpu.VMEM((16, 512), f32), pltpu.VMEM((16, 512), f32),
            pltpu.VMEM((512, 1024), f8), pltpu.VMEM((512, 1024), f8), pltpu.VMEM((2, 128, 512), f32),
            pltpu.SemaphoreType.DMA((5,)),
        ],
        compiler_params=params(44),
        cost_estimate=pl.CostEstimate(flops=9 * 10**9, bytes_accessed=4 * 10**6, transcendentals=0),
        name="residual_part",
    )(
        facets, peer, window, pack, jnp.asarray(tables["resid"]), jnp.asarray(tables["turn_c"]),
        jnp.asarray(tables["turn_s"]),
    )

    got = lax.all_to_all(send.reshape(128, CHUNKS // 4, 4, 128), ("facet", "rows"), split_axis=0, concat_axis=0, tiled=True)
    phases = pl.pallas_call(
        _phase_kernel,
        in_specs=[vmem] * 3,
        out_shape=shape((1024, 1024), bf16),
        scratch_shapes=[pltpu.VMEM((2, 1024, 512), bf16), pltpu.VMEM((2, 1024, 512), bf16)],
        compiler_params=params(60),
        cost_estimate=pl.CostEstimate(flops=3 * 10**9, bytes_accessed=2 * 10**6, transcendentals=2 * 10**5),
        name="row_phases",
    )(order, offsets, rows)

    return pl.pallas_call(
        _rows_kernel,
        in_specs=[vmem] + [hbm] * 4 + [anywhere],
        out_specs=hbm,
        out_shape=shape((1, 2, 512, 1024), f32),
        scratch_shapes=[
            pltpu.VMEM((256, 1024), bf16), pltpu.VMEM((256, 1024), bf16),
            pltpu.VMEM((64, 1024), f32), pltpu.VMEM((64, 1024), f32), pltpu.VMEM((512, 1024), bf16),
            pltpu.VMEM((512, 1024), bf16), pltpu.VMEM((1024, 2048), bf16), pltpu.VMEM((512, 1024), f32),
            pltpu.VMEM((2, 256, 256), bf16), pltpu.VMEM((2, 128, 256), bf16), pltpu.VMEM((2, 512, 1024), f32),
            pltpu.SemaphoreType.DMA((7,)), pltpu.SemaphoreType.DMA((8,)),
        ],
        compiler_params=params(50),
        cost_estimate=pl.CostEstimate(flops=5 * 10**9, bytes_accessed=12 * 10**6, transcendentals=0),
        name="row_transform",
    )(got.reshape(128 * CHUNKS, 128), jnp.asarray(tables["weave_hi"]), jnp.asarray(tables["weave_lo"]), pc, ps, phases)


def solution(mesh):
    return jax.shard_map(
        per_device,
        mesh=mesh,
        in_specs=(P("facet", None, "rows", None), P(), P(), P(), P(), P(), P()),
        out_specs=P("facet", None, "rows", None),
        check_vma=False,
    )
```

```python
import functools
import math

import jax
import jax.numpy as jnp
import ml_dtypes
import numpy as np
from jax import lax
from jax.experimental import pallas as pl
from jax.experimental.pallas import tpu as pltpu
from jax.sharding import PartitionSpec as P

NIMG = 262144
M = 1024
SUBROWS = 1024
TWO_PI = 2.0 * math.pi

BLOCK = 1024
SPAN = 4096
NODES = 32
WIDTH = 16384
ALL_NODES = 85
RANK = 4
OWN_RANK = 3
ERANK = 2
ROW_SCALE = 4.0
TABLE_SCALE = 32768.0
DATA_SCALE = 16.0

f32 = jnp.float32
bf16 = jnp.bfloat16
f8 = jnp.float8_e4m3fn


def _split(values):
    high = values.astype(np.float32).astype(ml_dtypes.bfloat16)
    low = (values - high.astype(np.float64)).astype(np.float32).astype(ml_dtypes.bfloat16)
    return high, low


def _kernel_sum(x, count):
    den = np.sin(np.pi * x / NIMG)
    zero = np.abs(den) < 1e-14
    return np.where(zero, float(count), np.sin(np.pi * x * count / NIMG) / np.where(zero, 1.0, den))


def _solve(gram, right):
    gram, right = gram.copy(), right.copy()
    n = len(gram)
    for i in range(n):
        for j in range(i + 1, n):
            factor = gram[j, i] / gram[i, i]
            gram[j] = gram[j] - factor * gram[i]
            right[j] = right[j] - factor * right[i]
    out = np.zeros_like(right)
    for i in range(n - 1, -1, -1):
        total = right[i].copy()
        for j in range(i + 1, n):
            total = total - gram[i, j] * out[j]
        out[i] = total / gram[i, i]
    return out


@functools.lru_cache(maxsize=None)
def _tables():
    scale = TWO_PI / NIMG
    bands = np.arange(M)
    product = (np.arange(BLOCK)[:, None] * bands[None, :]) % NIMG
    angle = (np.float32(scale) * product.astype(np.float32)).astype(np.float64)
    exact = scale * product
    resid_c = np.cos(angle).astype(np.float32).astype(ml_dtypes.bfloat16).astype(np.float64) - np.cos(exact)
    resid_s = np.sin(angle).astype(np.float32).astype(ml_dtypes.bfloat16).astype(np.float64) - np.sin(exact)
    half = M // 2
    resid = np.stack(
        [np.concatenate([v[:, h * half:(h + 1) * half] for v in (resid_c, resid_s - resid_c, resid_s + resid_c)], 1) for h in range(2)]
    )
    resid = (resid * TABLE_SCALE).astype(np.float32).astype(ml_dtypes.float8_e4m3fn)
    def spread(count, width, even):
        i = np.arange(count)
        return 511.5 + 512 * width * (even * ((2 * i + 1) / count - 1) - (1 - even) * np.cos(np.pi * (i + 0.5) / count))

    def interpolate(nodes, targets, columns):
        gram = _kernel_sum(nodes[:, None] - nodes[None, :], columns) + 1e-13 * columns * np.eye(len(nodes))
        return _solve(gram, _kernel_sum(nodes[:, None] - targets[None, :], columns))

    nodes, all_nodes = spread(NODES, 1.05, 0.25), spread(ALL_NODES, 1.04, 0.6)
    centre = (SPAN - 1) / 2
    at = scale * (np.arange(SPAN) - centre)[:, None] * nodes[None, :]
    sample = np.concatenate([np.cos(at), -np.sin(at)], 1)
    sample = np.concatenate(_split(sample), 1)
    middle = (WIDTH - 1) / 2
    interp = interpolate(nodes, all_nodes, SPAN)
    rows = []
    for span in range(WIDTH // SPAN):
        turn = scale * (span * SPAN + centre - middle) * all_nodes
        re, im = interp * np.cos(turn), -interp * np.sin(turn)
        rows += [np.concatenate([re, im], 1), np.concatenate([-im, re], 1)]
    joined = np.concatenate(rows, 0)
    join = np.zeros((OWN_RANK * 256, 512))
    for n in range(OWN_RANK):
        join[n * 256:(n + 1) * 256, n * 2 * ALL_NODES:(n + 1) * 2 * ALL_NODES] = joined
    join_hi, join_lo = _split(join)
    interp = interpolate(all_nodes, bands.astype(np.float64), WIDTH)
    turn = scale * middle * bands
    weave = np.zeros((256, M))
    weave[:2 * ALL_NODES] = np.concatenate([interp * np.cos(turn), interp * np.sin(turn)], 0)
    weave_hi, weave_lo = _split(weave)
    turn = TWO_PI * ((np.arange(16)[:, None] * (bands[None, :half] % 256)) % 256) / 256
    return dict(
        resid=resid, sample=sample, join_hi=join_hi, join_lo=join_lo, weave_hi=weave_hi, weave_lo=weave_lo,
        turn_c=np.cos(turn).astype(np.float32), turn_s=np.sin(turn).astype(np.float32),
    )


COL_A, COL_SC8, COL_CF8, COL_ROW = 0, 16, 24, 32
PACK = ((0, 1024), (1024, 2048), (2048, 2176), (2176, 2304), (2304, 2816))
CHUNKS = 20


def _angle(product):
    turns = lax.bitwise_and(product + NIMG, 2 * NIMG - 1) - NIMG
    return turns.astype(f32) * (math.pi / NIMG)


def _offset_row(order_ref, offsets_ref, which):
    slots = lax.broadcasted_iota(jnp.int32, (64, 64), 0)
    offsets = _to_column(offsets_ref[which:which + 1, :].astype(f32))
    return jnp.sum(jnp.where(slots == order_ref[...], offsets, 0.0), axis=0, keepdims=True)


def _to_column(row):
    at = lax.broadcasted_iota(jnp.int32, (64, 64), 0) == lax.broadcasted_iota(jnp.int32, (64, 64), 1)
    return jnp.sum(jnp.where(at, row, 0.0), axis=1, keepdims=True)


def _pick(row, index):
    lane = lax.broadcasted_iota(jnp.int32, row.shape, 1)
    return jnp.sum(jnp.where(lane == index, row, 0.0), axis=1, keepdims=True)


def _prepare(slot, half, order_ref, offsets_ref, cols_ref, rows_ref, band_ref,
             lc_ref, ls_ref, pc_ref, ps_ref, mc_ref, ms_ref):
    cf_row = _offset_row(order_ref, offsets_ref, 0)
    own_cf = _pick(cf_row, slot).astype(jnp.int32)
    cf = _to_column(cf_row).astype(jnp.int32)
    sc = _to_column(cols_ref[...].astype(f32)).astype(jnp.int32)
    sr = _to_column(rows_ref[...].astype(f32)).astype(jnp.int32)
    lane = lax.broadcasted_iota(jnp.int32, (64, 128), 1)
    row = lax.bitwise_and(4 * half + 4 * lax.bitwise_and(lane // 8, 1) + lax.bitwise_and(lane, 3), 7)
    odd = 2 * row - 7
    factor = jnp.where(
        lane < COL_SC8, 2 * (own_cf + 1024 * lane),
        jnp.where(lane < COL_CF8, 256 * (lane - COL_SC8), jnp.where(lane < COL_ROW, 256 * (lane - COL_CF8), odd)),
    )
    other = jnp.where(lane < COL_CF8, sc, jnp.where(lane < COL_ROW, cf, sr + 512))
    angle = _angle(factor * other)
    mc, ms = jnp.cos(angle), jnp.sin(angle)
    mc_ref[...] = mc
    ms_ref[...] = ms
    angle = _angle(2 * lane * sc)
    low_c, low_s = jnp.cos(angle), jnp.sin(angle)
    for i in range(8):
        c, s = mc[:, COL_SC8 + i:COL_SC8 + i + 1], ms[:, COL_SC8 + i:COL_SC8 + i + 1]
        lc_ref[:, i * 128:(i + 1) * 128] = c * low_c - s * low_s
        ls_ref[:, i * 128:(i + 1) * 128] = s * low_c + c * low_s
    angle = _angle(2 * lane * cf)
    low_c, low_s = jnp.cos(angle), jnp.sin(angle)
    for i in range(8):
        c, s = mc[:, COL_CF8 + i:COL_CF8 + i + 1], ms[:, COL_CF8 + i:COL_CF8 + i + 1]
        band = band_ref[:, i * 128:(i + 1) * 128]
        pc_ref[:, i * 128:(i + 1) * 128] = (c * low_c - s * low_s) * band
        ps_ref[:, i * 128:(i + 1) * 128] = (s * low_c + c * low_s) * band


def _combine(mc, ms, combine_ref):
    lane = lax.broadcasted_iota(jnp.int32, (64, 128), 1)
    row = 4 * lax.axis_index("rows") + 4 * lax.bitwise_and(lane // 8, 1) + lax.bitwise_and(lane, 3)
    place = (2 * lax.bitwise_and(row, 7) - 7).astype(f32) * (0.5 / ROW_SCALE)
    first = lax.bitwise_and(lane, 4) == 0
    to_re, to_im = jnp.where(first, mc, ms), jnp.where(first, -ms, mc)
    for n in range(ERANK):
        for part, value in ((0, to_re), (1, to_im)):
            base = part * 128 + n * 64
            combine_ref[base:base + 64, :] = (value * place if n else value)[:, COL_ROW:COL_ROW + 16].astype(bf16)


def _exact_kernel(order_hbm, offsets_hbm, cols_hbm, rows_hbm, band_hbm, data_hbm, window_hbm, sample_hbm, jh_hbm, jl_hbm,
                  pc_hbm, ps_hbm, pack_hbm,
                  order_ref, offsets_ref, cols_ref, rows_ref, band_ref, data_ref, window_ref, sample_ref, jh_ref, jl_ref,
                  pc_ref, ps_ref, out_ref, even_ref, odd_ref, acc_ref, terms_ref, sems, out_sems):
    loads = [
        pltpu.make_async_copy(source, target, sems.at[i])
        for i, (source, target) in enumerate((
            (order_hbm, order_ref), (offsets_hbm, offsets_ref), (cols_hbm, cols_ref), (rows_hbm, rows_ref),
            (band_hbm, band_ref), (data_hbm, data_ref), (window_hbm, window_ref), (sample_hbm, sample_ref),
            (jh_hbm, jh_ref), (jl_hbm, jl_ref),
        ))
    ]
    for load in loads:
        load.start()
    for load in loads[:5]:
        load.wait()
    acc_ref[...] = jnp.zeros_like(acc_ref)
    lc_ref, ls_ref, mc_ref, ms_ref, nodes_ref = (out_ref.at[:, a:b] for a, b in PACK)
    _prepare(lax.axis_index("facet"), lax.axis_index("rows"), order_ref, offsets_ref, cols_ref, rows_ref, band_ref,
             lc_ref, ls_ref, pc_ref, ps_ref, mc_ref, ms_ref)
    stores = [
        pltpu.make_async_copy(source, target, out_sems.at[i])
        for i, (source, target) in enumerate((
            (pc_ref, pc_hbm), (ps_ref, ps_hbm),
            (out_ref.at[:, 0:PACK[-1][0]], pack_hbm.at[:, 0:PACK[-1][0]]),
        ))
    ]
    for store in stores:
        store.start()
    for load in loads[5:8]:
        load.wait()

    def build(block, x_ref, bc, bs, i):
        cols = slice(i * 256, (i + 1) * 256)
        here = pl.ds(pl.multiple_of(block * BLOCK + i * 256, 256), 256)
        window = window_ref[:, here]
        re_rows = data_ref[0, 0, :, here] * window
        im_rows = data_ref[0, 1, :, here] * window
        for g in range(4):
            rows = slice(g * 16, (g + 1) * 16)
            lc, ls = lc_ref[rows, cols], ls_ref[rows, cols]
            c, s = bc[rows], bs[rows]
            ec = c * lc - s * ls
            es = s * lc + c * ls
            for r in range(4):
                dr, di = re_rows[r:r + 1], im_rows[r:r + 1]
                at = r * 64 + g * 16
                x_ref[at:at + 16, cols] = (dr * ec + di * es).astype(bf16)
                x_ref[256 + at:256 + at + 16, cols] = (di * ec - dr * es).astype(bf16)

    def turns(block):
        return _pick(mc_ref[...], block), _pick(ms_ref[...], block)

    def stage(block, x_ref, following, next_ref):
        bc, bs = turns(following)
        span = block // 4
        for i in range(4):
            rows = pl.ds(pl.multiple_of(lax.rem(block, 4) * BLOCK + i * 256, 256), 256)
            part = jnp.dot(x_ref[:, i * 256:(i + 1) * 256], sample_ref[rows, :], preferred_element_type=f32)
            build(following, next_ref, bc, bs, i)
            acc_ref[span] = acc_ref[span] + part

    bc, bs = turns(0)
    for i in range(4):
        build(0, even_ref, bc, bs, i)

    def body(pair, carry):
        stage(2 * pair, even_ref, 2 * pair + 1, odd_ref)
        stage(2 * pair + 1, odd_ref, lax.rem(2 * pair + 2, 16), even_ref)
        return carry

    lax.fori_loop(0, 8, body, 0)

    first = lax.broadcasted_iota(jnp.int32, (64, 128), 1) < 64
    lane = lax.broadcasted_iota(jnp.int32, (64, 128), 1)
    sign = jnp.where(lax.bitwise_and(lane, 32) == 0, -1.0, 1.0).astype(f32)
    places = [(r - 1.5) / ROW_SCALE for r in range(4)]
    spins = [
        [jnp.broadcast_to(ref[:, COL_ROW + r:COL_ROW + r + 1], (64, 128)) for ref in (mc_ref, ms_ref)] for r in range(4)
    ]
    for pair in range(2):
        sums = []
        for span in (2 * pair, 2 * pair + 1):
            direct, across = [None] * OWN_RANK, [None] * OWN_RANK
            for r in range(4):
                c, s = spins[r]
                re = acc_ref[span, r * 64:(r + 1) * 64]
                im = acc_ref[span, 256 + r * 64:256 + (r + 1) * 64]
                one, two = c * re + s * im, c * im - s * re
                for n in range(OWN_RANK):
                    direct[n] = one if r == 0 else direct[n] + one
                    across[n] = two if r == 0 else across[n] + two
                    one, two = one * places[r], two * places[r]
            sums.append((direct, across))
        for n in range(OWN_RANK):
            folded = []
            for which in range(2):
                a, b = sums[0][which][n], sums[1][which][n]
                folded.append(jnp.where(first, a, b) + pltpu.roll(jnp.where(first, b, a), 64, 1))
            at = n * 256 + pair * 128
            terms_ref[:, at:at + 128] = folded[0] + jnp.where(
                sign < 0, -pltpu.roll(folded[1], 96, 1), pltpu.roll(folded[1], 32, 1))
    for load in loads[8:]:
        load.wait()
    high, low = _halves(terms_ref[...])
    nodes_ref[...] = (
        jnp.dot(high, jh_ref[...], preferred_element_type=f32)
        + (jnp.dot(high, jl_ref[...], preferred_element_type=f32) + jnp.dot(low, jh_ref[...], preferred_element_type=f32))
    )
    last = pltpu.make_async_copy(nodes_ref, pack_hbm.at[:, PACK[-1][0]:PACK[-1][1]], out_sems.at[3])
    last.start()
    for store in stores:
        store.wait()
    last.wait()


def _residual_kernel(own_hbm, peer_ref, window_hbm, pack_ref, table_hbm, tc_hbm, ts_hbm, out_ref,
                     own_ref, window_ref, lc_ref, ls_ref, combine_ref, table_ref, tc_ref, ts_ref, even_ref, odd_ref, sum_ref, sems):
    loads = [
        pltpu.make_async_copy(source, target, sems.at[i])
        for i, (source, target) in enumerate((
            (own_hbm, own_ref), (window_hbm, window_ref),
            (table_hbm.at[lax.axis_index("rows")], table_ref), (tc_hbm, tc_ref), (ts_hbm, ts_ref),
        ))
    ]
    for load in loads:
        load.start()
    sum_ref[...] = jnp.zeros_like(sum_ref)
    mc_ref, ms_ref, nodes_ref = (pack_ref.at[:, a:b] for a, b in PACK[2:])
    lc_ref[...] = pack_ref[:, PACK[0][0]:PACK[0][1]].astype(bf16)
    ls_ref[...] = pack_ref[:, PACK[1][0]:PACK[1][1]].astype(bf16)
    _combine(mc_ref[...], ms_ref[...], combine_ref)
    for load in loads[:2]:
        load.wait()
    largest = jnp.zeros((4, 2048), f32)
    for i in range(8):
        here = slice(i * 2048, (i + 1) * 2048)
        window = window_ref[:, here]
        for ref in (own_ref, peer_ref):
            for part in range(2):
                largest = jnp.maximum(largest, jnp.abs(ref[0, part, :, here] * window))
    largest = jnp.maximum(jnp.max(jnp.max(largest, axis=1, keepdims=True), axis=0, keepdims=True), 1e-30)
    scale_in = DATA_SCALE / largest
    scale_out = largest * (1.0 / (DATA_SCALE * TABLE_SCALE))

    def mix(block, i):
        here = pl.ds(pl.multiple_of(block * BLOCK + i * 256, 256), 256)
        window = window_ref[:, here] * scale_in
        data = jnp.concatenate(
            [own_ref[0, 0, :, here], own_ref[0, 1, :, here], peer_ref[0, 0, :, here], peer_ref[0, 1, :, here]], 0
        )
        return jnp.dot(combine_ref[...], (data * window).astype(bf16), preferred_element_type=f32)

    def build(z_ref, j, i, rows, bc, bs):
        cols = slice(i * 256, (i + 1) * 256)
        lc, ls = lc_ref[:, cols], ls_ref[:, cols]
        ec = bc * lc - bs * ls
        es = bs * lc + bc * ls
        rows = rows.astype(bf16)
        for n in range(ERANK):
            gr, gi = rows[n * 64:(n + 1) * 64], rows[128 + n * 64:128 + (n + 1) * 64]
            at = j * 128 + n * 64
            zr, zi = gr * ec + gi * es, gi * ec - gr * es
            z_ref[at:at + 64, cols] = (zr + zi).astype(z_ref.dtype)
            z_ref[256 + at:256 + at + 64, cols] = zi.astype(z_ref.dtype)
            z_ref[512 + at:512 + at + 64, cols] = zr.astype(z_ref.dtype)

    def turns(block):
        return tuple(
            jnp.broadcast_to(_pick(ref[...], block), (64, 256)).astype(bf16) for ref in (mc_ref, ms_ref)
        )

    def stage(group, z_ref, following, next_ref):
        tasks = [(j, i) for j in range(2) for i in range(4)]
        building = following is not None
        if building:
            spins = [turns(following * 2 + j) for j in range(2)]
            ready = mix(following * 2, 0)
        at = 0
        for kc in range(2):
            for _ in range(1):
                cols = slice(kc * 256, (kc + 1) * 256)
                one = jnp.dot(z_ref[0:256], table_ref[:, cols], preferred_element_type=f32)
                two = jnp.dot(z_ref[256:512], table_ref[:, 512 + kc * 256:768 + kc * 256], preferred_element_type=f32)
                three = jnp.dot(z_ref[512:768], table_ref[:, 1024 + kc * 256:1280 + kc * 256], preferred_element_type=f32)
                for _ in range(4 if building else 0):
                    bj, bi = tasks[at]
                    at += 1
                    coming = mix(following * 2 + tasks[at][0], tasks[at][1]) if at < 8 else None
                    build(next_ref, bj, bi, ready, *spins[bj])
                    ready = coming
                re2, im2 = one + two, one - three
                for j in range(2):
                    re, im = re2[j * 128:(j + 1) * 128], im2[j * 128:(j + 1) * 128]
                    tc = tc_ref[pl.ds(group * 2 + j, 1), cols]
                    ts = ts_ref[pl.ds(group * 2 + j, 1), cols]
                    sum_ref[0, :, cols] = sum_ref[0, :, cols] + (re * tc + im * ts)
                    sum_ref[1, :, cols] = sum_ref[1, :, cols] + (im * tc - re * ts)

    for j in range(2):
        spin = turns(j)
        for i in range(4):
            build(even_ref, j, i, mix(j, i), *spin)
    for load in loads[2:]:
        load.wait()

    def body(pair, carry):
        stage(2 * pair, even_ref, 2 * pair + 1, odd_ref)
        stage(2 * pair + 1, odd_ref, 2 * pair + 2, even_ref)
        return carry

    lax.fori_loop(0, 3, body, 0)
    stage(6, even_ref, 7, odd_ref)
    stage(7, odd_ref, None, None)

    for copy in range(2):
        for i in range(CHUNKS - 16):
            out_ref[pl.ds(copy * CHUNKS + 16 + i, 64, stride=2 * CHUNKS), :] = nodes_ref[:, i * 128:(i + 1) * 128]
        for n in range(ERANK):
            for part in range(2):
                for kc in range(4):
                    at = copy * CHUNKS + n * 8 + part * 4 + kc
                    out_ref[pl.ds(at, 64, stride=2 * CHUNKS), :] = (
                        sum_ref[part, n * 64:(n + 1) * 64, kc * 128:(kc + 1) * 128] * scale_out
                    )


def _halves(value):
    high = value.astype(bf16)
    return high, (value - high.astype(f32)).astype(bf16)


def _phase_kernel(order_ref, offsets_ref, rows_ref, out_ref, all_ref, turned_ref):
    left_ref, gram_ref = out_ref.at[0:512], out_ref.at[512:1024]
    slot, half = lax.axis_index("facet"), lax.axis_index("rows")
    rf = _offset_row(order_ref, offsets_ref, 1).astype(jnp.int32)
    own_sr = _pick(rows_ref[...].astype(f32), slot).astype(jnp.int32)
    odd = jnp.concatenate([2 * rf + 7, 2 * rf + 7], 1)
    lane = lax.broadcasted_iota(jnp.int32, (128, 128), 1)
    quarter = jnp.where(lane < 64, 0, -(NIMG // 2))
    sign = jnp.where(lane < 64, -1.0, 1.0).astype(f32)
    for i in range(8):
        here = slice(i * 128, (i + 1) * 128)
        q = lax.broadcasted_iota(jnp.int32, (128, 128), 0) + i * 128 + half * 512
        q = lax.bitwise_and(q, 1023)
        turn = jnp.cos(_angle(odd * (own_sr + q) + quarter))
        other = sign * pltpu.roll(turn, 64, 1)
        g = (q - 512).astype(f32) * (TWO_PI / NIMG * ROW_SCALE)
        g2, g3 = g * g * 0.5, g * g * g * (1.0 / 6.0)
        for n, value in enumerate((turn, g * other, -g2 * turn, -g3 * other)):
            high, low = _halves(value)
            cols = slice(n * 128, (n + 1) * 128)
            all_ref[0, here, cols] = high
            all_ref[1, here, cols] = low
            high_t, low_t = _halves(sign * pltpu.roll(value, 64, 1))
            turned_ref[0, here, cols] = high_t
            turned_ref[1, here, cols] = low_t
            if i < 4 and n < 2:
                left_ref[here, n * 128:(n + 1) * 128] = high
                left_ref[here, 256 + n * 128:256 + (n + 1) * 128] = high
                left_ref[here, 512 + n * 128:512 + (n + 1) * 128] = low
            elif i < 4:
                left_ref[here, 512 + n * 128:512 + (n + 1) * 128] = high
    over_rows = (((0,), (0,)), ((), ()))
    gram = None
    for ref in (all_ref, turned_ref):
        for a, b in ((0, 0), (0, 1), (1, 0)):
            part = lax.dot_general(ref[a], ref[b], over_rows, preferred_element_type=f32)
            gram = part if gram is None else gram + part
    high, low = _halves(gram)
    gram_ref[:, 0:256] = high[:, 0:256]
    gram_ref[:, 256:512] = high[:, 0:256]
    gram_ref[:, 512:768] = low[:, 0:256]
    gram_ref[:, 768:1024] = high[:, 256:512]


def _rows_kernel(got_ref, wh_hbm, wl_hbm, pc_hbm, ps_hbm, phases_any, out_hbm,
                 wh_ref, wl_ref, pc_ref, ps_ref, gram_ref, left_ref, right_ref, value_ref, high_ref, low_ref,
                 out_ref, sems, out_sems):
    loads = [
        pltpu.make_async_copy(source, target, sems.at[i])
        for i, (source, target) in enumerate((
            (wh_hbm, wh_ref), (wl_hbm, wl_ref), (pc_hbm, pc_ref), (ps_hbm, ps_ref),
            (phases_any.at[512:1024], gram_ref), (phases_any.at[0:512], left_ref),
        ))
    ]
    for load in loads:
        load.start()
    parts = [
        jnp.concatenate([got_ref[pl.ds(h * CHUNKS + 16 + i, 64, stride=2 * CHUNKS), :] for i in range(4)], 1)
        for h in range(2)
    ]
    both, between = parts[0] + parts[1], parts[1] - parts[0]
    sums, diffs = [
        [(pltpu.roll(v, 512 - n * 2 * ALL_NODES, 1) if n else v)[:, 0:256] for n in range(OWN_RANK)]
        for v in (both, between)
    ]
    d = 2.0 / ROW_SCALE
    cube = 2.05 / (ROW_SCALE * ROW_SCALE)
    terms = (
        sums[0],
        sums[1] + d * diffs[0],
        sums[2] + (2 * d) * diffs[1] + (d * d) * sums[0],
        (cube + 3 * d * d) * sums[1] + (3 * d) * diffs[2] + (d * d * d) * diffs[0],
    )
    lane = lax.broadcasted_iota(jnp.int32, (64, 256), 1)
    for n, value in enumerate(terms):
        rows = slice(n * 64, (n + 1) * 64)
        value = jnp.where(lane < 2 * ALL_NODES, value, 0.0)
        for part in range(2):
            high, low = _halves(value)
            high_ref[part, rows, :] = high
            if n < 2:
                low_ref[part, rows, :] = low
            value = jnp.where(
                lane < ALL_NODES, pltpu.roll(value, 256 - ALL_NODES, 1), -pltpu.roll(value, ALL_NODES, 1))
    for load in loads[0:4]:
        load.wait()
    for i in range(4):
        cols = slice(i * 256, (i + 1) * 256)
        vals = []
        for part in range(2):
            wh, wl = wh_ref[:, cols], wl_ref[:, cols]
            main = jnp.dot(high_ref[part], wh, preferred_element_type=f32)
            rest = (
                jnp.dot(high_ref[part, 0:128], wl, preferred_element_type=f32)
                + jnp.dot(low_ref[part], wh, preferred_element_type=f32)
            )
            vals.append((main, rest))
        pc, ps = pc_ref[:, cols], ps_ref[:, cols]
        for n in range(RANK):
            rows = slice(n * 64, (n + 1) * 64)
            vr, vi = vals[0][0][rows], vals[1][0][rows]
            if n < ERANK:
                parts = []
                for part in range(2):
                    at = (i // 2) * CHUNKS + n * 8 + part * 4 + 2 * (i % 2)
                    parts.append(jnp.concatenate(
                        [got_ref[pl.ds(at + m, 64, stride=2 * CHUNKS), :] for m in range(2)], 1))
                vr = vr + vals[0][1][rows] + parts[0]
                vi = vi + vals[1][1][rows] + parts[1]
            cr = vr * pc + vi * ps
            ci = vi * pc - vr * ps
            at = n * 128
            value_ref[at:at + 64, cols] = cr
            value_ref[at + 64:at + 128, cols] = ci
            turned = slice(1024 + i * 256, 1024 + (i + 1) * 256)
            cr_high, ci_high = cr.astype(bf16), ci.astype(bf16)
            bases = (0, 512) if n < 2 else (512,)
            for base in bases:
                right_ref[base + at:base + at + 64, cols] = cr_high
                right_ref[base + at + 64:base + at + 128, cols] = ci_high
                right_ref[base + at:base + at + 64, turned] = ci_high
                right_ref[base + at + 64:base + at + 128, turned] = -cr_high
            if n < 2:
                cr_low = (cr - cr_high.astype(f32)).astype(bf16)
                ci_low = (ci - ci_high.astype(f32)).astype(bf16)
                right_ref[256 + at:256 + at + 64, cols] = cr_low
                right_ref[256 + at + 64:256 + at + 128, cols] = ci_low
                right_ref[256 + at:256 + at + 64, turned] = ci_low
                right_ref[256 + at + 64:256 + at + 128, turned] = -cr_low

    loads[4].wait()
    total = jnp.zeros((8, 256), f32)
    for i in range(4):
        cols = slice(i * 256, (i + 1) * 256)
        product = jnp.dot(gram_ref[...], right_ref[:, cols], preferred_element_type=f32) * value_ref[:, cols]
        total = total + jnp.sum(product.reshape(64, 8, 256), 0)
    mean = jnp.maximum(jnp.sum(total), 0.0) / (2.0 * SUBROWS * M)
    factor = lax.rsqrt(jnp.full((8, 128), mean, f32) + 1e-06)[0:1, 0:1]

    loads[5].wait()
    stores = []
    for part in range(2):
        for i in range(4):
            cols = slice(i * 256, (i + 1) * 256)
            right = right_ref[:, part * 1024 + i * 256:part * 1024 + (i + 1) * 256]
            out_ref[part, :, cols] = jnp.dot(left_ref[...], right, preferred_element_type=f32) * factor
            store = pltpu.make_async_copy(
                out_ref.at[part, :, cols], out_hbm.at[0, part, :, cols], out_sems.at[part * 4 + i])
            store.start()
            stores.append(store)
    for store in stores:
        store.wait()


def per_device(facets, facet_window, band_window, facet_order, facet_offsets, sub_cols, sub_rows):
    tables = _tables()
    peer = lax.ppermute(facets, "rows", [(0, 1), (1, 0)])
    order, cols, rows = (v.reshape(1, 64) for v in (facet_order, sub_cols, sub_rows))
    offsets = facet_offsets.T
    window = facet_window.reshape(1, 16384)
    hbm = pl.BlockSpec(memory_space=pltpu.HBM)
    anywhere = pl.BlockSpec(memory_space=pl.ANY)
    vmem = pl.BlockSpec(memory_space=pltpu.VMEM)
    shape = jax.ShapeDtypeStruct

    def params(mib):
        return pltpu.CompilerParams(vmem_limit_bytes=mib * 1024 * 1024)

    wide = shape((64, 1024), f32)
    pc, ps, pack = pl.pallas_call(
        _exact_kernel,
        in_specs=[hbm] * 10,
        out_specs=[hbm] * 3,
        out_shape=[wide, wide, shape((64, PACK[-1][1]), f32)],
        scratch_shapes=[
            pltpu.VMEM((1, 64), jnp.int32), pltpu.VMEM((2, 64), jnp.int32), pltpu.VMEM((1, 64), jnp.int32),
            pltpu.VMEM((1, 64), jnp.int32), pltpu.VMEM((1, M), f32), pltpu.VMEM((1, 2, 4, 16384), f32),
            pltpu.VMEM((1, 16384), f32), pltpu.VMEM((SPAN, 128), bf16),
            pltpu.VMEM((OWN_RANK * 256, 512), bf16), pltpu.VMEM((OWN_RANK * 256, 512), bf16),
            pltpu.VMEM((64, 1024), f32), pltpu.VMEM((64, 1024), f32), pltpu.VMEM((64, PACK[-1][1]), f32),
            pltpu.VMEM((512, BLOCK), bf16), pltpu.VMEM((512, BLOCK), bf16), pltpu.VMEM((4, 512, 128), f32),
            pltpu.VMEM((64, OWN_RANK * 256), f32),
            pltpu.SemaphoreType.DMA((10,)), pltpu.SemaphoreType.DMA((4,)),
        ],
        compiler_params=params(60),
        cost_estimate=pl.CostEstimate(flops=8 * 10**9, bytes_accessed=2 * 10**6, transcendentals=0),
        name="exact_part",
    )(order, offsets, cols, rows, band_window.reshape(1, M), facets, window, jnp.asarray(tables["sample"]),
      jnp.asarray(tables["join_hi"]), jnp.asarray(tables["join_lo"]))

    send = pl.pallas_call(
        _residual_kernel,
        in_specs=[hbm, vmem, hbm, vmem] + [hbm] * 3,
        out_shape=shape((128 * CHUNKS, 128), f32),
        scratch_shapes=[
            pltpu.VMEM((1, 2, 4, 16384), f32), pltpu.VMEM((1, 16384), f32),
            pltpu.VMEM((64, 1024), bf16), pltpu.VMEM((64, 1024), bf16), pltpu.VMEM((256, 16), bf16),
            pltpu.VMEM((1024, 1536), f8), pltpu.VMEM((16, 512), f32), pltpu.VMEM((16, 512), f32),
            pltpu.VMEM((768, 1024), f8), pltpu.VMEM((768, 1024), f8), pltpu.VMEM((2, 128, 512), f32),
            pltpu.SemaphoreType.DMA((5,)),
        ],
        compiler_params=params(44),
        cost_estimate=pl.CostEstimate(flops=9 * 10**9, bytes_accessed=4 * 10**6, transcendentals=0),
        name="residual_part",
    )(
        facets, peer, window, pack, jnp.asarray(tables["resid"]), jnp.asarray(tables["turn_c"]),
        jnp.asarray(tables["turn_s"]),
    )

    got = lax.all_to_all(send.reshape(128, CHUNKS // 4, 4, 128), ("facet", "rows"), split_axis=0, concat_axis=0, tiled=True)
    phases = pl.pallas_call(
        _phase_kernel,
        in_specs=[vmem] * 3,
        out_shape=shape((1024, 1024), bf16),
        scratch_shapes=[pltpu.VMEM((2, 1024, 512), bf16), pltpu.VMEM((2, 1024, 512), bf16)],
        compiler_params=params(60),
        cost_estimate=pl.CostEstimate(flops=3 * 10**9, bytes_accessed=2 * 10**6, transcendentals=2 * 10**5),
        name="row_phases",
    )(order, offsets, rows)

    return pl.pallas_call(
        _rows_kernel,
        in_specs=[vmem] + [hbm] * 4 + [anywhere],
        out_specs=hbm,
        out_shape=shape((1, 2, 512, 1024), f32),
        scratch_shapes=[
            pltpu.VMEM((256, 1024), bf16), pltpu.VMEM((256, 1024), bf16),
            pltpu.VMEM((64, 1024), f32), pltpu.VMEM((64, 1024), f32), pltpu.VMEM((512, 1024), bf16),
            pltpu.VMEM((512, 1024), bf16), pltpu.VMEM((1024, 2048), bf16), pltpu.VMEM((512, 1024), f32),
            pltpu.VMEM((2, 256, 256), bf16), pltpu.VMEM((2, 128, 256), bf16), pltpu.VMEM((2, 512, 1024), f32),
            pltpu.SemaphoreType.DMA((7,)), pltpu.SemaphoreType.DMA((8,)),
        ],
        compiler_params=params(50),
        cost_estimate=pl.CostEstimate(flops=5 * 10**9, bytes_accessed=12 * 10**6, transcendentals=0),
        name="row_transform",
    )(got.reshape(128 * CHUNKS, 128), jnp.asarray(tables["weave_hi"]), jnp.asarray(tables["weave_lo"]), pc, ps, phases)


def solution(mesh):
    return jax.shard_map(
        per_device,
        mesh=mesh,
        in_specs=(P("facet", None, "rows", None), P(), P(), P(), P(), P(), P()),
        out_specs=P("facet", None, "rows", None),
        check_vma=False,
    )
```
